32 devices in a mesh: fsdp: 4 (over y, core), blk: 2 (over x), seq: 4 (over z).
Axes of the slice: x: 2, y: 2, z: 4, core: 2. Of those that a mesh axis runs over, the one named last changes fastest.
Arguments:
- tokens: float32 [4, 1024, 768], P('fsdp', ('blk', 'seq')), may hold values from -6 to 6
- counts: int32 [4, 8], P('fsdp'), may hold values from 1 to 128, 820 in all within a row
- norm_gain: bfloat16 [2, 768], replicated, may hold values from 0.5 to 1.5
- norm_bias: bfloat16 [2, 768], replicated, may hold values from -4 to 4
- vec_bias: bfloat16 [4, 768], replicated, may hold values from -4 to 4
- up_bias: bfloat16 [3072], replicated, may hold values from -6 to 6
- w_qkv: bfloat16 [768, 2304], P('fsdp'), may hold values from -0.3125 to 0.3125
- w_out: bfloat16 [768, 768], P('fsdp'), may hold values from -1.25 to 1.25
- w_up: bfloat16 [768, 3072], P('fsdp'), may hold values from -0.21875 to 0.21875
- w_down: bfloat16 [3072, 768], P('fsdp'), may hold values from -0.109375 to 0.109375
- grad_out: float32 [4, 1024, 768], P('fsdp', ('blk', 'seq')), may hold values from -6 to 6
Outputs:
- activations: float32 [4, 1024, 768], P('fsdp', ('blk', 'seq'))
- grad_tokens: float32 [4, 1024, 768], P('fsdp', ('blk', 'seq'))
- grad_norm_gain: float32 [2, 768], P(None, 'fsdp')
- grad_norm_bias: float32 [2, 768], P(None, 'fsdp')
- grad_vec_bias: float32 [4, 768], P(None, 'fsdp')
- grad_up_bias: float32 [3072], P('fsdp')
- grad_w_qkv: float32 [768, 2304], P('fsdp')
- grad_w_out: float32 [768, 768], P('fsdp')
- grad_w_up: float32 [768, 3072], P('fsdp')
- grad_w_down: float32 [3072, 768], P('fsdp')
The draws below stay inside these ranges and needn't reach their ends.
Inputs may be any that keep to these rules, and one draw needn't show every extreme that they name: `counts`: row i lists, for the 8 devices that hold image i in order, how many of their 128 slots carry tokens; these come first. A row sums to 820 and holds 128 at least once.
All inputs are finite; a program needn't handle non-finite values.
Results may differ from the reference program's by a relative error of at most 0.02.
Values may be sent and summed in bfloat16 or wider, within the bound.
No kernel may reach another device: no remote copies, remote signals or barrier semaphores. Data moves between devices by JAX's collectives and lax.ppermute only.
A program may use at most 128 MiB of HBM per device.

```python
import math
from functools import partial
import jax
import jax.numpy as jnp
import numpy as np
from jax import lax

D = 768
H = 12
HD = 64
FF = 3072
SLOT_DEV = 128
PIECES = 8
SLOTS = 1024
LENGTH = 820
IMAGES = 4


def steps_of(stream_key, extent, split, low, top_value):
    def one(axis_at, blocks):
        draws = jax.random.uniform(jax.random.fold_in(jax.random.fold_in(stream_key, 6), axis_at), (blocks,), jnp.float32, low / len(split), top_value / len(split))
        return jnp.repeat(jnp.exp(draws), extent[axis_at] // blocks).reshape((-1,) + (1,) * (len(extent) - axis_at - 1))

    gain = one(*split[0])
    for cut in split[1:]:
        gain = gain * one(*cut)
    return gain


def length_profile(count, total, most, skew):
    portions = [(1 << 20) // math.isqrt(rank ** skew) + 1 for rank in range(2, count + 1)]
    surplus, given = total - most - (count - 1), [1] * (count - 1)
    while surplus > 0:
        free = [i for i in range(count - 1) if given[i] < most]
        whole, left = sum([portions[i] for i in free]), surplus
        for i in free:
            addition = min(most - given[i], max(1, left * portions[i] // whole), surplus)
            given[i] = given[i] + addition
            surplus = surplus - addition
    return np.array([most] + given)


def ragged(own_key, count, total, most, lean):
    if count == 2:
        one = jax.random.randint(own_key, (), max(1, total - most), min(most, total - 1) + 1)
        return jnp.stack([one, total - one])
    lengths = jnp.asarray(length_profile(count, total, most, lean), jnp.int32)
    twos = (count - 1) // 2
    donor, receiver = lengths[1:1 + 2 * twos:2], lengths[2:2 + 2 * twos:2]
    margin = jnp.minimum(donor - 1, most - receiver)
    shifted = jax.random.randint(jax.random.fold_in(own_key, 1), (twos,), 0, 1 << 20) % (margin + 1)
    lengths = lengths.at[1:1 + 2 * twos:2].set(donor - shifted).at[2:2 + 2 * twos:2].set(receiver + shifted)
    return lengths[jax.random.permutation(jax.random.fold_in(own_key, 2), count)]


def gaussian(stream_key, shape, scale, reach, cuts=(), kind=jnp.bfloat16):
    loudness = steps_of(stream_key, shape, cuts, -0.22, 0.18) if cuts else 1.0
    drawn = jax.random.normal(stream_key, shape, jnp.float32) * scale * loudness
    return jnp.minimum(jnp.maximum(drawn, -reach), reach).astype(kind)


def setup_inputs(seed: int = 0) -> dict:
    key_list = jax.random.split(jax.random.key(seed), 12)
    tokens = gaussian(key_list[0], (IMAGES, SLOTS, D), 1.0, 6.0, ((0, 4), (1, 8)), jnp.float32)
    counts = jax.vmap(lambda own: ragged(own, PIECES, LENGTH, SLOT_DEV, 1))(jax.random.split(key_list[1], IMAGES)).reshape((IMAGES, PIECES)).astype(jnp.int32)
    norm_gain = jnp.clip(1.0 + 0.1 * jax.random.normal(key_list[2], (2, D), jnp.float32), 0.5, 1.5).astype(jnp.bfloat16)
    norm_bias = gaussian(key_list[3], (2, D), 0.3, 4.0)
    vec_bias = gaussian(key_list[4], (4, D), 0.3, 4.0)
    up_bias = gaussian(key_list[5], (FF,), 0.5, 6.0)
    w_qkv = gaussian(key_list[6], (D, 3 * D), (D // 2) ** -0.5, 0.3125, ((0, 4),))
    w_out = gaussian(key_list[7], (D, D), (D // 32) ** -0.5, 1.25, ((0, 4),))
    w_up = gaussian(key_list[8], (D, FF), D ** -0.5, 0.21875, ((0, 4),))
    w_down = gaussian(key_list[9], (FF, D), FF ** -0.5, 0.109375, ((0, 4),))
    grad_out = gaussian(key_list[10], (IMAGES, SLOTS, D), 1.0, 6.0, ((0, 4), (1, 8)), jnp.float32)
    return dict(tokens=tokens, counts=counts, norm_gain=norm_gain, norm_bias=norm_bias, vec_bias=vec_bias, up_bias=up_bias, w_qkv=w_qkv, w_out=w_out, w_up=w_up, w_down=w_down, grad_out=grad_out)


@jax.custom_vjp
def low(v):
    return lax.optimization_barrier(v.astype(jnp.bfloat16)).astype(jnp.float32)

@jax.custom_vjp
def low_back(v):
    return v

def low_keep(v):
    return (low(v), None)

def low_pass(kept, grad):
    return (grad,)

def back_keep(v):
    return (v, None)

def back_low(kept, grad):
    return (low(grad),)
low.defvjp(low_keep, low_pass)
low_back.defvjp(back_keep, back_low)
EPSILON = 1e-06
MASKED = -1e+30
PRECISE = lax.Precision.HIGHEST

def layer_norm(matrix_rows, gain_row, shift_row):
    centre = matrix_rows - lax.optimization_barrier(jnp.mean(matrix_rows, axis=-1, keepdims=True))
    spread = lax.optimization_barrier(jnp.mean(centre * centre, axis=-1, keepdims=True))
    return centre * lax.rsqrt(spread + EPSILON) * gain_row + shift_row

def head_attend(key_valid, triple):
    queries, keys_in, values = triple
    scores = jnp.dot(queries, keys_in.T, precision=PRECISE) * HD ** (-0.5)
    scores = low_back(scores)
    scores = jnp.where(key_valid[None, :], scores, MASKED)
    log_total = jax.nn.logsumexp(scores, axis=-1, keepdims=True)
    soft_weights = low(jnp.exp(scores - log_total))
    return jnp.dot(soft_weights, values, precision=PRECISE)

def image_forward(params, couple):
    rows_in, is_token = couple
    norm_gain, norm_bias, vec_bias, up_bias, w_qkv, w_out, w_up, w_down = params
    slot_total = rows_in.shape[0]
    normed1 = low(layer_norm(rows_in, norm_gain[0], norm_bias[0]))
    zero_bias = jnp.zeros_like(vec_bias[0])
    projected = jnp.dot(normed1, w_qkv, precision=PRECISE) + jnp.concatenate([vec_bias[0], zero_bias, vec_bias[1]])
    projected = low(low_back(projected))
    split_qkv = projected.reshape(slot_total, 3, H, HD).transpose(1, 2, 0, 3)
    attended = lax.map(jax.checkpoint(partial(head_attend, is_token)), (split_qkv[0], split_qkv[1], split_qkv[2]))
    attended = low(low_back(attended.transpose(1, 0, 2).reshape(slot_total, H * HD)))
    branch = low_back(jnp.dot(attended, w_out, precision=PRECISE) + vec_bias[2])
    middle = rows_in + branch
    normed2 = low(layer_norm(middle, norm_gain[1], norm_bias[1]))
    up_proj = low_back(jnp.dot(normed2, w_up, precision=PRECISE) + up_bias)
    hidden = low(jax.nn.gelu(up_proj, approximate=False))
    outcome = low_back(jnp.dot(hidden, w_down, precision=PRECISE) + vec_bias[3])
    return jnp.where(is_token[:, None], middle + outcome, 0.0)

def reference(tokens, counts, norm_gain, norm_bias, vec_bias, up_bias, w_qkv, w_out, w_up, w_down, grad_out):
    slot_index = jnp.arange(SLOTS, dtype=jnp.int32)
    slot_limit = jnp.repeat(counts, SLOT_DEV, axis=1)
    is_token = (slot_index % SLOT_DEV)[None, :] < slot_limit
    params = (norm_gain.astype(jnp.float32), norm_bias.astype(jnp.float32), vec_bias.astype(jnp.float32), up_bias.astype(jnp.float32), w_qkv.astype(jnp.float32), w_out.astype(jnp.float32), w_up.astype(jnp.float32), w_down.astype(jnp.float32))

    def forward(inputs, weights):
        per_image = jax.checkpoint(partial(image_forward, weights))
        return lax.map(per_image, (inputs, is_token))
    result, pullback = jax.vjp(forward, tokens.astype(jnp.float32), params)
    grad_tokens, weight_grads = pullback(grad_out.astype(jnp.float32))
    return (result, grad_tokens, weight_grads[0], weight_grads[1], weight_grads[2], weight_grads[3], weight_grads[4], weight_grads[5], weight_grads[6], weight_grads[7])
```

```python
import functools

import jax
import jax.numpy as jnp
from jax import lax
from jax.experimental import pallas as pl
from jax.experimental.pallas import tpu as pltpu
from jax.sharding import PartitionSpec as P

HD = 64
EPSILON = 1e-06
MASKED = -1e30
SCALE = HD ** (-0.5)
BF = jnp.bfloat16
F32 = jnp.float32
VMEM_LIMIT = 44 * 1024 * 1024


def dot_nn(left_side, right_side):
    return lax.dot_general(
        left_side, right_side, (((1,), (0,)), ((), ())), preferred_element_type=F32
    )


def dot_nt(left_side, right_side):
    return lax.dot_general(
        left_side, right_side, (((1,), (1,)), ((), ())), preferred_element_type=F32
    )


def dot_tn(left_side, right_side):
    return lax.dot_general(
        left_side, right_side, (((0,), (0,)), ((), ())), preferred_element_type=F32
    )


def swap(array, axis, bits):
    return lax.ppermute(array, axis, [(i, i ^ bits) for i in range(lax.axis_size(axis))])


def from_all(array, axis):
    return [array] + [swap(array, axis, j) for j in range(1, lax.axis_size(axis))]


def doubled(array, axis):
    pieces = {0: array}
    bit = lax.axis_size(axis) // 2
    while bit:
        pieces.update({j | bit: swap(piece, axis, bit) for j, piece in list(pieces.items())})
        bit //= 2
    return [pieces[j] for j in range(lax.axis_size(axis))]


def mirrored(position, count):
    result = jnp.zeros_like(position)
    bit = 1
    while bit < count:
        result = result * 2 + (position // bit) % 2
        bit *= 2
    return result


def picker(sources):
    total = sources.shape[0]
    return (lax.broadcasted_iota(jnp.int32, (total, total), 0) == sources[None, :]).astype(BF)


def piece_bias(counts_ref, first_piece, pieces, slot_rows):
    row = lax.broadcasted_iota(jnp.int32, (pieces * slot_rows, 1), 0)
    limit = jnp.zeros_like(row)
    for piece in range(pieces):
        end = counts_ref[first_piece + piece] + piece * slot_rows
        limit = jnp.where(row >= piece * slot_rows, end, limit)
    return jnp.where(row < limit, 0.0, MASKED)


def attend_kernel(blocks, heads, pieces, slot_rows, counts_ref, q_ref, *refs):
    kv_refs, (out_ref, log_ref) = refs[:blocks], refs[blocks:]
    width = heads * HD
    biases = [piece_bias(counts_ref, m * pieces, pieces, slot_rows) for m in range(blocks)]
    for head in range(heads):
        low, high = head * HD, (head + 1) * HD
        query = q_ref[:, low:high] * SCALE
        scores = [dot_nt(kv[:, low:high], query) + bias for kv, bias in zip(kv_refs, biases)]
        top = functools.reduce(
            jnp.maximum, [jnp.max(block, axis=0, keepdims=True) for block in scores]
        )
        powers = [jnp.exp(block - top) for block in scores]
        total = sum(jnp.sum(block, axis=0, keepdims=True) for block in powers)
        inverse = 1.0 / total
        result = sum(
            dot_tn((block * inverse).astype(BF), kv[:, width + low : width + high])
            for block, kv in zip(powers, kv_refs)
        )
        out_ref[:, low:high] = result.astype(BF)
        log_ref[head : head + 1, :] = top + jnp.log(total)


def attend_back_kernel(blocks, heads, pieces, slot_rows, counts_ref, q_ref, log_ref, d_ref, *refs):
    kv_refs, dq_ref, dkv_refs = refs[:blocks], refs[blocks], refs[blocks + 1 :]
    width = heads * HD
    biases = [piece_bias(counts_ref, m * pieces, pieces, slot_rows) for m in range(blocks)]
    for head in range(heads):
        low, high = head * HD, (head + 1) * HD
        query = q_ref[:, low:high] * SCALE
        d_out = d_ref[:, low:high]
        log_row = log_ref[head : head + 1, :]
        softs, d_softs, delta = [], [], 0.0
        for kv, bias in zip(kv_refs, biases):
            soft = jnp.exp(dot_nt(kv[:, low:high], query) + bias - log_row)
            d_soft = dot_nt(kv[:, width + low : width + high], d_out)
            delta = delta + jnp.sum(soft * d_soft, axis=0, keepdims=True)
            softs.append(soft)
            d_softs.append(d_soft)
        d_query = 0.0
        for kv, dkv, soft, d_soft in zip(kv_refs, dkv_refs, softs, d_softs):
            d_scores = (soft * (d_soft - delta)).astype(BF)
            d_query = d_query + dot_tn(d_scores, kv[:, low:high])
            dkv[:, low:high] = dot_nn(d_scores, query).astype(dkv.dtype)
            dkv[:, width + low : width + high] = dot_nn(soft.astype(BF), d_out).astype(dkv.dtype)
        dq_ref[:, low:high] = (d_query * SCALE).astype(BF)


def attend(counts, queries, kv_blocks, slot_rows):
    rows, width = queries.shape
    blocks, heads = len(kv_blocks), width // HD
    pieces = kv_blocks[0].shape[0] // slot_rows
    return pl.pallas_call(
        functools.partial(attend_kernel, blocks, heads, pieces, slot_rows),
        out_shape=(
            jax.ShapeDtypeStruct((rows, width), BF),
            jax.ShapeDtypeStruct((heads, rows), F32),
        ),
        in_specs=[pl.BlockSpec(memory_space=pltpu.SMEM)]
        + [pl.BlockSpec(memory_space=pltpu.VMEM)] * (1 + blocks),
        out_specs=(pl.BlockSpec(memory_space=pltpu.VMEM),) * 2,
        compiler_params=pltpu.CompilerParams(vmem_limit_bytes=VMEM_LIMIT),
        cost_estimate=pl.CostEstimate(
            flops=4 * rows * blocks * rows * width,
            bytes_accessed=2 * rows * width * (2 + 2 * blocks),
            transcendentals=rows * rows * blocks * heads,
        ),
        name="attend",
    )(counts, queries, *kv_blocks)


def attend_back(counts, queries, log_total, d_out, kv_blocks, slot_rows):
    rows, width = queries.shape
    blocks, heads = len(kv_blocks), width // HD
    pieces = kv_blocks[0].shape[0] // slot_rows
    return pl.pallas_call(
        functools.partial(attend_back_kernel, blocks, heads, pieces, slot_rows),
        out_shape=(jax.ShapeDtypeStruct((rows, width), BF),)
        + tuple(
            jax.ShapeDtypeStruct(block.shape, F32 if m == 0 else BF)
            for m, block in enumerate(kv_blocks)
        ),
        in_specs=[pl.BlockSpec(memory_space=pltpu.SMEM)]
        + [pl.BlockSpec(memory_space=pltpu.VMEM)] * (3 + blocks),
        out_specs=(pl.BlockSpec(memory_space=pltpu.VMEM),) * (1 + blocks),
        compiler_params=pltpu.CompilerParams(vmem_limit_bytes=VMEM_LIMIT),
        cost_estimate=pl.CostEstimate(
            flops=10 * rows * blocks * rows * width,
            bytes_accessed=2 * rows * width * (3 + 5 * blocks),
            transcendentals=rows * rows * blocks * heads,
        ),
        name="attend_back",
    )(counts, queries, log_total, d_out, *kv_blocks)


def normalised(matrix_rows):
    centre = matrix_rows - jnp.mean(matrix_rows, axis=-1, keepdims=True)
    inverse = lax.rsqrt(jnp.mean(centre * centre, axis=-1, keepdims=True) + EPSILON)
    return centre * inverse, inverse


def norm_back(upstream, unit_rows, inverse, gain_row):
    scaled = upstream * gain_row
    d_rows = inverse * (
        scaled
        - jnp.mean(scaled, axis=-1, keepdims=True)
        - unit_rows * jnp.mean(scaled * unit_rows, axis=-1, keepdims=True)
    )
    return d_rows, jnp.sum(upstream * unit_rows, axis=0), jnp.sum(upstream, axis=0)


def owner_sums(left_side, right_side):
    half = left_side.shape[1] // 2
    sent = dot_tn(left_side[:, half:], right_side).astype(BF)
    arrived = swap(sent, "fsdp", 1)
    current = dot_tn(left_side[:, :half], right_side) + arrived.astype(F32)
    bit = 2
    while bit < lax.axis_size("fsdp"):
        half = current.shape[0] // 2
        arrived = swap(current[half:].astype(BF), "fsdp", bit)
        current = current[:half] + arrived.astype(F32)
        bit *= 2
    return current


def split_sums(array, axis):
    count = lax.axis_size(axis)
    rows = array.shape[0] // count
    own = array[:rows].astype(F32)
    for j in range(1, count):
        own = own + swap(array[j * rows : (j + 1) * rows].astype(BF), axis, j).astype(F32)
    return own


def sum_over(array, axes):
    total = array
    count = 1
    for name in axes:
        count *= lax.axis_size(name)
    for j in range(1, count):
        total = total + lax.ppermute(array, axes, [(i, i ^ j) for i in range(count)])
    return total


def in_order(pieces, index):
    result = []
    for place in range(len(pieces)):
        chosen = pieces[place]
        for other in range(1, len(pieces)):
            chosen = jnp.where(index == other, pieces[place ^ other], chosen)
        result.append(chosen)
    return result


def shards(
    tokens, counts, norm_gain, norm_bias, vec_bias, up_bias, w_qkv, w_out, w_up, w_down, grad_out
):
    owners, blocks, seqs = (lax.axis_size(name) for name in ("fsdp", "blk", "seq"))
    own, blk, seq = (lax.axis_index(name) for name in ("fsdp", "blk", "seq"))
    rows, width = tokens.shape[1:]
    head_width = width // seqs
    own_rows = width // owners
    hidden_rows = w_down.shape[0] // blocks
    hidden_width = hidden_rows * owners
    out_width = width // blocks

    gains = norm_gain.astype(F32)
    shifts = norm_bias.astype(F32)
    biases = vec_bias.astype(F32)

    qkv_mine = lax.dynamic_slice_in_dim(
        w_qkv.reshape(own_rows, 3, seqs, head_width), seq, 1, axis=2
    ).reshape(own_rows, 3 * head_width)
    up_mine = lax.dynamic_slice_in_dim(
        w_up.reshape(own_rows, owners, blocks, hidden_rows), blk, 1, axis=2
    ).reshape(own_rows, hidden_width)
    down_mine = lax.dynamic_slice_in_dim(w_down, blk * hidden_rows, hidden_rows, axis=0)
    up_shift = lax.dynamic_slice_in_dim(
        up_bias.reshape(owners, blocks, hidden_rows), blk, 1, axis=1
    ).reshape(hidden_width).astype(F32)
    qkv_shift = jnp.concatenate(
        [
            lax.dynamic_slice_in_dim(biases[0], seq * head_width, head_width),
            jnp.zeros((head_width,), F32),
            lax.dynamic_slice_in_dim(biases[1], seq * head_width, head_width),
        ]
    )

    place = jnp.arange(width, dtype=jnp.int32)
    owner_of = own ^ mirrored(place // own_rows, owners)
    seq_rows, blk_rows = own_rows // seqs, own_rows // blocks
    in_own = place % own_rows
    by_seq = owner_of * own_rows + (seq ^ (in_own // seq_rows)) * seq_rows + in_own % seq_rows
    by_blk = owner_of * own_rows + (blk ^ (in_own // blk_rows)) * blk_rows + in_own % blk_rows
    heads_place = (seq ^ (place // head_width)) * head_width + place % head_width
    hidden_place = jnp.arange(hidden_width, dtype=jnp.int32)
    in_hidden = hidden_place % hidden_rows
    chunk = hidden_rows // seqs
    by_hidden = (
        (own ^ mirrored(hidden_place // hidden_rows, owners)) * hidden_rows
        + (seq ^ (in_hidden // chunk)) * chunk
        + in_hidden % chunk
    )
    heads_pick = picker(heads_place)
    by_seq_heads = (seq ^ (by_seq // head_width)) * head_width + by_seq % head_width

    inputs = tokens[0]
    own_count = counts[0, blk * seqs + seq]
    own_valid = lax.broadcasted_iota(jnp.int32, (rows, 1), 0) < own_count
    piece_of = jnp.arange(blocks * seqs, dtype=jnp.int32)
    key_counts = counts[0][(blk ^ (piece_of // seqs)) * seqs + (seq ^ (piece_of % seqs))]

    unit1, inverse1 = normalised(inputs)
    normed1 = (unit1 * gains[0] + shifts[0]).astype(BF)
    normed1_all = jnp.concatenate(from_all(normed1, "seq"))
    qkv_rows = doubled(qkv_mine, "fsdp")
    qkv_full = jnp.concatenate(in_order(qkv_rows, own))

    full_out = lax.all_gather(w_out, "fsdp", axis=0, tiled=True)
    full_up = lax.all_gather(up_mine, "fsdp", axis=0, tiled=True)
    full_down = lax.all_gather(down_mine, "fsdp", axis=0, tiled=True)

    grad_rows = jnp.where(own_valid, grad_out[0], 0.0)
    d_outcome = grad_rows.astype(BF)
    d_outcome_all = jnp.concatenate(from_all(d_outcome, "blk"))

    projected = (dot_nn(normed1_all, qkv_full) + qkv_shift).astype(BF)
    queries = projected[:, :head_width]
    kv_blocks = from_all(projected[:, head_width:], "blk")
    attended, log_total = attend(key_counts, queries, kv_blocks, rows)
    token_att = jnp.concatenate(
        [attended[:rows]]
        + [swap(attended[k * rows : (k + 1) * rows], "seq", k) for k in range(1, seqs)],
        axis=1,
    )
    heads_out = dot_nn(heads_pick, full_out).astype(BF)

    middle = inputs + dot_nn(token_att, heads_out) + biases[2]
    unit2, inverse2 = normalised(middle)
    normed2 = (unit2 * gains[1] + shifts[1]).astype(BF)
    normed2_all = jnp.concatenate(from_all(normed2, "blk"))
    up_proj = dot_nn(normed2_all, full_up) + up_shift
    chance = 0.5 * (1.0 + lax.erf(up_proj * (0.5**0.5)))
    hidden = (up_proj * chance).astype(BF)
    slope = chance + up_proj * (jnp.exp(-0.5 * up_proj * up_proj) * 0.3989422804014327)
    d_hidden = dot_nt(d_outcome_all, full_down)
    d_up = (d_hidden * slope).astype(BF)
    d_normed2 = split_sums(dot_nt(d_up, full_up), "blk")
    outcome = split_sums(dot_nn(hidden, full_down), "blk")
    activations = jnp.where(own_valid, middle + outcome + biases[3], 0.0)

    d_middle_norm, d_gain_two, d_shift_two = norm_back(d_normed2, unit2, inverse2, gains[1])
    d_middle = grad_rows + d_middle_norm
    d_branch = d_middle.astype(BF)
    d_heads = dot_nt(d_branch, heads_out).astype(BF)
    d_attended = jnp.concatenate(
        [d_heads[:, :head_width]]
        + [
            swap(d_heads[:, k * head_width : (k + 1) * head_width], "seq", k)
            for k in range(1, seqs)
        ]
    )
    sum_down = split_sums(owner_sums(dot_nn(hidden, picker(by_hidden)).astype(BF), d_outcome_all), "seq")
    sum_up = split_sums(owner_sums(dot_nn(normed2_all, picker(by_seq)).astype(BF), d_up), "seq")

    back = attend_back(key_counts, queries, log_total, d_attended, kv_blocks, rows)
    d_query, d_kv = back[0], back[1]
    for m in range(1, blocks):
        d_kv = d_kv + swap(back[1 + m], "blk", m).astype(F32)
    d_projected = jnp.concatenate([d_query, d_kv.astype(BF)], axis=1)
    d_normed1 = split_sums(dot_nt(d_projected, qkv_full), "seq")
    d_inputs, d_gain_one, d_shift_one = norm_back(d_normed1, unit1, inverse1, gains[0])
    grad_tokens = d_middle + d_inputs

    sum_qkv = split_sums(
        owner_sums(dot_nn(normed1_all, picker(by_blk)).astype(BF), d_projected), "blk"
    )
    att_all = jnp.concatenate(from_all(token_att, "blk"))
    branch_all = jnp.concatenate(
        [lax.dynamic_slice_in_dim(d_branch, blk * out_width, out_width, axis=1)]
        + [
            swap(
                lax.dynamic_slice_in_dim(d_branch, (blk ^ m) * out_width, out_width, axis=1),
                "blk",
                m,
            )
            for m in range(1, blocks)
        ]
    )
    sum_out = split_sums(
        owner_sums(dot_nn(att_all, picker(by_seq_heads)).astype(BF), branch_all), "seq"
    )

    bias_sums = jnp.sum(d_projected.astype(F32), axis=0)
    is_seq = (jnp.arange(seqs) == seq)[:, None]
    is_blk = (jnp.arange(blocks) == blk)[None, :, None]
    up_sums = jnp.sum(d_up.astype(F32), axis=0).reshape(owners, 1, hidden_rows)
    vectors = jnp.concatenate(
        [
            d_gain_one,
            d_gain_two,
            d_shift_one,
            d_shift_two,
            jnp.where(is_seq, bias_sums[None, :head_width], 0.0).reshape(-1),
            jnp.where(is_seq, bias_sums[None, 2 * head_width :], 0.0).reshape(-1),
            jnp.sum(d_branch.astype(F32), axis=0),
            jnp.sum(d_outcome.astype(F32), axis=0),
            jnp.where(is_blk, up_sums, 0.0).reshape(-1),
        ]
    ).reshape(-1, 128)
    vectors = sum_over(sum_over(vectors, ("fsdp",)), ("blk", "seq")).reshape(-1)
    mine = lax.dynamic_slice_in_dim(
        vectors[: 8 * width].reshape(8, width), own * own_rows, own_rows, axis=1
    )
    up_total = lax.dynamic_slice_in_dim(
        vectors[8 * width :], own * blocks * hidden_rows, blocks * hidden_rows
    )

    def spread(array):
        return from_all(jnp.concatenate(from_all(array.astype(BF), "seq")), "blk")

    down_pieces = jnp.concatenate(spread(sum_down))
    spot = jnp.arange(blocks * hidden_rows, dtype=jnp.int32)
    in_spot = spot % hidden_rows
    down_from = (
        (blk ^ (spot // hidden_rows)) * hidden_rows
        + (seq ^ (in_spot // chunk)) * chunk
        + in_spot % chunk
    )
    grad_down = dot_nn(picker(down_from), down_pieces)
    row = jnp.arange(own_rows, dtype=jnp.int32)
    seq_pick = picker((seq ^ (row // seq_rows)) * seq_rows + row % seq_rows)
    blk_pick = picker((blk ^ (row // blk_rows)) * blk_rows + row % blk_rows)
    up_pieces = [dot_nn(seq_pick, piece) for piece in spread(sum_up)]
    grad_up = jnp.stack(
        [piece.reshape(own_rows, owners, hidden_rows) for piece in in_order(up_pieces, blk)], axis=2
    ).reshape(own_rows, owners * blocks * hidden_rows)
    out_pieces = [dot_nn(seq_pick, piece) for piece in spread(sum_out)]
    grad_w_out = jnp.concatenate(in_order(out_pieces, blk), axis=1)
    qkv_pieces = spread(sum_qkv)
    qkv_columns = [
        dot_nn(
            blk_pick,
            jnp.concatenate([piece[k * blk_rows : (k + 1) * blk_rows] for piece in qkv_pieces]),
        )
        for k in range(seqs)
    ]
    grad_qkv = jnp.stack(
        [piece.reshape(own_rows, 3, head_width) for piece in in_order(qkv_columns, seq)], axis=2
    ).reshape(own_rows, 3 * width)
    return (
        activations[None],
        grad_tokens[None],
        mine[0:2],
        mine[2:4],
        mine[4:8],
        up_total,
        grad_qkv,
        grad_w_out,
        grad_up,
        grad_down,
    )


def solution(mesh):
    rows = P("fsdp", ("blk", "seq"), None)
    split = P("fsdp", None)
    return jax.shard_map(
        shards,
        mesh=mesh,
        in_specs=(rows, split, P(), P(), P(), P(), split, split, split, split, rows),
        out_specs=(
            rows,
            rows,
            P(None, "fsdp"),
            P(None, "fsdp"),
            P(None, "fsdp"),
            P("fsdp"),
            split,
            split,
            split,
            split,
        ),
        check_vma=False,
    )
```

```python
import functools

import jax
import jax.numpy as jnp
from jax import lax
from jax.experimental import pallas as pl
from jax.experimental.pallas import tpu as pltpu
from jax.sharding import PartitionSpec as P

HD = 64
EPSILON = 1e-06
MASKED = -1e30
SCALE = HD ** (-0.5)
BF = jnp.bfloat16
F32 = jnp.float32
VMEM_LIMIT = 44 * 1024 * 1024


def dot_nn(left_side, right_side):
    return lax.dot_general(
        left_side, right_side, (((1,), (0,)), ((), ())), preferred_element_type=F32
    )


def dot_nt(left_side, right_side):
    return lax.dot_general(
        left_side, right_side, (((1,), (1,)), ((), ())), preferred_element_type=F32
    )


def dot_tn(left_side, right_side):
    return lax.dot_general(
        left_side, right_side, (((0,), (0,)), ((), ())), preferred_element_type=F32
    )


def swap(array, axis, bits):
    return lax.ppermute(array, axis, [(i, i ^ bits) for i in range(lax.axis_size(axis))])


def from_all(array, axis):
    return [array] + [swap(array, axis, j) for j in range(1, lax.axis_size(axis))]


def doubled(array, axis):
    pieces = {0: array}
    bit = lax.axis_size(axis) // 2
    while bit:
        pieces.update({j | bit: swap(piece, axis, bit) for j, piece in list(pieces.items())})
        bit //= 2
    return [pieces[j] for j in range(lax.axis_size(axis))]


def piece_bias(counts_ref, first_piece, pieces, slot_rows):
    row = lax.broadcasted_iota(jnp.int32, (pieces * slot_rows, 1), 0)
    limit = jnp.zeros_like(row)
    for piece in range(pieces):
        end = counts_ref[first_piece + piece] + piece * slot_rows
        limit = jnp.where(row >= piece * slot_rows, end, limit)
    return jnp.where(row < limit, 0.0, MASKED)


def attend_kernel(blocks, heads, pieces, slot_rows, counts_ref, q_ref, *refs):
    kv_refs, (out_ref, log_ref) = refs[:blocks], refs[blocks:]
    width = heads * HD
    biases = [piece_bias(counts_ref, m * pieces, pieces, slot_rows) for m in range(blocks)]
    for head in range(heads):
        low, high = head * HD, (head + 1) * HD
        query = q_ref[:, low:high] * SCALE
        scores = [dot_nt(kv[:, low:high], query) + bias for kv, bias in zip(kv_refs, biases)]
        top = functools.reduce(
            jnp.maximum, [jnp.max(block, axis=0, keepdims=True) for block in scores]
        )
        powers = [jnp.exp(block - top) for block in scores]
        total = sum(jnp.sum(block, axis=0, keepdims=True) for block in powers)
        inverse = 1.0 / total
        result = sum(
            dot_tn((block * inverse).astype(BF), kv[:, width + low : width + high])
            for block, kv in zip(powers, kv_refs)
        )
        out_ref[:, low:high] = result.astype(BF)
        log_ref[head : head + 1, :] = top + jnp.log(total)


def attend_back_kernel(blocks, heads, pieces, slot_rows, counts_ref, q_ref, log_ref, d_ref, *refs):
    kv_refs, dq_ref, dkv_refs = refs[:blocks], refs[blocks], refs[blocks + 1 :]
    width = heads * HD
    biases = [piece_bias(counts_ref, m * pieces, pieces, slot_rows) for m in range(blocks)]
    for head in range(heads):
        low, high = head * HD, (head + 1) * HD
        query = q_ref[:, low:high] * SCALE
        d_out = d_ref[:, low:high]
        log_row = log_ref[head : head + 1, :]
        softs, d_softs, delta = [], [], 0.0
        for kv, bias in zip(kv_refs, biases):
            soft = jnp.exp(dot_nt(kv[:, low:high], query) + bias - log_row)
            d_soft = dot_nt(kv[:, width + low : width + high], d_out)
            delta = delta + jnp.sum(soft * d_soft, axis=0, keepdims=True)
            softs.append(soft)
            d_softs.append(d_soft)
        d_query = 0.0
        for kv, dkv, soft, d_soft in zip(kv_refs, dkv_refs, softs, d_softs):
            d_scores = (soft * (d_soft - delta)).astype(BF)
            d_query = d_query + dot_tn(d_scores, kv[:, low:high])
            dkv[:, low:high] = dot_nn(d_scores, query).astype(dkv.dtype)
            dkv[:, width + low : width + high] = dot_nn(soft.astype(BF), d_out).astype(dkv.dtype)
        dq_ref[:, low:high] = (d_query * SCALE).astype(BF)


def attend(counts, queries, kv_blocks, slot_rows):
    rows, width = queries.shape
    blocks, heads = len(kv_blocks), width // HD
    pieces = kv_blocks[0].shape[0] // slot_rows
    return pl.pallas_call(
        functools.partial(attend_kernel, blocks, heads, pieces, slot_rows),
        out_shape=(
            jax.ShapeDtypeStruct((rows, width), BF),
            jax.ShapeDtypeStruct((heads, rows), F32),
        ),
        in_specs=[pl.BlockSpec(memory_space=pltpu.SMEM)]
        + [pl.BlockSpec(memory_space=pltpu.VMEM)] * (1 + blocks),
        out_specs=(pl.BlockSpec(memory_space=pltpu.VMEM),) * 2,
        compiler_params=pltpu.CompilerParams(vmem_limit_bytes=VMEM_LIMIT),
        cost_estimate=pl.CostEstimate(
            flops=4 * rows * blocks * rows * width,
            bytes_accessed=2 * rows * width * (2 + 2 * blocks),
            transcendentals=rows * rows * blocks * heads,
        ),
        name="attend",
    )(counts, queries, *kv_blocks)


def attend_back(counts, queries, log_total, d_out, kv_blocks, slot_rows):
    rows, width = queries.shape
    blocks, heads = len(kv_blocks), width // HD
    pieces = kv_blocks[0].shape[0] // slot_rows
    return pl.pallas_call(
        functools.partial(attend_back_kernel, blocks, heads, pieces, slot_rows),
        out_shape=(jax.ShapeDtypeStruct((rows, width), BF),)
        + tuple(
            jax.ShapeDtypeStruct(block.shape, F32 if m == 0 else BF)
            for m, block in enumerate(kv_blocks)
        ),
        in_specs=[pl.BlockSpec(memory_space=pltpu.SMEM)]
        + [pl.BlockSpec(memory_space=pltpu.VMEM)] * (3 + blocks),
        out_specs=(pl.BlockSpec(memory_space=pltpu.VMEM),) * (1 + blocks),
        compiler_params=pltpu.CompilerParams(vmem_limit_bytes=VMEM_LIMIT),
        cost_estimate=pl.CostEstimate(
            flops=10 * rows * blocks * rows * width,
            bytes_accessed=2 * rows * width * (3 + 5 * blocks),
            transcendentals=rows * rows * blocks * heads,
        ),
        name="attend_back",
    )(counts, queries, log_total, d_out, *kv_blocks)


def normalised(matrix_rows):
    centre = matrix_rows - jnp.mean(matrix_rows, axis=-1, keepdims=True)
    inverse = lax.rsqrt(jnp.mean(centre * centre, axis=-1, keepdims=True) + EPSILON)
    return centre * inverse, inverse


def norm_back(upstream, unit_rows, inverse, gain_row):
    scaled = upstream * gain_row
    d_rows = inverse * (
        scaled
        - jnp.mean(scaled, axis=-1, keepdims=True)
        - unit_rows * jnp.mean(scaled * unit_rows, axis=-1, keepdims=True)
    )
    return d_rows, jnp.sum(upstream * unit_rows, axis=0), jnp.sum(upstream, axis=0)


def after(value, *others):
    return lax.optimization_barrier((value, others))[0]


def take(array, index, size=1):
    return lax.dynamic_slice_in_dim(array, index, size, axis=0)


def core_sums(grads, own):
    owners, rows, columns = grads.shape
    pairs = grads.reshape(owners // 2, 2, rows, columns)
    bit = own % 2
    sent = lax.dynamic_slice_in_dim(pairs, 1 - bit, 1, axis=1)[:, 0]
    kept = lax.dynamic_slice_in_dim(pairs, bit, 1, axis=1)[:, 0]
    return kept.astype(F32) + swap(sent.astype(BF), "fsdp", 1).astype(F32)


def owner_sums(halved, own):
    bit = 2
    while bit < lax.axis_size("fsdp"):
        pairs = halved.reshape(halved.shape[0] // 2, 2, *halved.shape[1:])
        high = (own // bit) % 2
        sent = lax.dynamic_slice_in_dim(pairs, 1 - high, 1, axis=1)[:, 0]
        kept = lax.dynamic_slice_in_dim(pairs, high, 1, axis=1)[:, 0]
        halved = kept + swap(sent.astype(BF), "fsdp", bit).astype(F32)
        bit *= 2
    return halved[0]


def chunk_sums(array, axis, index):
    count = lax.axis_size(axis)
    rows = array.shape[0] // count
    total = take(array, index * rows, rows)
    for j in range(1, count):
        sent = take(array, (index ^ j) * rows, rows).astype(BF)
        total = total + swap(sent, axis, j).astype(F32)
    return total.astype(BF)


def split_sums(array, axis):
    count = lax.axis_size(axis)
    rows = array.shape[0] // count
    own = array[:rows].astype(F32)
    for j in range(1, count):
        own = own + swap(array[j * rows : (j + 1) * rows].astype(BF), axis, j).astype(F32)
    return own


def sum_over(array, axes):
    for name in axes:
        bit = 1
        while bit < lax.axis_size(name):
            array = array + swap(array, name, bit)
            bit *= 2
    return array


def in_order(pieces, index):
    result = []
    for place in range(len(pieces)):
        chosen = pieces[place]
        for other in range(1, len(pieces)):
            chosen = jnp.where(index == other, pieces[place ^ other], chosen)
        result.append(chosen)
    return result


def place_kernel(seqs, blocks, layouts, place_ref, *refs):
    pieces = refs[: blocks * seqs]
    outs = refs[blocks * seqs : -2]
    held, sems = refs[-2:]
    blk, seq = place_ref[0], place_ref[1]
    copies = [
        pltpu.make_async_copy(
            pieces[m * seqs + k],
            held.at[jnp.bitwise_xor(blk, m), jnp.bitwise_xor(seq, k)],
            sems.at[m * seqs + k],
        )
        for m in range(blocks)
        for k in range(seqs)
    ]
    for copy in copies:
        copy.start()
    for copy in copies:
        copy.wait()
    for out, spots in zip(outs, layouts):
        for b in range(blocks):
            for k in range(seqs):
                for first, size, row, column in spots(b, k):
                    piece = held[b, k, :, first : first + size]
                    out[row : row + piece.shape[0], column : column + size] = piece.astype(F32)


def put_in_place(pieces, blk, seq, shapes, layouts, label):
    blocks, seqs = len(pieces), len(pieces[0])
    piece = pieces[0][0]
    return pl.pallas_call(
        functools.partial(place_kernel, seqs, blocks, layouts),
        out_shape=tuple(jax.ShapeDtypeStruct(shape, F32) for shape in shapes),
        in_specs=[pl.BlockSpec(memory_space=pltpu.SMEM)]
        + [pl.BlockSpec(memory_space=pl.ANY)] * (blocks * seqs),
        out_specs=(pl.BlockSpec(memory_space=pltpu.VMEM),) * len(shapes),
        scratch_shapes=[
            pltpu.VMEM((blocks, seqs) + piece.shape, BF),
            pltpu.SemaphoreType.DMA((blocks * seqs,)),
        ],
        compiler_params=pltpu.CompilerParams(vmem_limit_bytes=VMEM_LIMIT),
        cost_estimate=pl.CostEstimate(
            flops=0, bytes_accessed=6 * blocks * seqs * piece.size, transcendentals=0
        ),
        name=label,
    )(jnp.stack([blk, seq]), *[one for row in pieces for one in row])


def shards(
    tokens, counts, norm_gain, norm_bias, vec_bias, up_bias, w_qkv, w_out, w_up, w_down, grad_out
):
    owners, blocks, seqs = (lax.axis_size(name) for name in ("fsdp", "blk", "seq"))
    own, blk, seq = (lax.axis_index(name) for name in ("fsdp", "blk", "seq"))
    rows, width = tokens.shape[1:]
    head_width = width // seqs
    own_rows = width // owners
    hidden_rows = w_down.shape[0] // blocks
    hidden_width = hidden_rows * owners
    out_width = width // blocks

    gains = norm_gain.astype(F32)
    shifts = norm_bias.astype(F32)
    biases = vec_bias.astype(F32)

    inputs = tokens[0]
    unit1, inverse1 = normalised(inputs)
    normed1 = (unit1 * gains[0] + shifts[0]).astype(BF)
    qkv_mine = jnp.concatenate(
        [
            lax.dynamic_slice_in_dim(w_qkv, part * width + seq * head_width, head_width, axis=1)
            for part in range(3)
        ],
        axis=1,
    )
    normed1_all = jnp.concatenate(from_all(normed1, "seq"))
    qkv_full = jnp.concatenate(in_order(doubled(qkv_mine, "fsdp"), own))

    full_out = lax.all_gather(w_out, "fsdp", axis=0, tiled=True)
    up_late, down_late, grad_late = after((w_up, w_down, grad_out), normed1, qkv_mine)
    up_mine = jnp.concatenate(
        [
            lax.dynamic_slice_in_dim(
                up_late, (i * blocks + blk) * hidden_rows, hidden_rows, axis=1
            )
            for i in range(owners)
        ],
        axis=1,
    )
    full_up = lax.all_gather(up_mine, "fsdp", axis=0, tiled=True)
    down_mine = take(down_late, blk * hidden_rows, hidden_rows)
    full_down = jnp.concatenate(in_order(doubled(down_mine, "fsdp"), own))
    up_shift = jnp.concatenate(
        [
            lax.dynamic_slice_in_dim(up_bias, (i * blocks + blk) * hidden_rows, hidden_rows)
            for i in range(owners)
        ]
    ).astype(F32)
    qkv_shift = jnp.concatenate(
        [
            lax.dynamic_slice_in_dim(biases[0], seq * head_width, head_width),
            jnp.zeros((head_width,), F32),
            lax.dynamic_slice_in_dim(biases[1], seq * head_width, head_width),
        ]
    )
    own_count = counts[0, blk * seqs + seq]
    own_valid = lax.broadcasted_iota(jnp.int32, (rows, 1), 0) < own_count
    key_counts = jnp.stack(
        [counts[0, (blk ^ m) * seqs + (seq ^ k)] for m in range(blocks) for k in range(seqs)]
    )
    grad_rows = jnp.where(own_valid, grad_late[0], 0.0)
    d_outcome = grad_rows.astype(BF)
    d_outcome_all = jnp.concatenate(from_all(d_outcome, "blk"))

    key_value = (
        dot_nn(normed1_all, qkv_full[:, head_width:]) + qkv_shift[head_width:]
    ).astype(BF)
    kv_blocks = from_all(key_value, "blk")
    queries = (
        dot_nn(after(normed1_all, key_value), qkv_full[:, :head_width]) + qkv_shift[:head_width]
    ).astype(BF)
    attended, log_total = attend(key_counts, queries, kv_blocks, rows)
    att_pieces = [attended[:rows]] + [
        swap(attended[k * rows : (k + 1) * rows], "seq", k) for k in range(1, seqs)
    ]
    token_att = jnp.concatenate(in_order(att_pieces, seq), axis=1)
    middle = inputs + dot_nn(token_att, full_out) + biases[2]
    unit2, inverse2 = normalised(middle)
    normed2 = (unit2 * gains[1] + shifts[1]).astype(BF)

    d_hidden = lax.optimization_barrier(dot_nt(after(d_outcome_all, normed2), full_down))
    normed2_all = jnp.concatenate(from_all(normed2, "blk"))
    up_proj = dot_nn(after(normed2_all, d_hidden), full_up) + up_shift
    chance = 0.5 * (1.0 + lax.erf(up_proj * (0.5**0.5)))
    hidden = (up_proj * chance).astype(BF)
    slope = chance + up_proj * (jnp.exp(-0.5 * up_proj * up_proj) * 0.3989422804014327)
    d_up = (d_hidden * slope).astype(BF)
    d_normed2_parts = dot_nt(d_up, full_up).astype(BF)
    d_normed2 = split_sums(d_normed2_parts, "blk")
    half_down = core_sums(
        dot_tn(after(hidden, d_normed2_parts), d_outcome_all).astype(BF).reshape(
            owners, hidden_rows, width
        ),
        own,
    )
    d_middle_norm, d_gain_two, d_shift_two = norm_back(d_normed2, unit2, inverse2, gains[1])
    d_middle = grad_rows + d_middle_norm
    d_branch = d_middle.astype(BF)
    d_head_pieces = [
        dot_nt(d_branch, take(full_out, (seq ^ k) * head_width, head_width)).astype(BF)
        for k in range(seqs)
    ]
    d_attended = jnp.concatenate(
        [d_head_pieces[0]] + [swap(d_head_pieces[k], "seq", k) for k in range(1, seqs)]
    )
    branch_late, att_late, d_up_late = after((d_branch, token_att, d_up), *d_head_pieces)
    att_all = jnp.concatenate(from_all(att_late, "blk"))
    branch_all = jnp.concatenate(
        [
            lax.dynamic_slice_in_dim(branch_late, blk * out_width, out_width, axis=1),
        ]
        + [
            swap(
                lax.dynamic_slice_in_dim(branch_late, (blk ^ m) * out_width, out_width, axis=1),
                "blk",
                m,
            )
            for m in range(1, blocks)
        ]
    )
    grads_up = jnp.concatenate(
        [dot_tn(normed2_all, d_up_late).astype(BF), dot_tn(att_all, branch_all).astype(BF)], axis=1
    )
    half_up = core_sums(grads_up.reshape(owners, own_rows, hidden_width + out_width), own)

    d_attended = after(d_attended, half_down, half_up)
    back = attend_back(key_counts, queries, log_total, d_attended, kv_blocks, rows)
    own_down = owner_sums(half_down, own)
    own_up = owner_sums(half_up, own)
    d_query, d_kv = back[0], back[1]
    for m in range(1, blocks):
        d_kv = d_kv + swap(back[1 + m], "blk", m).astype(F32)
    d_kv = after(d_kv.astype(BF), own_down)
    d_projected = jnp.concatenate([d_query, d_kv], axis=1)
    d_normed1_parts = dot_nt(d_projected, qkv_full).astype(BF)
    d_normed1 = split_sums(d_normed1_parts, "seq")
    sum_down = chunk_sums(own_down, "seq", seq)

    normed1_late, hidden_late = after((normed1_all, hidden), d_normed1_parts)
    half_qkv = core_sums(
        dot_tn(normed1_late, d_projected).astype(BF).reshape(owners, own_rows, 3 * head_width), own
    )
    outcome = split_sums(dot_nn(hidden_late, full_down), "blk")
    activations = jnp.where(own_valid, middle + outcome + biases[3], 0.0)
    sum_up = chunk_sums(own_up, "seq", seq)
    sum_qkv = chunk_sums(owner_sums(half_qkv, own), "blk", blk)
    d_normed1 = after(d_normed1, sum_down)
    d_inputs, d_gain_one, d_shift_one = norm_back(d_normed1, unit1, inverse1, gains[0])
    grad_tokens = d_middle + d_inputs

    bias_sums = jnp.sum(d_projected.astype(F32), axis=0)
    is_seq = (jnp.arange(seqs) == seq)[:, None]
    is_blk = (jnp.arange(blocks) == blk)[None, :, None]
    up_sums = jnp.sum(d_up.astype(F32), axis=0).reshape(owners, 1, hidden_rows)
    vectors = jnp.concatenate(
        [
            d_gain_one,
            d_gain_two,
            d_shift_one,
            d_shift_two,
            jnp.where(is_seq, bias_sums[None, :head_width], 0.0).reshape(-1),
            jnp.where(is_seq, bias_sums[None, 2 * head_width :], 0.0).reshape(-1),
            jnp.sum(d_branch.astype(F32), axis=0),
            jnp.sum(d_outcome.astype(F32), axis=0),
            jnp.where(is_blk, up_sums, 0.0).reshape(-1),
        ]
    ).reshape(-1, 128)
    vectors = sum_over(vectors, ("fsdp", "seq", "blk")).reshape(-1)
    mine = lax.dynamic_slice_in_dim(
        vectors[: 8 * width].reshape(8, width), own * own_rows, own_rows, axis=1
    )
    up_total = lax.dynamic_slice_in_dim(
        vectors[8 * width :], own * blocks * hidden_rows, blocks * hidden_rows
    )

    def spread(array):
        over_seq = from_all(array, "seq")
        over_blk = from_all(jnp.stack(over_seq), "blk")
        return [[piece[k] for k in range(seqs)] for piece in over_blk]

    chunk, seq_rows, blk_rows = hidden_rows // seqs, own_rows // seqs, own_rows // blocks
    (grad_down,) = put_in_place(
        spread(sum_down),
        blk,
        seq,
        [(blocks * hidden_rows, width)],
        [lambda b, k: [(0, width, b * hidden_rows + k * chunk, 0)]],
        "place_down",
    )
    grad_up, grad_w_out = put_in_place(
        spread(sum_up),
        blk,
        seq,
        [(own_rows, blocks * hidden_width), (own_rows, width)],
        [
            lambda b, k: [
                (i * hidden_rows, hidden_rows, k * seq_rows, (i * blocks + b) * hidden_rows)
                for i in range(owners)
            ],
            lambda b, k: [(hidden_width, out_width, k * seq_rows, b * out_width)],
        ],
        "place_up",
    )
    (grad_qkv,) = put_in_place(
        spread(sum_qkv),
        blk,
        seq,
        [(own_rows, 3 * width)],
        [
            lambda b, k: [
                (i * head_width, head_width, b * blk_rows, i * width + k * head_width)
                for i in range(3)
            ]
        ],
        "place_qkv",
    )
    return (
        activations[None],
        grad_tokens[None],
        mine[0:2],
        mine[2:4],
        mine[4:8],
        up_total,
        grad_qkv,
        grad_w_out,
        grad_up,
        grad_down,
    )


def solution(mesh):
    rows = P("fsdp", ("blk", "seq"), None)
    split = P("fsdp", None)
    return jax.shard_map(
        shards,
        mesh=mesh,
        in_specs=(rows, split, P(), P(), P(), P(), split, split, split, split, rows),
        out_specs=(
            rows,
            rows,
            P(None, "fsdp"),
            P(None, "fsdp"),
            P(None, "fsdp"),
            P("fsdp"),
            split,
            split,
            split,
            split,
        ),
        check_vma=False,
    )
```

```python
import functools

import jax
import jax.numpy as jnp
from jax import lax
from jax.experimental import pallas as pl
from jax.experimental.pallas import tpu as pltpu
from jax.sharding import PartitionSpec as P

HD = 64
EPSILON = 1e-06
MASKED = -1e30
SCALE = HD ** (-0.5)
BF = jnp.bfloat16
F32 = jnp.float32
VMEM_LIMIT = 44 * 1024 * 1024


def dot_nn(left_side, right_side):
    return lax.dot_general(
        left_side, right_side, (((1,), (0,)), ((), ())), preferred_element_type=F32
    )


def dot_nt(left_side, right_side):
    return lax.dot_general(
        left_side, right_side, (((1,), (1,)), ((), ())), preferred_element_type=F32
    )


def dot_tn(left_side, right_side):
    return lax.dot_general(
        left_side, right_side, (((0,), (0,)), ((), ())), preferred_element_type=F32
    )


def swap(array, axis, bits):
    return lax.ppermute(array, axis, [(i, i ^ bits) for i in range(lax.axis_size(axis))])


def from_all(array, axis):
    return [array] + [swap(array, axis, j) for j in range(1, lax.axis_size(axis))]


def doubled(array, axis):
    pieces = {0: array}
    bit = lax.axis_size(axis) // 2
    while bit:
        pieces.update({j | bit: swap(piece, axis, bit) for j, piece in list(pieces.items())})
        bit //= 2
    return [pieces[j] for j in range(lax.axis_size(axis))]


def piece_bias(place_ref, counts_ref, block, pieces, slot_rows):
    row = lax.broadcasted_iota(jnp.int32, (pieces * slot_rows, 1), 0)
    limit = jnp.zeros_like(row)
    for piece in range(pieces):
        held = (place_ref[0] ^ block) * pieces + (place_ref[1] ^ piece)
        end = counts_ref[0, held] + piece * slot_rows
        limit = jnp.where(row >= piece * slot_rows, end, limit)
    return jnp.where(row < limit, 0.0, MASKED)


def attend_kernel(blocks, heads, pieces, slot_rows, place_ref, counts_ref, q_ref, *refs):
    kv_refs, (out_ref, log_ref) = refs[:blocks], refs[blocks:]
    width = heads * HD
    biases = [piece_bias(place_ref, counts_ref, m, pieces, slot_rows) for m in range(blocks)]
    for head in range(heads):
        low, high = head * HD, (head + 1) * HD
        query = q_ref[:, low:high] * SCALE
        scores = [dot_nt(kv[:, low:high], query) + bias for kv, bias in zip(kv_refs, biases)]
        top = functools.reduce(
            jnp.maximum, [jnp.max(block, axis=0, keepdims=True) for block in scores]
        )
        powers = [jnp.exp(block - top) for block in scores]
        total = sum(jnp.sum(block, axis=0, keepdims=True) for block in powers)
        inverse = 1.0 / total
        result = sum(
            dot_tn((block * inverse).astype(BF), kv[:, width + low : width + high])
            for block, kv in zip(powers, kv_refs)
        )
        out_ref[:, low:high] = result.astype(BF)
        log_ref[head : head + 1, :] = top + jnp.log(total)


def attend_back_kernel(
    blocks, heads, pieces, slot_rows, place_ref, counts_ref, q_ref, log_ref, d_ref, *refs
):
    kv_refs, dq_ref, dkv_refs = refs[:blocks], refs[blocks], refs[blocks + 1 :]
    width = heads * HD
    biases = [piece_bias(place_ref, counts_ref, m, pieces, slot_rows) for m in range(blocks)]
    for head in range(heads):
        low, high = head * HD, (head + 1) * HD
        query = q_ref[:, low:high] * SCALE
        d_out = d_ref[:, low:high]
        log_row = log_ref[head : head + 1, :]
        softs, d_softs, delta = [], [], 0.0
        for kv, bias in zip(kv_refs, biases):
            soft = jnp.exp(dot_nt(kv[:, low:high], query) + bias - log_row)
            d_soft = dot_nt(kv[:, width + low : width + high], d_out)
            delta = delta + jnp.sum(soft * d_soft, axis=0, keepdims=True)
            softs.append(soft)
            d_softs.append(d_soft)
        d_query = 0.0
        for kv, dkv, soft, d_soft in zip(kv_refs, dkv_refs, softs, d_softs):
            d_scores = (soft * (d_soft - delta)).astype(BF)
            d_query = d_query + dot_tn(d_scores, kv[:, low:high])
            dkv[:, low:high] = dot_nn(d_scores, query).astype(dkv.dtype)
            dkv[:, width + low : width + high] = dot_nn(soft.astype(BF), d_out).astype(dkv.dtype)
        dq_ref[:, low:high] = (d_query * SCALE).astype(BF)


def attend(place, counts, queries, kv_blocks, slot_rows):
    rows, width = queries.shape
    blocks, heads = len(kv_blocks), width // HD
    pieces = kv_blocks[0].shape[0] // slot_rows
    return pl.pallas_call(
        functools.partial(attend_kernel, blocks, heads, pieces, slot_rows),
        out_shape=(
            jax.ShapeDtypeStruct((rows, width), BF),
            jax.ShapeDtypeStruct((heads, rows), F32),
        ),
        in_specs=[pl.BlockSpec(memory_space=pltpu.SMEM)] * 2
        + [pl.BlockSpec(memory_space=pltpu.VMEM)] * (1 + blocks),
        out_specs=(pl.BlockSpec(memory_space=pltpu.VMEM),) * 2,
        compiler_params=pltpu.CompilerParams(vmem_limit_bytes=VMEM_LIMIT),
        cost_estimate=pl.CostEstimate(
            flops=4 * rows * blocks * rows * width,
            bytes_accessed=2 * rows * width * (2 + 2 * blocks),
            transcendentals=rows * rows * blocks * heads,
        ),
        name="attend",
    )(place, counts, queries, *kv_blocks)


def attend_back(place, counts, queries, log_total, d_out, kv_blocks, slot_rows):
    rows, width = queries.shape
    blocks, heads = len(kv_blocks), width // HD
    pieces = kv_blocks[0].shape[0] // slot_rows
    return pl.pallas_call(
        functools.partial(attend_back_kernel, blocks, heads, pieces, slot_rows),
        out_shape=(jax.ShapeDtypeStruct((rows, width), BF),)
        + tuple(
            jax.ShapeDtypeStruct(block.shape, F32 if m == 0 else BF)
            for m, block in enumerate(kv_blocks)
        ),
        in_specs=[pl.BlockSpec(memory_space=pltpu.SMEM)] * 2
        + [pl.BlockSpec(memory_space=pltpu.VMEM)] * (3 + blocks),
        out_specs=(pl.BlockSpec(memory_space=pltpu.VMEM),) * (1 + blocks),
        compiler_params=pltpu.CompilerParams(vmem_limit_bytes=VMEM_LIMIT),
        cost_estimate=pl.CostEstimate(
            flops=10 * rows * blocks * rows * width,
            bytes_accessed=2 * rows * width * (3 + 5 * blocks),
            transcendentals=rows * rows * blocks * heads,
        ),
        name="attend_back",
    )(place, counts, queries, log_total, d_out, *kv_blocks)


def normalised(matrix_rows):
    centre = matrix_rows - jnp.mean(matrix_rows, axis=-1, keepdims=True)
    inverse = lax.rsqrt(jnp.mean(centre * centre, axis=-1, keepdims=True) + EPSILON)
    return centre * inverse, inverse


def norm_back(upstream, unit_rows, inverse, gain_row):
    scaled = upstream * gain_row
    d_rows = inverse * (
        scaled
        - jnp.mean(scaled, axis=-1, keepdims=True)
        - unit_rows * jnp.mean(scaled * unit_rows, axis=-1, keepdims=True)
    )
    return d_rows, jnp.sum(upstream * unit_rows, axis=0), jnp.sum(upstream, axis=0)


def after(value, *others):
    return lax.optimization_barrier((value, others))[0]


def take(array, index, size=1):
    return lax.dynamic_slice_in_dim(array, index, size, axis=0)


def core_sums(grads, own):
    owners, rows, columns = grads.shape
    pairs = grads.reshape(owners // 2, 2, rows, columns)
    bit = own % 2
    sent = lax.dynamic_slice_in_dim(pairs, 1 - bit, 1, axis=1)[:, 0]
    kept = lax.dynamic_slice_in_dim(pairs, bit, 1, axis=1)[:, 0]
    return kept.astype(F32) + swap(sent.astype(BF), "fsdp", 1).astype(F32)


def owner_sums(halved, own):
    bit = 2
    while bit < lax.axis_size("fsdp"):
        pairs = halved.reshape(halved.shape[0] // 2, 2, *halved.shape[1:])
        high = (own // bit) % 2
        sent = lax.dynamic_slice_in_dim(pairs, 1 - high, 1, axis=1)[:, 0]
        kept = lax.dynamic_slice_in_dim(pairs, high, 1, axis=1)[:, 0]
        halved = kept + swap(sent.astype(BF), "fsdp", bit).astype(F32)
        bit *= 2
    return halved[0]


def chunk_sums(array, axis, index):
    count = lax.axis_size(axis)
    rows = array.shape[0] // count
    total = take(array, index * rows, rows)
    for j in range(1, count):
        sent = take(array, (index ^ j) * rows, rows).astype(BF)
        total = total + swap(sent, axis, j).astype(F32)
    return total.astype(BF)


def split_sums(array, axis):
    count = lax.axis_size(axis)
    rows = array.shape[0] // count
    own = array[:rows].astype(F32)
    for j in range(1, count):
        own = own + swap(array[j * rows : (j + 1) * rows].astype(BF), axis, j).astype(F32)
    return own


def sum_over(array, axes):
    for name in axes:
        bit = 1
        while bit < lax.axis_size(name):
            array = array + swap(array, name, bit)
            bit *= 2
    return array


def in_order(pieces, index):
    result = []
    for place in range(len(pieces)):
        chosen = pieces[place]
        for other in range(1, len(pieces)):
            chosen = jnp.where(index == other, pieces[place ^ other], chosen)
        result.append(chosen)
    return result


def place_kernel(seqs, blocks, layouts, place_ref, *refs):
    pieces = refs[: blocks * seqs]
    outs = refs[blocks * seqs : -2]
    held, sems = refs[-2:]
    blk, seq = place_ref[0], place_ref[1]
    copies = [
        pltpu.make_async_copy(
            pieces[m * seqs + k],
            held.at[jnp.bitwise_xor(blk, m), jnp.bitwise_xor(seq, k)],
            sems.at[m * seqs + k],
        )
        for m in range(blocks)
        for k in range(seqs)
    ]
    for copy in copies:
        copy.start()
    for copy in copies:
        copy.wait()
    for out, spots in zip(outs, layouts):
        for b in range(blocks):
            for k in range(seqs):
                for first, size, row, column in spots(b, k):
                    piece = held[b, k, :, first : first + size]
                    out[row : row + piece.shape[0], column : column + size] = piece.astype(F32)


def put_in_place(pieces, place, shapes, layouts, label):
    blocks, seqs = len(pieces), len(pieces[0])
    piece = pieces[0][0]
    return pl.pallas_call(
        functools.partial(place_kernel, seqs, blocks, layouts),
        out_shape=tuple(jax.ShapeDtypeStruct(shape, F32) for shape in shapes),
        in_specs=[pl.BlockSpec(memory_space=pltpu.SMEM)]
        + [pl.BlockSpec(memory_space=pl.ANY)] * (blocks * seqs),
        out_specs=(pl.BlockSpec(memory_space=pltpu.VMEM),) * len(shapes),
        scratch_shapes=[
            pltpu.VMEM((blocks, seqs) + piece.shape, BF),
            pltpu.SemaphoreType.DMA((blocks * seqs,)),
        ],
        compiler_params=pltpu.CompilerParams(vmem_limit_bytes=VMEM_LIMIT),
        cost_estimate=pl.CostEstimate(
            flops=0, bytes_accessed=6 * blocks * seqs * piece.size, transcendentals=0
        ),
        name=label,
    )(place, *[one for row in pieces for one in row])


def shards(
    tokens, counts, norm_gain, norm_bias, vec_bias, up_bias, w_qkv, w_out, w_up, w_down, grad_out
):
    owners, blocks, seqs = (lax.axis_size(name) for name in ("fsdp", "blk", "seq"))
    own, blk, seq = (lax.axis_index(name) for name in ("fsdp", "blk", "seq"))
    rows, width = tokens.shape[1:]
    head_width = width // seqs
    own_rows = width // owners
    hidden_rows = w_down.shape[0] // blocks
    hidden_width = hidden_rows * owners
    out_width = width // blocks

    gains = norm_gain.astype(F32)
    shifts = norm_bias.astype(F32)
    biases = vec_bias.astype(F32)

    inputs = tokens[0]
    unit1, inverse1 = normalised(inputs)
    normed1 = (unit1 * gains[0] + shifts[0]).astype(BF)
    qkv_mine = jnp.concatenate(
        [
            lax.dynamic_slice_in_dim(w_qkv, part * width + seq * head_width, head_width, axis=1)
            for part in range(3)
        ],
        axis=1,
    )
    normed1_all = jnp.concatenate(from_all(normed1, "seq"))
    qkv_full = jnp.concatenate(in_order(doubled(qkv_mine, "fsdp"), own))

    up_late, down_late, out_late, grad_late = after(
        (w_up, w_down, w_out, grad_out), normed1, qkv_mine
    )
    full_out = jnp.concatenate(in_order(doubled(out_late, "fsdp"), own))
    up_mine = jnp.concatenate(
        [
            lax.dynamic_slice_in_dim(
                up_late, (i * blocks + blk) * hidden_rows, hidden_rows, axis=1
            )
            for i in range(owners)
        ],
        axis=1,
    )
    full_up = lax.all_gather(up_mine, "fsdp", axis=0, tiled=True)
    down_mine = take(down_late, blk * hidden_rows, hidden_rows)
    full_down = lax.all_gather(down_mine, "fsdp", axis=0, tiled=True)
    up_shift = jnp.concatenate(
        [
            lax.dynamic_slice_in_dim(up_bias, (i * blocks + blk) * hidden_rows, hidden_rows)
            for i in range(owners)
        ]
    ).astype(F32)
    qkv_shift = jnp.concatenate(
        [
            lax.dynamic_slice_in_dim(biases[0], seq * head_width, head_width),
            jnp.zeros((head_width,), F32),
            lax.dynamic_slice_in_dim(biases[1], seq * head_width, head_width),
        ]
    )
    own_count = counts[0, blk * seqs + seq]
    own_valid = lax.broadcasted_iota(jnp.int32, (rows, 1), 0) < own_count
    place = jnp.stack([blk, seq]).astype(jnp.int32)
    grad_rows = jnp.where(own_valid, grad_late[0], 0.0)
    d_outcome = grad_rows.astype(BF)
    d_outcome_all = jnp.concatenate(from_all(d_outcome, "blk"))

    key_value = (
        dot_nn(after(normed1_all, d_outcome_all), qkv_full[:, head_width:])
        + qkv_shift[head_width:]
    ).astype(BF)
    kv_blocks = from_all(key_value, "blk")
    queries = (
        dot_nn(after(normed1_all, key_value), qkv_full[:, :head_width]) + qkv_shift[:head_width]
    ).astype(BF)
    queries = after(queries, full_out)
    attended, log_total = attend(place, counts, queries, kv_blocks, rows)
    att_pieces = [attended[:rows]] + [
        swap(attended[k * rows : (k + 1) * rows], "seq", k) for k in range(1, seqs)
    ]
    token_att = jnp.concatenate(in_order(att_pieces, seq), axis=1)
    middle = inputs + dot_nn(token_att, full_out) + biases[2]
    unit2, inverse2 = normalised(middle)
    normed2 = (unit2 * gains[1] + shifts[1]).astype(BF)

    d_hidden = lax.optimization_barrier(dot_nt(after(d_outcome_all, normed2), full_down))
    normed2_all = jnp.concatenate(from_all(normed2, "blk"))
    up_proj = dot_nn(after(normed2_all, d_hidden), full_up) + up_shift
    chance = 0.5 * (1.0 + lax.erf(up_proj * (0.5**0.5)))
    hidden = (up_proj * chance).astype(BF)
    slope = chance + up_proj * (jnp.exp(-0.5 * up_proj * up_proj) * 0.3989422804014327)
    d_up = (d_hidden * slope).astype(BF)
    d_normed2_parts = dot_nt(d_up, full_up).astype(BF)
    d_normed2 = split_sums(d_normed2_parts, "blk")
    half_down = core_sums(
        dot_tn(after(hidden, d_normed2_parts), d_outcome_all).astype(BF).reshape(
            owners, hidden_rows, width
        ),
        own,
    )
    d_middle_norm, d_gain_two, d_shift_two = norm_back(d_normed2, unit2, inverse2, gains[1])
    d_middle = grad_rows + d_middle_norm
    d_branch = d_middle.astype(BF)
    d_head_pieces = [
        dot_nt(d_branch, take(full_out, (seq ^ k) * head_width, head_width)).astype(BF)
        for k in range(seqs)
    ]
    d_attended = jnp.concatenate(
        [d_head_pieces[0]] + [swap(d_head_pieces[k], "seq", k) for k in range(1, seqs)]
    )
    d_attended = after(d_attended, half_down)
    back = attend_back(place, counts, queries, log_total, d_attended, kv_blocks, rows)
    own_down = owner_sums(half_down, own)
    att_late, d_up_late = after((token_att, d_up), back)
    grads_up = jnp.concatenate(
        [dot_tn(normed2_all, d_up_late).astype(BF), dot_tn(att_late, d_branch).astype(BF)], axis=1
    )
    half_up = core_sums(grads_up.reshape(owners, own_rows, hidden_width + width), own)
    d_query, d_kv = back[0], back[1]
    for m in range(1, blocks):
        d_kv = d_kv + swap(back[1 + m], "blk", m).astype(F32)
    d_kv = after(d_kv.astype(BF), own_down)
    d_projected = jnp.concatenate([d_query, d_kv], axis=1)
    d_normed1_parts = dot_nt(d_projected, qkv_full).astype(BF)
    d_normed1 = split_sums(d_normed1_parts, "seq")

    normed1_late = after(normed1_all, d_normed1_parts)
    sum_down = chunk_sums(own_down, "seq", seq)
    half_qkv = core_sums(
        dot_tn(normed1_late, d_projected).astype(BF).reshape(owners, own_rows, 3 * head_width), own
    )
    own_up = owner_sums(half_up, own)
    own_out = own_up[:, hidden_width:]
    kept_out = lax.dynamic_slice_in_dim(own_out, blk * out_width, out_width, axis=1)
    for m in range(1, blocks):
        sent = lax.dynamic_slice_in_dim(own_out, (blk ^ m) * out_width, out_width, axis=1)
        kept_out = kept_out + swap(sent.astype(BF), "blk", m).astype(F32)
    sum_up = chunk_sums(
        jnp.concatenate([own_up[:, :hidden_width], kept_out], axis=1), "seq", seq
    )
    d_normed1, hidden_late = after((d_normed1, hidden), kept_out)
    outcome = split_sums(dot_nn(hidden_late, full_down), "blk")
    activations = jnp.where(own_valid, middle + outcome + biases[3], 0.0)
    sum_qkv = chunk_sums(owner_sums(half_qkv, own), "blk", blk)
    d_inputs, d_gain_one, d_shift_one = norm_back(d_normed1, unit1, inverse1, gains[0])
    grad_tokens = d_middle + d_inputs

    bias_sums = jnp.sum(d_projected.astype(F32), axis=0)
    is_seq = (jnp.arange(seqs) == seq)[:, None]
    is_blk = (jnp.arange(blocks) == blk)[None, :, None]
    up_sums = jnp.sum(d_up.astype(F32), axis=0).reshape(owners, 1, hidden_rows)
    vectors = jnp.concatenate(
        [
            d_gain_one,
            d_gain_two,
            d_shift_one,
            d_shift_two,
            jnp.where(is_seq, bias_sums[None, :head_width], 0.0).reshape(-1),
            jnp.where(is_seq, bias_sums[None, 2 * head_width :], 0.0).reshape(-1),
            jnp.sum(d_branch.astype(F32), axis=0),
            jnp.sum(d_outcome.astype(F32), axis=0),
            jnp.where(is_blk, up_sums, 0.0).reshape(-1),
        ]
    ).reshape(-1, 128)
    vectors = sum_over(after(vectors, sum_up), ("fsdp", "seq", "blk")).reshape(-1)
    mine = lax.dynamic_slice_in_dim(
        vectors[: 8 * width].reshape(8, width), own * own_rows, own_rows, axis=1
    )
    up_total = lax.dynamic_slice_in_dim(
        vectors[8 * width :], own * blocks * hidden_rows, blocks * hidden_rows
    )

    def spread(array):
        over_seq = [from_all(one, "blk") for one in from_all(array, "seq")]
        return [[one[m] for one in over_seq] for m in range(blocks)]

    chunk, seq_rows, blk_rows = hidden_rows // seqs, own_rows // seqs, own_rows // blocks
    (grad_down,) = put_in_place(
        spread(sum_down),
        place,
        [(blocks * hidden_rows, width)],
        [lambda b, k: [(0, width, b * hidden_rows + k * chunk, 0)]],
        "place_down",
    )
    grad_up, grad_w_out = put_in_place(
        spread(sum_up),
        place,
        [(own_rows, blocks * hidden_width), (own_rows, width)],
        [
            lambda b, k: [
                (i * hidden_rows, hidden_rows, k * seq_rows, (i * blocks + b) * hidden_rows)
                for i in range(owners)
            ],
            lambda b, k: [(hidden_width, out_width, k * seq_rows, b * out_width)],
        ],
        "place_up",
    )
    (grad_qkv,) = put_in_place(
        spread(after(sum_qkv, sum_up)),
        place,
        [(own_rows, 3 * width)],
        [
            lambda b, k: [
                (i * head_width, head_width, b * blk_rows, i * width + k * head_width)
                for i in range(3)
            ]
        ],
        "place_qkv",
    )
    return (
        activations[None],
        grad_tokens[None],
        mine[0:2],
        mine[2:4],
        mine[4:8],
        up_total,
        grad_qkv,
        grad_w_out,
        grad_up,
        grad_down,
    )


def solution(mesh):
    rows = P("fsdp", ("blk", "seq"), None)
    split = P("fsdp", None)
    return jax.shard_map(
        shards,
        mesh=mesh,
        in_specs=(rows, split, P(), P(), P(), P(), split, split, split, split, rows),
        out_specs=(
            rows,
            rows,
            P(None, "fsdp"),
            P(None, "fsdp"),
            P(None, "fsdp"),
            P("fsdp"),
            split,
            split,
            split,
            split,
        ),
        check_vma=False,
    )
```

```python
import functools

import jax
import jax.numpy as jnp
from jax import lax
from jax.experimental import pallas as pl
from jax.experimental.pallas import tpu as pltpu
from jax.sharding import PartitionSpec as P

HD = 64
EPSILON = 1e-06
MASKED = -1e30
SCALE = HD ** (-0.5)
BF = jnp.bfloat16
F32 = jnp.float32
VMEM_LIMIT = 44 * 1024 * 1024


def dot_nn(left_side, right_side):
    return lax.dot_general(
        left_side, right_side, (((1,), (0,)), ((), ())), preferred_element_type=F32
    )


def dot_nt(left_side, right_side):
    return lax.dot_general(
        left_side, right_side, (((1,), (1,)), ((), ())), preferred_element_type=F32
    )


def dot_tn(left_side, right_side):
    return lax.dot_general(
        left_side, right_side, (((0,), (0,)), ((), ())), preferred_element_type=F32
    )


def swap(array, axis, bits):
    return lax.ppermute(array, axis, [(i, i ^ bits) for i in range(lax.axis_size(axis))])


def from_all(array, axis):
    return [array] + [swap(array, axis, j) for j in range(1, lax.axis_size(axis))]


def doubled(array, axis):
    pieces = {0: array}
    bit = lax.axis_size(axis) // 2
    while bit:
        pieces.update({j | bit: swap(piece, axis, bit) for j, piece in list(pieces.items())})
        bit //= 2
    return [pieces[j] for j in range(lax.axis_size(axis))]


def piece_bias(place_ref, counts_ref, block, pieces, slot_rows):
    row = lax.broadcasted_iota(jnp.int32, (pieces * slot_rows, 1), 0)
    limit = jnp.zeros_like(row)
    for piece in range(pieces):
        held = (place_ref[0] ^ block) * pieces + (place_ref[1] ^ piece)
        end = counts_ref[0, held] + piece * slot_rows
        limit = jnp.where(row >= piece * slot_rows, end, limit)
    return jnp.where(row < limit, 0.0, MASKED)


def own_rows_valid(place_ref, counts_ref, seqs, rows):
    count = counts_ref[0, place_ref[0] * seqs + place_ref[1]]
    return lax.broadcasted_iota(jnp.int32, (rows, 1), 0) < count


def normalised(matrix_rows):
    centre = matrix_rows - jnp.mean(matrix_rows, axis=-1, keepdims=True)
    inverse = lax.rsqrt(jnp.mean(centre * centre, axis=-1, keepdims=True) + EPSILON)
    return centre * inverse, inverse


def norm_back(upstream, unit_rows, inverse, gain_row):
    scaled = upstream * gain_row
    return inverse * (
        scaled
        - jnp.mean(scaled, axis=-1, keepdims=True)
        - unit_rows * jnp.mean(scaled * unit_rows, axis=-1, keepdims=True)
    )


def row_of(ref, index):
    return ref[...].astype(F32)[index : index + 1]


def fetches(pieces, own, first, size, target, sems):
    return [
        pltpu.make_async_copy(
            piece.at[pl.ds(first, size)],
            target.at[pl.ds(pl.multiple_of((own ^ j) * size, 16), size)],
            sems.at[j],
        )
        for j, piece in enumerate(pieces)
    ]


def prepare_kernel(
    seqs, place_ref, counts_ref, tokens_ref, grad_ref, gain_ref, shift_ref, normed_ref, outcome_ref
):
    unit = normalised(tokens_ref[...])[0]
    normed_ref[...] = (unit * row_of(gain_ref, 0) + row_of(shift_ref, 0)).astype(BF)
    valid = own_rows_valid(place_ref, counts_ref, seqs, grad_ref.shape[0])
    outcome_ref[...] = jnp.where(valid, grad_ref[...], 0.0).astype(BF)


def attend_kernel(blocks, heads, pieces, slot_rows, place_ref, counts_ref, q_ref, *refs):
    kv_refs, out_refs, log_ref = refs[:blocks], refs[blocks:-1], refs[-1]
    width = heads * HD
    biases = [piece_bias(place_ref, counts_ref, m, pieces, slot_rows) for m in range(blocks)]
    for head in range(heads):
        low, high = head * HD, (head + 1) * HD
        query = q_ref[:, low:high] * SCALE
        scores = [dot_nt(kv[:, low:high], query) + bias for kv, bias in zip(kv_refs, biases)]
        top = functools.reduce(
            jnp.maximum, [jnp.max(block, axis=0, keepdims=True) for block in scores]
        )
        powers = [jnp.exp(block - top) for block in scores]
        total = sum(jnp.sum(block, axis=0, keepdims=True) for block in powers)
        inverse = 1.0 / total
        result = sum(
            dot_tn((block * inverse).astype(BF), kv[:, width + low : width + high])
            for block, kv in zip(powers, kv_refs)
        ).astype(BF)
        for k, out_ref in enumerate(out_refs):
            out_ref[:, low:high] = result[k * slot_rows : (k + 1) * slot_rows]
        log_ref[head : head + 1, :] = top + jnp.log(total)


def attend_back_kernel(blocks, heads, pieces, slot_rows, place_ref, counts_ref, q_ref, log_ref, *refs):
    d_refs, refs = refs[:pieces], refs[pieces:]
    kv_refs, dq_ref, dkv_refs = refs[:blocks], refs[blocks], refs[blocks + 1 :]
    width = heads * HD
    biases = [piece_bias(place_ref, counts_ref, m, pieces, slot_rows) for m in range(blocks)]
    for head in range(heads):
        low, high = head * HD, (head + 1) * HD
        query = q_ref[:, low:high] * SCALE
        d_out = jnp.concatenate([d_ref[:, low:high] for d_ref in d_refs])
        log_row = log_ref[head : head + 1, :]
        softs, d_softs, delta = [], [], 0.0
        for kv, bias in zip(kv_refs, biases):
            soft = jnp.exp(dot_nt(kv[:, low:high], query) + bias - log_row)
            d_soft = dot_nt(kv[:, width + low : width + high], d_out)
            delta = delta + jnp.sum(soft * d_soft, axis=0, keepdims=True)
            softs.append(soft)
            d_softs.append(d_soft)
        d_query = 0.0
        for kv, dkv, soft, d_soft in zip(kv_refs, dkv_refs, softs, d_softs):
            d_scores = (soft * (d_soft - delta)).astype(BF)
            d_query = d_query + dot_tn(d_scores, kv[:, low:high])
            dkv[:, low:high] = dot_nn(d_scores, query).astype(dkv.dtype)
            dkv[:, width + low : width + high] = dot_nn(soft.astype(BF), d_out).astype(dkv.dtype)
        dq_ref[:, low:high] = (d_query * SCALE).astype(BF)


def project_kernel(owners, seqs, place_ref, *refs):
    pieces, att_refs = refs[:owners], refs[owners : owners + seqs]
    tokens_ref, vec_ref, gain_ref, shift_ref, middle_ref, normed_ref, w_ref, sems = refs[owners + seqs :]
    own_rows, head_width = w_ref.shape[0] // owners, w_ref.shape[0] // seqs
    copies = fetches(pieces, place_ref[2], 0, own_rows, w_ref, sems)
    for copy in copies:
        copy.start()
    middle = tokens_ref[...] + row_of(vec_ref, 2)
    for copy in copies:
        copy.wait()
    for k, att_ref in enumerate(att_refs):
        first = pl.multiple_of((place_ref[1] ^ k) * head_width, 16)
        middle = middle + dot_nn(att_ref[...], w_ref[pl.ds(first, head_width), :])
    middle_ref[...] = middle
    unit = normalised(middle)[0]
    normed_ref[...] = (unit * row_of(gain_ref, 1) + row_of(shift_ref, 1)).astype(BF)


def hidden_kernel(owners, blocks, own_rows, hidden_rows, place_ref, *refs):
    pieces, refs = refs[:owners], refs[owners:]
    normed_refs, outcome_refs, refs = refs[:blocks], refs[blocks : 2 * blocks], refs[2 * blocks :]
    shift_ref, hidden_ref, d_up_ref, sums_ref = refs[:4]
    d_normed_refs, out_refs = refs[4 : 4 + blocks], refs[4 + blocks : 4 + 2 * blocks]
    up_ref, down_ref, sems = refs[4 + 2 * blocks :]
    parts, width = up_ref.shape[0], up_ref.shape[1]
    own = place_ref[2]
    waits = []
    for part in range(parts):
        waits += fetches(
            pieces, own, (1 + part) * own_rows, own_rows, up_ref.at[part], sems.at[part]
        )
    waits += fetches(pieces, own, (1 + parts) * own_rows, hidden_rows, down_ref, sems.at[parts])
    for copy in waits:
        copy.start()
    normed = jnp.concatenate([ref[...] for ref in normed_refs])
    outcome = jnp.concatenate([ref[...] for ref in outcome_refs])
    for copy in waits:
        copy.wait()
    size = min(384, parts * width)
    d_normed, result = 0.0, 0.0
    for first in range(0, parts * width, size):
        part, column = first // width, first % width
        up_weights = up_ref[part, :, column : column + size]
        down_weights = down_ref[first : first + size, :]
        up_proj = dot_nn(normed, up_weights) + shift_ref[:, first : first + size]
        chance = 0.5 * (1.0 + lax.erf(up_proj * (0.5**0.5)))
        hidden = (up_proj * chance).astype(BF)
        slope = chance + up_proj * (jnp.exp(-0.5 * up_proj * up_proj) * 0.3989422804014327)
        d_up = (dot_nt(outcome, down_weights) * slope).astype(BF)
        hidden_ref[:, first : first + size] = hidden
        d_up_ref[:, first : first + size] = d_up
        sums_ref[:, first : first + size] = jnp.sum(d_up.astype(F32), axis=0, keepdims=True)
        d_normed = d_normed + dot_nt(d_up, up_weights)
        result = result + dot_nn(hidden, down_weights)
    rows = normed_refs[0].shape[0]
    for m in range(blocks):
        d_normed_refs[m][...] = d_normed[m * rows : (m + 1) * rows].astype(d_normed_refs[m].dtype)
        out_refs[m][...] = result[m * rows : (m + 1) * rows].astype(out_refs[m].dtype)


def middle_kernel(owners, seqs, blocks, place_ref, counts_ref, *refs):
    pieces, refs = refs[:owners], refs[owners:]
    d_normed_refs, refs = refs[:blocks], refs[blocks:]
    middle_in_ref, grad_ref, gain_ref, d_middle_ref, d_branch_ref, sums_ref = refs[:6]
    head_refs, (w_ref, sems) = refs[6 : 6 + seqs], refs[6 + seqs :]
    own_rows, head_width = w_ref.shape[0] // owners, w_ref.shape[0] // seqs
    copies = fetches(pieces, place_ref[2], 0, own_rows, w_ref, sems)
    for copy in copies:
        copy.start()
    valid = own_rows_valid(place_ref, counts_ref, seqs, grad_ref.shape[0])
    grad_rows = jnp.where(valid, grad_ref[...], 0.0)
    unit, inverse = normalised(middle_in_ref[...])
    upstream = sum(ref[...].astype(F32) for ref in d_normed_refs)
    d_middle = grad_rows + norm_back(upstream, unit, inverse, row_of(gain_ref, 1))
    d_branch = d_middle.astype(BF)
    d_middle_ref[...] = d_middle
    d_branch_ref[...] = d_branch
    for copy in copies:
        copy.wait()
    for k, head_ref in enumerate(head_refs):
        first = pl.multiple_of((place_ref[1] ^ k) * head_width, 16)
        head_ref[...] = dot_nt(d_branch, w_ref[pl.ds(first, head_width), :]).astype(BF)
    rows = (
        upstream * unit,
        upstream,
        d_branch.astype(F32),
        grad_rows.astype(BF).astype(F32),
    )
    for index, one in enumerate(rows):
        sums_ref[index : index + 1, :] = jnp.sum(one, axis=0, keepdims=True)


def grads_kernel(owners, seqs, blocks, own_rows, hidden_rows, place_ref, *refs):
    normed_refs, outcome_refs, refs = refs[:blocks], refs[blocks : 2 * blocks], refs[2 * blocks :]
    hidden_ref, d_up_ref, sent_ref, kept_ref = refs
    width = outcome_refs[0].shape[1]
    parts = d_up_ref.shape[1] // width
    bit = place_ref[2] & 1
    normed = jnp.concatenate([ref[...] for ref in normed_refs])
    outcome = jnp.concatenate([ref[...] for ref in outcome_refs])
    chunk, up_chunk = hidden_rows // seqs, own_rows // seqs
    for owner in range(owners):
        down = dot_tn(hidden_ref[:, owner * hidden_rows : (owner + 1) * hidden_rows], outcome)
        rows_in = normed[:, owner * own_rows : (owner + 1) * own_rows]
        ups = [
            dot_tn(rows_in, d_up_ref[:, part * width : (part + 1) * width]) for part in range(parts)
        ]

        def store(ref, owner=owner, down=down, ups=ups):
            for k in range(seqs):
                ref[owner // 2, k, 0:chunk, :] = down[k * chunk : (k + 1) * chunk].astype(BF)
                for part, up in enumerate(ups):
                    first = chunk + part * up_chunk
                    ref[owner // 2, k, first : first + up_chunk, :] = up[
                        k * up_chunk : (k + 1) * up_chunk
                    ].astype(BF)

        @pl.when(bit == owner % 2)
        def keep():
            store(kept_ref)

        @pl.when(bit != owner % 2)
        def send():
            store(sent_ref)


def first_back_kernel(pieces, *refs):
    part_refs, (tokens_ref, d_middle_ref, gain_ref, out_ref) = refs[:pieces], refs[pieces:]
    upstream = sum(ref[...].astype(F32) for ref in part_refs)
    unit, inverse = normalised(tokens_ref[...])
    out_ref[...] = d_middle_ref[...] + norm_back(upstream, unit, inverse, row_of(gain_ref, 0))


def place_kernel(seqs, blocks, layouts, place_ref, *refs):
    pieces = refs[: blocks * seqs]
    outs = refs[blocks * seqs : -2]
    held, sems = refs[-2:]
    blk, seq = place_ref[0], place_ref[1]
    copies = [
        pltpu.make_async_copy(
            pieces[m * seqs + k],
            held.at[jnp.bitwise_xor(blk, m), jnp.bitwise_xor(seq, k)],
            sems.at[m * seqs + k],
        )
        for m in range(blocks)
        for k in range(seqs)
    ]
    for copy in copies:
        copy.start()
    for copy in copies:
        copy.wait()
    for out, spots in zip(outs, layouts):
        for b in range(blocks):
            for k in range(seqs):
                for top, rows, first, size, row, column in spots(b, k):
                    piece = held[b, k, top : top + rows, first : first + size]
                    out[row : row + rows, column : column + size] = piece.astype(F32)


def run(kernel, label, outs, scalars, remote, arrays, scratch=(), flops=0, powers=0):
    moved = sum(one.size * one.dtype.itemsize for one in (*remote, *arrays))
    moved += sum(one.size * one.dtype.itemsize for one in outs)
    return pl.pallas_call(
        kernel,
        out_shape=tuple(outs),
        in_specs=[pl.BlockSpec(memory_space=pltpu.SMEM)] * len(scalars)
        + [pl.BlockSpec(memory_space=pl.ANY)] * len(remote)
        + [pl.BlockSpec(memory_space=pltpu.VMEM)] * len(arrays),
        out_specs=(pl.BlockSpec(memory_space=pltpu.VMEM),) * len(outs),
        scratch_shapes=list(scratch),
        compiler_params=pltpu.CompilerParams(vmem_limit_bytes=VMEM_LIMIT),
        cost_estimate=pl.CostEstimate(flops=flops, bytes_accessed=moved, transcendentals=powers),
        name=label,
    )(*scalars, *remote, *arrays)


def shape(dims, kind):
    return jax.ShapeDtypeStruct(tuple(dims), kind)


def after(value, *others):
    return lax.optimization_barrier((value, others))[0]


def pick(pairs, axis, index):
    return sum(
        lax.dynamic_index_in_dim(one, index, axis, keepdims=False).astype(F32) for one in pairs
    )


def owner_sums(kept, arrived, own):
    terms, sent = (kept, arrived), None
    bit = 2
    while bit < lax.axis_size("fsdp"):
        terms = tuple(one.reshape(one.shape[0] // 2, 2, *one.shape[1:]) for one in terms)
        high = (own // bit) % 2
        sent = pick(terms, 1, 1 - high).astype(BF)
        terms = (pick(terms, 1, high), swap(sent, "fsdp", bit))
        bit *= 2
    return tuple(one[0] for one in terms), sent


def chunk_sums(terms, axis, index):
    total = pick(terms, 0, index)
    for j in range(1, lax.axis_size(axis)):
        total = total + swap(pick(terms, 0, index ^ j).astype(BF), axis, j).astype(F32)
    return total


def sum_parts(parts, axis):
    return [parts[0]] + [swap(parts[j], axis, j) for j in range(1, len(parts))]


def tree_sum(pieces):
    pieces = [piece.astype(F32) for piece in pieces]
    while len(pieces) > 1:
        pieces = [pieces[i] + pieces[i + 1] for i in range(0, len(pieces), 2)]
    return pieces[0]


def in_order(pieces, index):
    result = []
    for place in range(len(pieces)):
        chosen = pieces[place]
        for other in range(1, len(pieces)):
            chosen = jnp.where(index == other, pieces[place ^ other], chosen)
        result.append(chosen)
    return result


def padded(rows, count, width):
    return jnp.pad(rows, ((0, 0), (0, count - rows.shape[1]), (0, width - rows.shape[2])))


def shards(
    tokens, counts, norm_gain, norm_bias, vec_bias, up_bias, w_qkv, w_out, w_up, w_down, grad_out
):
    owners, blocks, seqs = (lax.axis_size(name) for name in ("fsdp", "blk", "seq"))
    own, blk, seq = (lax.axis_index(name) for name in ("fsdp", "blk", "seq"))
    place = jnp.stack([blk, seq, own]).astype(jnp.int32)
    rows, width = tokens.shape[1:]
    head_width = width // seqs
    own_rows = width // owners
    hidden_rows = w_down.shape[0] // blocks
    hidden_width = hidden_rows * owners
    parts = hidden_width // width
    inputs, grad_in = tokens[0], grad_out[0]
    vmem, dma = pltpu.VMEM, pltpu.SemaphoreType.DMA

    normed1, d_outcome = run(
        functools.partial(prepare_kernel, seqs),
        "prepare",
        [shape((rows, width), BF)] * 2,
        [place, counts],
        [],
        [inputs, grad_in, norm_gain, norm_bias],
    )
    normed1_pieces = from_all(normed1, "seq")
    qkv_late = after(w_qkv, normed1)
    qkv_mine = jnp.concatenate(
        [
            lax.dynamic_slice_in_dim(qkv_late, part * width + seq * head_width, head_width, axis=1)
            for part in range(3)
        ],
        axis=1,
    )
    qkv_pieces = doubled(qkv_mine, "fsdp")
    qkv_full = jnp.concatenate(in_order(qkv_pieces, own))

    up_late, down_late, out_late = after((w_up, w_down, w_out), qkv_mine)
    up_columns = [
        lax.dynamic_slice_in_dim(up_late, (i * blocks + blk) * hidden_rows, hidden_rows, axis=1)
        for i in range(owners)
    ]
    in_part = owners // parts
    weights_mine = jnp.concatenate(
        [out_late]
        + [
            jnp.concatenate(up_columns[part * in_part : (part + 1) * in_part], axis=1)
            for part in range(parts)
        ]
        + [lax.dynamic_slice_in_dim(down_late, blk * hidden_rows, hidden_rows, axis=0)]
    )
    weights = doubled(after(weights_mine, qkv_pieces[owners // 2]), "fsdp")
    outcome_pieces = from_all(after(d_outcome, weights_mine), "blk")
    gain_row, shift_row = norm_gain[0].astype(F32), norm_bias[0].astype(F32)
    biases = vec_bias.astype(F32)
    qkv_shift = jnp.concatenate(
        [
            lax.dynamic_slice_in_dim(biases[0], seq * head_width, head_width),
            jnp.zeros((head_width,), F32),
            lax.dynamic_slice_in_dim(biases[1], seq * head_width, head_width),
        ]
    )
    up_shift = (
        jnp.concatenate(
            [
                lax.dynamic_slice_in_dim(up_bias, (i * blocks + blk) * hidden_rows, hidden_rows)
                for i in range(owners)
            ]
        )
        .astype(F32)
        .reshape(1, hidden_width)
    )

    normed1_all = jnp.concatenate(normed1_pieces)
    key_value = (
        dot_nn(normed1_all, qkv_full[:, head_width:]) + qkv_shift[head_width:]
    ).astype(BF)
    kv_blocks = from_all(key_value, "blk")
    queries = (
        dot_nn(after(normed1_all, key_value), qkv_full[:, :head_width]) + qkv_shift[:head_width]
    ).astype(BF)
    block_rows, heads = seqs * rows, head_width // HD
    powers = block_rows * block_rows * blocks * heads
    *att_out, log_total = run(
        functools.partial(attend_kernel, blocks, heads, seqs, rows),
        "attend",
        [shape((rows, head_width), BF)] * seqs + [shape((heads, block_rows), F32)],
        [place, counts],
        [],
        [queries, *kv_blocks],
        flops=4 * HD * powers,
        powers=powers,
    )
    att_pieces = sum_parts(att_out, "seq")
    middle, normed2 = run(
        functools.partial(project_kernel, owners, seqs),
        "project",
        [shape((rows, width), F32), shape((rows, width), BF)],
        [place],
        weights,
        [*att_pieces, inputs, vec_bias, norm_gain, norm_bias],
        [vmem((width, width), BF), dma((owners,))],
        flops=2 * rows * width * width,
    )

    normed_pieces = from_all(normed2, "blk")
    all_rows = blocks * rows
    row_shapes = [shape((rows, width), F32)] + [shape((rows, width), BF)] * (blocks - 1)
    hidden, d_up, up_sums, *rest = run(
        functools.partial(hidden_kernel, owners, blocks, own_rows, hidden_rows),
        "hidden",
        [shape((all_rows, hidden_width), BF)] * 2
        + [shape((1, hidden_width), F32)]
        + row_shapes * 2,
        [place],
        weights,
        [*normed_pieces, *outcome_pieces, up_shift],
        [
            vmem((parts, width, width), BF),
            vmem((hidden_width, width), BF),
            dma((parts + 1, owners)),
        ],
        flops=8 * all_rows * width * hidden_width,
        powers=2 * all_rows * hidden_width,
    )
    d_normed_parts, result_parts = rest[:blocks], rest[blocks:]
    d_normed_pieces = sum_parts(d_normed_parts, "blk")
    chunk, up_chunk = hidden_rows // seqs, own_rows // seqs
    chunk_rows = chunk + parts * up_chunk
    sent, kept = run(
        functools.partial(grads_kernel, owners, seqs, blocks, own_rows, hidden_rows),
        "grads",
        [shape((owners // 2, seqs, chunk_rows, width), BF)] * 2,
        [place],
        [],
        [*normed_pieces, *outcome_pieces, hidden, d_up],
        flops=4 * all_rows * width * hidden_width,
    )
    arrived = swap(sent, "fsdp", 1)
    d_middle, d_branch, middle_sums, *d_heads = run(
        functools.partial(middle_kernel, owners, seqs, blocks),
        "middle",
        [shape((rows, width), F32), shape((rows, width), BF), shape((4, width), F32)]
        + [shape((rows, head_width), BF)] * seqs,
        [place, counts],
        weights,
        [*after(tuple(d_normed_pieces), sent), middle, grad_in, norm_gain],
        [vmem((width, width), BF), dma((owners,))],
        flops=2 * rows * width * width,
    )
    d_att_pieces = sum_parts(d_heads, "seq")
    own_terms, feed_sent = owner_sums(kept, arrived, own)

    att_late, branch_late = after((tuple(att_pieces), d_branch), *d_heads)
    token_att = jnp.concatenate(in_order(att_late, seq), axis=1)
    early = jnp.concatenate(
        [
            padded(
                middle_sums.reshape(4, owners, own_rows).transpose(1, 0, 2), 4, width
            ),
            padded(
                jnp.where(
                    (jnp.arange(blocks) == blk)[None, :, None],
                    up_sums.reshape(owners, 1, hidden_rows),
                    0.0,
                ).reshape(owners, 1, blocks * hidden_rows),
                12,
                width,
            ),
        ],
        axis=1,
    ).astype(BF)
    out_grads = jnp.concatenate(
        [dot_tn(token_att, branch_late).astype(BF).reshape(owners, own_rows, width), early], axis=1
    )
    out_sums = lax.psum(
        lax.psum_scatter(
            out_grads.reshape(owners * (own_rows + 16), width),
            "fsdp",
            scatter_dimension=0,
            tiled=True,
        ),
        ("blk", "seq"),
    ).astype(F32)

    d_query, d_kv, *d_kv_sent = run(
        functools.partial(attend_back_kernel, blocks, heads, seqs, rows),
        "attend_back",
        [shape((block_rows, head_width), BF), shape((block_rows, 2 * head_width), F32)]
        + [shape((block_rows, 2 * head_width), BF)] * (blocks - 1),
        [after(place, feed_sent), counts],
        [],
        [queries, log_total, *d_att_pieces, *kv_blocks],
        flops=10 * HD * powers,
        powers=powers,
    )
    for m in range(1, blocks):
        d_kv = d_kv + swap(d_kv_sent[m - 1], "blk", m).astype(F32)
    d_kv = after(d_kv.astype(BF), own_terms)
    d_projected = jnp.concatenate([d_query, d_kv], axis=1)
    d_normed1_all = dot_nt(d_projected, qkv_full).astype(BF)
    d_normed1_pieces = sum_parts(
        [d_normed1_all[k * rows : (k + 1) * rows] for k in range(seqs)], "seq"
    )
    feed_sums = chunk_sums(own_terms, "seq", seq).astype(BF)

    normed1_late, result_late = after((normed1_all, tuple(result_parts[1:])), d_normed1_all)
    qkv_grads = dot_tn(normed1_late, d_projected)
    column_sums = jnp.sum(d_projected.astype(F32), axis=0)
    unit_grads = (qkv_grads - shift_row[:, None] * column_sums[None, :]) / gain_row[:, None]
    qkv_float = qkv_full.astype(F32)
    is_seq = (jnp.arange(seqs) == seq)[:, None]
    late = jnp.stack(
        [
            jnp.sum(qkv_float * unit_grads, axis=1),
            jnp.sum(qkv_float * column_sums[None, :], axis=1),
            jnp.where(is_seq, column_sums[None, :head_width], 0.0).reshape(-1),
            jnp.where(is_seq, column_sums[None, 2 * head_width :], 0.0).reshape(-1),
        ]
    )
    late = padded(late.reshape(4, owners, own_rows).transpose(1, 0, 2), 16, 3 * head_width)
    qkv_grads = jnp.concatenate(
        [qkv_grads.astype(BF).reshape(owners, own_rows, 3 * head_width), late.astype(BF)], axis=1
    ).reshape(owners // 2, 2, own_rows + 16, 3 * head_width)
    qkv_arrived = swap(
        lax.dynamic_index_in_dim(qkv_grads, 1 - own % 2, 1, keepdims=False), "fsdp", 1
    )
    qkv_terms, _ = owner_sums(
        lax.dynamic_index_in_dim(qkv_grads, own % 2, 1, keepdims=False), qkv_arrived, own
    )
    qkv_own = sum(one.astype(F32) for one in qkv_terms)
    blk_rows = own_rows // blocks

    def qkv_part(index):
        return jnp.concatenate(
            [lax.dynamic_slice_in_dim(qkv_own, index * blk_rows, blk_rows), qkv_own[own_rows:]]
        )

    qkv_sums = tree_sum(
        [qkv_part(blk).astype(BF)]
        + [swap(qkv_part(blk ^ m).astype(BF), "blk", m) for m in range(1, blocks)]
    ).astype(BF)

    (grad_tokens,) = run(
        functools.partial(first_back_kernel, seqs),
        "first_back",
        [shape((rows, width), F32)],
        [],
        [],
        [*d_normed1_pieces, inputs, d_middle, norm_gain],
    )
    outcome = result_parts[0]
    for m in range(1, blocks):
        outcome = outcome + swap(result_late[m - 1], "blk", m).astype(F32)
    valid = lax.broadcasted_iota(jnp.int32, (rows, 1), 0) < counts[0, blk * seqs + seq]
    activations = jnp.where(valid, middle + outcome + biases[3], 0.0)

    feed_seq = from_all(feed_sums, "seq")
    feed_all = [from_all(one, "blk") for one in feed_seq]
    qkv_seq = from_all(qkv_sums, "seq")
    qkv_all = [from_all(one, "blk") for one in qkv_seq]
    held = pltpu.VMEM((blocks, seqs, chunk_rows, width), BF)
    grad_down, grad_up = run(
        functools.partial(
            place_kernel,
            seqs,
            blocks,
            [
                lambda b, k: [(0, chunk, 0, width, b * hidden_rows + k * chunk, 0)],
                lambda b, k: [
                    (
                        chunk + (i * hidden_rows // width) * up_chunk,
                        up_chunk,
                        i * hidden_rows % width,
                        hidden_rows,
                        k * up_chunk,
                        (i * blocks + b) * hidden_rows,
                    )
                    for i in range(owners)
                ],
            ],
        ),
        "place_feed",
        [shape((blocks * hidden_rows, width), F32), shape((own_rows, blocks * hidden_width), F32)],
        [after(place, qkv_seq)],
        [feed_all[k][m] for m in range(blocks) for k in range(seqs)],
        [],
        [held, dma((blocks * seqs,))],
    )
    (grad_qkv,) = run(
        functools.partial(
            place_kernel,
            seqs,
            blocks,
            [
                lambda b, k: [
                    (
                        0,
                        blk_rows,
                        i * head_width,
                        head_width,
                        b * blk_rows,
                        i * width + k * head_width,
                    )
                    for i in range(3)
                ]
            ],
        ),
        "place_qkv",
        [shape((own_rows, 3 * width), F32)],
        [place],
        [qkv_all[k][m] for m in range(blocks) for k in range(seqs)],
        [],
        [
            pltpu.VMEM((blocks, seqs, blk_rows + 16, 3 * head_width), BF),
            dma((blocks * seqs,)),
        ],
    )
    late_sums = tree_sum([one[blk_rows : blk_rows + 4, :own_rows] for one in qkv_seq])
    early_sums = out_sums[own_rows : own_rows + 4, :own_rows]
    return (
        activations[None],
        grad_tokens[None],
        jnp.stack([late_sums[0], early_sums[0]]),
        jnp.stack([late_sums[1], early_sums[1]]),
        jnp.stack([late_sums[2], late_sums[3], early_sums[2], early_sums[3]]),
        out_sums[own_rows + 4, : blocks * hidden_rows],
        grad_qkv,
        out_sums[:own_rows],
        grad_up,
        grad_down,
    )


def solution(mesh):
    rows = P("fsdp", ("blk", "seq"), None)
    split = P("fsdp", None)
    return jax.shard_map(
        shards,
        mesh=mesh,
        in_specs=(rows, split, P(), P(), P(), P(), split, split, split, split, rows),
        out_specs=(
            rows,
            rows,
            P(None, "fsdp"),
            P(None, "fsdp"),
            P(None, "fsdp"),
            P("fsdp"),
            split,
            split,
            split,
            split,
        ),
        check_vma=False,
    )
```

```python
import functools

import jax
import jax.numpy as jnp
from jax import lax
from jax.experimental import pallas as pl
from jax.experimental.pallas import tpu as pltpu
from jax.sharding import PartitionSpec as P

HD = 64
EPSILON = 1e-06
MASKED = -1e30
SCALE = HD ** (-0.5)
BF = jnp.bfloat16
F32 = jnp.float32
VMEM_LIMIT = 44 * 1024 * 1024


def dot_nn(left_side, right_side):
    return lax.dot_general(
        left_side, right_side, (((1,), (0,)), ((), ())), preferred_element_type=F32
    )


def dot_nt(left_side, right_side):
    return lax.dot_general(
        left_side, right_side, (((1,), (1,)), ((), ())), preferred_element_type=F32
    )


def dot_tn(left_side, right_side):
    return lax.dot_general(
        left_side, right_side, (((0,), (0,)), ((), ())), preferred_element_type=F32
    )


def swap(array, axis, bits):
    return lax.ppermute(array, axis, [(i, i ^ bits) for i in range(lax.axis_size(axis))])


def from_all(array, axis):
    return [array] + [swap(array, axis, j) for j in range(1, lax.axis_size(axis))]


def doubled(array, axis):
    pieces = {0: array}
    bit = lax.axis_size(axis) // 2
    while bit:
        pieces.update({j | bit: swap(piece, axis, bit) for j, piece in list(pieces.items())})
        bit //= 2
    return [pieces[j] for j in range(lax.axis_size(axis))]


def piece_bias(place_ref, counts_ref, block, pieces, slot_rows):
    row = lax.broadcasted_iota(jnp.int32, (pieces * slot_rows, 1), 0)
    limit = jnp.zeros_like(row)
    for piece in range(pieces):
        held = (place_ref[0] ^ block) * pieces + (place_ref[1] ^ piece)
        end = counts_ref[0, held] + piece * slot_rows
        limit = jnp.where(row >= piece * slot_rows, end, limit)
    return jnp.where(row < limit, 0.0, MASKED)


def own_rows_valid(place_ref, counts_ref, seqs, rows):
    count = counts_ref[0, place_ref[0] * seqs + place_ref[1]]
    return lax.broadcasted_iota(jnp.int32, (rows, 1), 0) < count


def normalised(matrix_rows):
    centre = matrix_rows - jnp.mean(matrix_rows, axis=-1, keepdims=True)
    inverse = lax.rsqrt(jnp.mean(centre * centre, axis=-1, keepdims=True) + EPSILON)
    return centre * inverse, inverse


def norm_back(upstream, unit_rows, inverse, gain_row):
    scaled = upstream * gain_row
    return inverse * (
        scaled
        - jnp.mean(scaled, axis=-1, keepdims=True)
        - unit_rows * jnp.mean(scaled * unit_rows, axis=-1, keepdims=True)
    )


def row_of(ref, index):
    return ref[...].astype(F32)[index : index + 1]


def fetches(pieces, own, first, size, target, sems):
    return [
        pltpu.make_async_copy(
            piece.at[pl.ds(first, size)],
            target.at[pl.ds(pl.multiple_of((own ^ j) * size, 16), size)],
            sems.at[j],
        )
        for j, piece in enumerate(pieces)
    ]


def prepare_kernel(
    seqs,
    place_ref,
    counts_ref,
    tokens_ref,
    grad_ref,
    gain_ref,
    shift_ref,
    qkv_ref,
    normed_ref,
    outcome_ref,
    mine_ref,
):
    width = tokens_ref.shape[1]
    size = width // seqs
    for part in range(3):
        chosen = qkv_ref[:, part * width : part * width + size]
        for k in range(1, seqs):
            first = part * width + k * size
            chosen = jnp.where(place_ref[1] == k, qkv_ref[:, first : first + size], chosen)
        mine_ref[:, part * size : (part + 1) * size] = chosen
    unit = normalised(tokens_ref[...])[0]
    normed_ref[...] = (unit * row_of(gain_ref, 0) + row_of(shift_ref, 0)).astype(BF)
    valid = own_rows_valid(place_ref, counts_ref, seqs, grad_ref.shape[0])
    outcome_ref[...] = jnp.where(valid, grad_ref[...], 0.0).astype(BF)


def pack_kernel(owners, blocks, parts, place_ref, up_ref, down_ref, out_ref, sems):
    rows, width = up_ref.shape[0], down_ref.shape[1]
    size = down_ref.shape[0] // blocks
    copies = []
    for i in range(owners):
        first = pl.multiple_of((i * blocks + place_ref[0]) * size, 128)
        part, column = divmod(i * size, width)
        copies.append((up_ref.at[:, pl.ds(first, size)],
                       out_ref.at[pl.ds(part * rows, rows), pl.ds(column, size)]))
    first = pl.multiple_of(place_ref[0] * size, 16)
    copies.append((down_ref.at[pl.ds(first, size)], out_ref.at[pl.ds(parts * rows, size)]))
    copies = [
        pltpu.make_async_copy(source, target, sems.at[i])
        for i, (source, target) in enumerate(copies)
    ]
    for copy in copies:
        copy.start()
    for copy in copies:
        copy.wait()


def qkv_kernel(owners, seqs, place_ref, *refs):
    pieces, normed_refs, refs = refs[:owners], refs[owners : owners + seqs], refs[owners + seqs :]
    shift_ref, kv_ref, q_ref, w_ref, sems = refs
    own_rows, size = pieces[0].shape[0], q_ref.shape[1]
    copies = fetches(pieces, place_ref[2], 0, own_rows, w_ref, sems)
    for copy in copies:
        copy.start()
    normed = jnp.concatenate([ref[...] for ref in normed_refs])
    for copy in copies:
        copy.wait()
    result = (dot_nn(normed, w_ref[...]) + shift_ref[...]).astype(BF)
    q_ref[...] = result[:, :size]
    kv_ref[...] = result[:, size:]


def attend_kernel(blocks, heads, pieces, slot_rows, place_ref, counts_ref, q_ref, *refs):
    kv_refs, out_refs, log_ref = refs[:blocks], refs[blocks:-1], refs[-1]
    width = heads * HD
    biases = [piece_bias(place_ref, counts_ref, m, pieces, slot_rows) for m in range(blocks)]
    for head in range(heads):
        low, high = head * HD, (head + 1) * HD
        query = q_ref[:, low:high] * SCALE
        scores = [dot_nt(kv[:, low:high], query) + bias for kv, bias in zip(kv_refs, biases)]
        top = functools.reduce(
            jnp.maximum, [jnp.max(block, axis=0, keepdims=True) for block in scores]
        )
        powers = [jnp.exp(block - top) for block in scores]
        total = sum(jnp.sum(block, axis=0, keepdims=True) for block in powers)
        inverse = 1.0 / total
        result = sum(
            dot_tn((block * inverse).astype(BF), kv[:, width + low : width + high])
            for block, kv in zip(powers, kv_refs)
        ).astype(BF)
        for k, out_ref in enumerate(out_refs):
            out_ref[:, low:high] = result[k * slot_rows : (k + 1) * slot_rows]
        log_ref[head : head + 1, :] = top + jnp.log(total)


def attend_back_kernel(blocks, heads, pieces, slot_rows, place_ref, counts_ref, q_ref, log_ref, *refs):
    d_refs, refs = refs[:pieces], refs[pieces:]
    kv_refs, dq_ref, dkv_refs = refs[:blocks], refs[blocks], refs[blocks + 1 :]
    width = heads * HD
    biases = [piece_bias(place_ref, counts_ref, m, pieces, slot_rows) for m in range(blocks)]
    for head in range(heads):
        low, high = head * HD, (head + 1) * HD
        query = q_ref[:, low:high] * SCALE
        d_out = jnp.concatenate([d_ref[:, low:high] for d_ref in d_refs])
        log_row = log_ref[head : head + 1, :]
        softs, d_softs, delta = [], [], 0.0
        for kv, bias in zip(kv_refs, biases):
            soft = jnp.exp(dot_nt(kv[:, low:high], query) + bias - log_row)
            d_soft = dot_nt(kv[:, width + low : width + high], d_out)
            delta = delta + jnp.sum(soft * d_soft, axis=0, keepdims=True)
            softs.append(soft)
            d_softs.append(d_soft)
        d_query = 0.0
        for kv, dkv, soft, d_soft in zip(kv_refs, dkv_refs, softs, d_softs):
            d_scores = (soft * (d_soft - delta)).astype(BF)
            d_query = d_query + dot_tn(d_scores, kv[:, low:high])
            dkv[:, low:high] = dot_nn(d_scores, query).astype(dkv.dtype)
            dkv[:, width + low : width + high] = dot_nn(soft.astype(BF), d_out).astype(dkv.dtype)
        dq_ref[:, low:high] = (d_query * SCALE).astype(BF)


def project_kernel(owners, seqs, place_ref, *refs):
    pieces, att_refs = refs[:owners], refs[owners : owners + seqs]
    tokens_ref, vec_ref, gain_ref, shift_ref, middle_ref, normed_ref, w_ref, sems = refs[owners + seqs :]
    own_rows, head_width = w_ref.shape[0] // owners, w_ref.shape[0] // seqs
    copies = fetches(pieces, place_ref[2], 0, own_rows, w_ref, sems)
    for copy in copies:
        copy.start()
    middle = tokens_ref[...] + row_of(vec_ref, 2)
    for copy in copies:
        copy.wait()
    for k, att_ref in enumerate(att_refs):
        first = pl.multiple_of((place_ref[1] ^ k) * head_width, 16)
        middle = middle + dot_nn(att_ref[...], w_ref[pl.ds(first, head_width), :])
    middle_ref[...] = middle
    unit = normalised(middle)[0]
    normed_ref[...] = (unit * row_of(gain_ref, 1) + row_of(shift_ref, 1)).astype(BF)


def hidden_kernel(owners, blocks, own_rows, hidden_rows, place_ref, *refs):
    pieces, refs = refs[:owners], refs[owners:]
    normed_refs, outcome_refs, refs = refs[:blocks], refs[blocks : 2 * blocks], refs[2 * blocks :]
    shift_ref, hidden_ref, d_up_ref, sums_ref = refs[:4]
    d_normed_refs, out_refs = refs[4 : 4 + blocks], refs[4 + blocks : 4 + 2 * blocks]
    up_ref, down_ref, sems = refs[4 + 2 * blocks :]
    parts, width = up_ref.shape[0], up_ref.shape[1]
    own = place_ref[2]
    waits = []
    for part in range(parts):
        waits += fetches(
            pieces, own, part * own_rows, own_rows, up_ref.at[part], sems.at[part]
        )
    waits += fetches(pieces, own, parts * own_rows, hidden_rows, down_ref, sems.at[parts])
    for copy in waits:
        copy.start()
    normed = jnp.concatenate([ref[...] for ref in normed_refs])
    outcome = jnp.concatenate([ref[...] for ref in outcome_refs])
    for copy in waits:
        copy.wait()
    size = min(384, parts * width)
    d_normed, result = 0.0, 0.0
    for first in range(0, parts * width, size):
        part, column = first // width, first % width
        up_weights = up_ref[part, :, column : column + size]
        down_weights = down_ref[first : first + size, :]
        up_proj = dot_nn(normed, up_weights) + shift_ref[:, first : first + size]
        chance = 0.5 * (1.0 + lax.erf(up_proj * (0.5**0.5)))
        hidden = (up_proj * chance).astype(BF)
        slope = chance + up_proj * (jnp.exp(-0.5 * up_proj * up_proj) * 0.3989422804014327)
        d_up = (dot_nt(outcome, down_weights) * slope).astype(BF)
        hidden_ref[:, first : first + size] = hidden
        d_up_ref[:, first : first + size] = d_up
        sums_ref[:, first : first + size] = jnp.sum(d_up.astype(F32), axis=0, keepdims=True)
        d_normed = d_normed + dot_nt(d_up, up_weights)
        result = result + dot_nn(hidden, down_weights)
    rows = normed_refs[0].shape[0]
    for m in range(blocks):
        d_normed_refs[m][...] = d_normed[m * rows : (m + 1) * rows].astype(d_normed_refs[m].dtype)
        out_refs[m][...] = result[m * rows : (m + 1) * rows].astype(out_refs[m].dtype)


def middle_kernel(owners, seqs, blocks, place_ref, counts_ref, *refs):
    pieces, refs = refs[:owners], refs[owners:]
    d_normed_refs, refs = refs[:blocks], refs[blocks:]
    middle_in_ref, grad_ref, gain_ref, d_middle_ref, d_branch_ref, sums_ref = refs[:6]
    head_refs, (w_ref, sems) = refs[6 : 6 + seqs], refs[6 + seqs :]
    own_rows, head_width = w_ref.shape[0] // owners, w_ref.shape[0] // seqs
    copies = fetches(pieces, place_ref[2], 0, own_rows, w_ref, sems)
    for copy in copies:
        copy.start()
    valid = own_rows_valid(place_ref, counts_ref, seqs, grad_ref.shape[0])
    grad_rows = jnp.where(valid, grad_ref[...], 0.0)
    unit, inverse = normalised(middle_in_ref[...])
    upstream = sum(ref[...].astype(F32) for ref in d_normed_refs)
    d_middle = grad_rows + norm_back(upstream, unit, inverse, row_of(gain_ref, 1))
    d_branch = d_middle.astype(BF)
    d_middle_ref[...] = d_middle
    d_branch_ref[...] = d_branch
    for copy in copies:
        copy.wait()
    for k, head_ref in enumerate(head_refs):
        first = pl.multiple_of((place_ref[1] ^ k) * head_width, 16)
        head_ref[...] = dot_nt(d_branch, w_ref[pl.ds(first, head_width), :]).astype(BF)
    rows = (
        upstream * unit,
        upstream,
        d_branch.astype(F32),
        grad_rows.astype(BF).astype(F32),
    )
    for index, one in enumerate(rows):
        sums_ref[index : index + 1, :] = jnp.sum(one, axis=0, keepdims=True)


def grads_kernel(owners, seqs, blocks, own_rows, hidden_rows, place_ref, *refs):
    normed_refs, outcome_refs, refs = refs[:blocks], refs[blocks : 2 * blocks], refs[2 * blocks :]
    hidden_ref, d_up_ref, sent_ref, kept_ref = refs
    width = outcome_refs[0].shape[1]
    parts = d_up_ref.shape[1] // width
    bit = place_ref[2] & 1
    normed = jnp.concatenate([ref[...] for ref in normed_refs])
    outcome = jnp.concatenate([ref[...] for ref in outcome_refs])
    chunk, up_chunk = hidden_rows // seqs, own_rows // seqs
    for owner in range(owners):
        down = dot_tn(hidden_ref[:, owner * hidden_rows : (owner + 1) * hidden_rows], outcome)
        rows_in = normed[:, owner * own_rows : (owner + 1) * own_rows]
        ups = [
            dot_tn(rows_in, d_up_ref[:, part * width : (part + 1) * width]) for part in range(parts)
        ]

        def store(ref, owner=owner, down=down, ups=ups):
            for k in range(seqs):
                ref[owner // 2, k, 0:chunk, :] = down[k * chunk : (k + 1) * chunk].astype(BF)
                for part, up in enumerate(ups):
                    first = chunk + part * up_chunk
                    ref[owner // 2, k, first : first + up_chunk, :] = up[
                        k * up_chunk : (k + 1) * up_chunk
                    ].astype(BF)

        @pl.when(bit == owner % 2)
        def keep():
            store(kept_ref)

        @pl.when(bit != owner % 2)
        def send():
            store(sent_ref)


def step_kernel(bit, place_ref, kept_ref, arrived_ref, sent_ref, next_ref):
    high = (place_ref[2] // bit) & 1
    for i in range(sent_ref.shape[0]):
        for ref, index in ((sent_ref, 2 * i + 1 - high), (next_ref, 2 * i + high)):
            ref[i] = (kept_ref[index].astype(F32) + arrived_ref[index].astype(F32)).astype(BF)


def chunk_kernel(seqs, place_ref, kept_ref, arrived_ref, *out_refs):
    for j in range(seqs):
        index = place_ref[1] ^ j
        total = kept_ref[0, index].astype(F32) + arrived_ref[0, index].astype(F32)
        out_refs[j][...] = total.astype(BF)


def add_kernel(*refs):
    refs[-1][...] = sum(ref[...].astype(F32) for ref in refs[:-1]).astype(BF)


def project_back_kernel(blocks, seqs, *refs):
    q_ref, kv_refs, w_ref, refs = refs[0], refs[1 : 1 + blocks], refs[1 + blocks], refs[2 + blocks :]
    normed_refs, (gain_ref, shift_ref), refs = refs[:seqs], refs[seqs : seqs + 2], refs[seqs + 2 :]
    projected_ref, columns_ref, sums_ref, part_refs = refs[0], refs[1], refs[2], refs[3:]
    d_kv = sum(ref[...].astype(F32) for ref in kv_refs).astype(BF)
    d_projected = jnp.concatenate([q_ref[...], d_kv], axis=1)
    projected_ref[...] = d_projected
    columns_ref[...] = jnp.sum(d_projected.astype(F32), axis=0, keepdims=True)
    rows = normed_refs[0].shape[0]
    gain, shift = row_of(gain_ref, 0), row_of(shift_ref, 0)
    with_normed, plain = 0.0, 0.0
    for k in range(seqs):
        part = dot_nt(d_projected[k * rows : (k + 1) * rows], w_ref[...])
        part_refs[k][...] = part.astype(BF)
        with_normed = with_normed + jnp.sum(
            part * (normed_refs[k][...].astype(F32) - shift), axis=0, keepdims=True
        )
        plain = plain + jnp.sum(part, axis=0, keepdims=True)
    sums_ref[0:1, :] = with_normed / gain
    sums_ref[1:2, :] = plain


def last_grads_kernel(owners, seqs, blocks, place_ref, *refs):
    normed_refs, att_refs, refs = refs[:seqs], refs[seqs : 2 * seqs], refs[2 * seqs :]
    (projected_ref, branch_ref, columns_ref, first_ref, middle_ref, up_ref) = refs[:6]
    sent_ref, kept_ref, att_ref = refs[6:]
    width, size = branch_ref.shape[1], att_refs[0].shape[1]
    own_rows, hidden_rows = width // owners, up_ref.shape[1] // owners
    third = 3 * size
    bit = place_ref[2] & 1
    for k in range(seqs):
        att_ref[place_ref[1] ^ k] = att_refs[k][...]
    normed = jnp.concatenate([ref[...] for ref in normed_refs])
    projected, branch = projected_ref[...], branch_ref[...]
    for owner in range(owners):
        first = owner * own_rows
        group, column = divmod(first, size)
        qkv = dot_tn(normed[:, first : first + own_rows], projected).astype(BF)
        out = dot_tn(att_ref[group][:, column : column + own_rows], branch).astype(BF)
        is_group = place_ref[1] == group
        bias = [
            jnp.where(is_group, columns_ref[:, start : start + own_rows], 0.0)
            for start in (column, 2 * size + column)
        ]
        lines = [
            first_ref[0:1, first : first + own_rows],
            first_ref[1:2, first : first + own_rows],
            *bias,
        ] + [middle_ref[i : i + 1, first : first + own_rows] for i in range(4)]
        lines = jnp.concatenate(lines).astype(BF)
        up_line = up_ref[:, owner * hidden_rows : (owner + 1) * hidden_rows]
        up_line = jnp.concatenate(
            [jnp.where(place_ref[0] == b, up_line, 0.0) for b in range(blocks)], axis=1
        ).astype(BF)

        def store(ref, owner=owner, qkv=qkv, out=out, lines=lines, up_line=up_line):
            ref[owner // 2, 0:own_rows, 0:third] = qkv
            ref[owner // 2, 0:own_rows, third:] = out
            ref[owner // 2, own_rows:, :] = jnp.zeros((16, third + width), BF)
            ref[owner // 2, own_rows : own_rows + 8, 0:own_rows] = lines
            ref[owner // 2, own_rows + 8 : own_rows + 9, 0 : up_line.shape[1]] = up_line

        @pl.when(bit == owner % 2)
        def keep():
            store(kept_ref)

        @pl.when(bit != owner % 2)
        def send():
            store(sent_ref)


def block_kernel(blocks, place_ref, kept_ref, arrived_ref, *out_refs):
    total = kept_ref[0].astype(F32) + arrived_ref[0].astype(F32)
    own_rows = total.shape[0] - 16
    size = own_rows // blocks
    for m in range(blocks):
        chosen = total[:size]
        for j in range(1, blocks):
            chosen = jnp.where(place_ref[0] ^ m == j, total[j * size : (j + 1) * size], chosen)
        out_refs[m][0:size, :] = chosen.astype(BF)
        out_refs[m][size:, :] = total[own_rows:].astype(BF)


def seq_kernel(blocks, seqs, place_ref, *refs):
    in_refs, main_ref, out_refs = refs[:blocks], refs[blocks], refs[blocks + 1 :]
    terms = [ref[...].astype(F32) for ref in in_refs]
    while len(terms) > 1:
        terms = [terms[i] + terms[i + 1] for i in range(0, len(terms), 2)]
    total = terms[0]
    size = total.shape[0] - 16
    width = main_ref.shape[1]
    head = width // seqs
    third = 3 * head
    main_ref[...] = total[:, :width].astype(BF)
    for j in range(seqs):
        chosen = total[:size, third : third + head]
        for k in range(1, seqs):
            first = third + k * head
            chosen = jnp.where(place_ref[1] ^ j == k, total[:size, first : first + head], chosen)
        out_refs[j][...] = chosen.astype(BF)


def join_kernel(seqs, main_ref, *refs):
    out_ref = refs[seqs]
    size, head = refs[0].shape
    out_ref[...] = main_ref[...]
    total = sum(ref[...].astype(F32) for ref in refs[:seqs])
    out_ref[0:size, 3 * head :] = total.astype(BF)


def first_back_kernel(pieces, *refs):
    part_refs, (tokens_ref, d_middle_ref, gain_ref, out_ref) = refs[:pieces], refs[pieces:]
    upstream = sum(ref[...].astype(F32) for ref in part_refs)
    unit, inverse = normalised(tokens_ref[...])
    out_ref[...] = d_middle_ref[...] + norm_back(upstream, unit, inverse, row_of(gain_ref, 0))


def place_kernel(seqs, blocks, layouts, place_ref, *refs):
    pieces = refs[: blocks * seqs]
    outs = refs[blocks * seqs : -2]
    held, sems = refs[-2:]
    blk, seq = place_ref[0], place_ref[1]
    copies = [
        pltpu.make_async_copy(
            pieces[m * seqs + k],
            held.at[jnp.bitwise_xor(blk, m), jnp.bitwise_xor(seq, k)],
            sems.at[m * seqs + k],
        )
        for m in range(blocks)
        for k in range(seqs)
    ]
    for copy in copies:
        copy.start()
    for copy in copies:
        copy.wait()
    for out, spots in zip(outs, layouts):
        for b in range(blocks):
            for k in range(seqs):
                for top, rows, first, size, row, column in spots(b, k):
                    piece = held[b, k, top : top + rows, first : first + size]
                    out[row : row + rows, column : column + size] = piece.astype(F32)


def run(kernel, label, outs, scalars, remote, arrays, scratch=(), waits=(), in_hbm=False):
    inputs = len(scalars) + len(remote) + len(arrays)

    def without_waits(*refs):
        kernel(*refs[:inputs], *refs[inputs + len(waits) :])

    return pl.pallas_call(
        without_waits,
        out_shape=tuple(outs),
        in_specs=[pl.BlockSpec(memory_space=pltpu.SMEM)] * len(scalars)
        + [pl.BlockSpec(memory_space=pltpu.HBM)] * len(remote)
        + [pl.BlockSpec(memory_space=pltpu.VMEM)] * len(arrays)
        + [pl.BlockSpec(memory_space=pltpu.HBM)] * len(waits),
        out_specs=(pl.BlockSpec(memory_space=pltpu.HBM if in_hbm else pltpu.VMEM),) * len(outs),
        scratch_shapes=list(scratch),
        compiler_params=pltpu.CompilerParams(vmem_limit_bytes=VMEM_LIMIT),
        cost_estimate=pl.CostEstimate(flops=1, bytes_accessed=1, transcendentals=0),
        name=label,
    )(*scalars, *remote, *arrays, *waits)


def shape(dims, kind):
    return jax.ShapeDtypeStruct(tuple(dims), kind)


def owner_sums(kept, arrived, place, label):
    sent, bit = None, 2
    while bit < lax.axis_size("fsdp"):
        half = (kept.shape[0] // 2, *kept.shape[1:])
        sent, kept = run(
            functools.partial(step_kernel, bit),
            label,
            [shape(half, BF)] * 2,
            [place],
            [],
            [kept, arrived],
        )
        arrived = swap(sent, "fsdp", bit)
        bit *= 2
    return kept, arrived, sent


def sum_parts(parts, axis):
    return [parts[0]] + [swap(parts[j], axis, j) for j in range(1, len(parts))]


def tree_sum(pieces):
    pieces = [piece.astype(F32) for piece in pieces]
    while len(pieces) > 1:
        pieces = [pieces[i] + pieces[i + 1] for i in range(0, len(pieces), 2)]
    return pieces[0]


def shards(
    tokens, counts, norm_gain, norm_bias, vec_bias, up_bias, w_qkv, w_out, w_up, w_down, grad_out
):
    owners, blocks, seqs = (lax.axis_size(name) for name in ("fsdp", "blk", "seq"))
    own, blk, seq = (lax.axis_index(name) for name in ("fsdp", "blk", "seq"))
    place = jnp.stack([blk, seq, own]).astype(jnp.int32)
    rows, width = tokens.shape[1:]
    head_width = width // seqs
    heads, third = head_width // HD, 3 * head_width
    own_rows = width // owners
    hidden_rows = w_down.shape[0] // blocks
    hidden_width = hidden_rows * owners
    parts = hidden_width // width
    block_rows, all_rows = seqs * rows, blocks * rows
    inputs, grad_in = tokens[0], grad_out[0]
    vmem, dma = pltpu.VMEM, pltpu.SemaphoreType.DMA

    normed1, d_outcome, qkv_mine = run(
        functools.partial(prepare_kernel, seqs),
        "prepare",
        [shape((rows, width), BF)] * 2 + [shape((own_rows, third), BF)],
        [place, counts],
        [],
        [inputs, grad_in, norm_gain, norm_bias, w_qkv],
    )
    normed1_pieces = from_all(normed1, "seq")
    qkv_pieces = doubled(qkv_mine, "fsdp")
    out_pieces = doubled(w_out, "fsdp")
    outcome_pieces = from_all(d_outcome, "blk")

    packed = shape((parts * own_rows + hidden_rows, width), BF)
    if hidden_rows % 128 == 0:
        (weights_mine,) = run(
            functools.partial(pack_kernel, owners, blocks, parts),
            "pack",
            [packed],
            [place],
            [w_up, w_down],
            [],
            [dma((owners + 1,))],
            waits=[qkv_pieces[owners // 2], out_pieces[owners // 2]],
            in_hbm=True,
        )
    else:
        columns = [
            lax.dynamic_slice_in_dim(w_up, (i * blocks + blk) * hidden_rows, hidden_rows, axis=1)
            for i in range(owners)
        ]
        in_part = owners // parts
        weights_mine = jnp.concatenate(
            [
                jnp.concatenate(columns[part * in_part : (part + 1) * in_part], axis=1)
                for part in range(parts)
            ]
            + [lax.dynamic_slice_in_dim(w_down, blk * hidden_rows, hidden_rows, axis=0)]
        )
    weights = doubled(weights_mine, "fsdp")
    biases = vec_bias.astype(F32)
    qkv_shift = jnp.concatenate(
        [
            lax.dynamic_slice_in_dim(biases[0], seq * head_width, head_width),
            jnp.zeros((head_width,), F32),
            lax.dynamic_slice_in_dim(biases[1], seq * head_width, head_width),
        ]
    ).reshape(1, third)
    up_shift = (
        lax.dynamic_index_in_dim(up_bias.reshape(owners, blocks, hidden_rows), blk, 1, False)
        .astype(F32)
        .reshape(1, hidden_width)
    )

    key_value, queries, qkv_full = run(
        functools.partial(qkv_kernel, owners, seqs),
        "project_in",
        [
            shape((block_rows, 2 * head_width), BF),
            shape((block_rows, head_width), BF),
            shape((width, third), BF),
        ],
        [place],
        qkv_pieces,
        [*normed1_pieces, qkv_shift],
        [dma((owners,))],
    )
    kv_blocks = from_all(key_value, "blk")
    *att_out, log_total = run(
        functools.partial(attend_kernel, blocks, heads, seqs, rows),
        "attend",
        [shape((rows, head_width), BF)] * seqs + [shape((heads, block_rows), F32)],
        [place, counts],
        [],
        [queries, *kv_blocks],
    )
    att_pieces = sum_parts(att_out, "seq")
    middle, normed2 = run(
        functools.partial(project_kernel, owners, seqs),
        "project_out",
        [shape((rows, width), F32), shape((rows, width), BF)],
        [place],
        out_pieces,
        [*att_pieces, inputs, vec_bias, norm_gain, norm_bias],
        [vmem((width, width), BF), dma((owners,))],
    )

    normed_pieces = from_all(normed2, "blk")
    row_shapes = [shape((rows, width), F32)] + [shape((rows, width), BF)] * (blocks - 1)
    hidden, d_up, up_sums, *rest = run(
        functools.partial(hidden_kernel, owners, blocks, own_rows, hidden_rows),
        "hidden",
        [shape((all_rows, hidden_width), BF)] * 2
        + [shape((1, hidden_width), F32)]
        + row_shapes * 2,
        [place],
        weights,
        [*normed_pieces, *outcome_pieces, up_shift],
        [
            vmem((parts, width, width), BF),
            vmem((hidden_width, width), BF),
            dma((parts + 1, owners)),
        ],
    )
    d_normed_pieces = sum_parts(rest[:blocks], "blk")
    chunk, up_chunk = hidden_rows // seqs, own_rows // seqs
    chunk_rows = chunk + parts * up_chunk
    sent, kept = run(
        functools.partial(grads_kernel, owners, seqs, blocks, own_rows, hidden_rows),
        "feed_grads",
        [shape((owners // 2, seqs, chunk_rows, width), BF)] * 2,
        [place],
        [],
        [*normed_pieces, *outcome_pieces, hidden, d_up],
    )
    d_middle, d_branch, middle_sums, *d_heads = run(
        functools.partial(middle_kernel, owners, seqs, blocks),
        "middle",
        [shape((rows, width), F32), shape((rows, width), BF), shape((4, width), F32)]
        + [shape((rows, head_width), BF)] * seqs,
        [place, counts],
        out_pieces,
        [*d_normed_pieces, middle, grad_in, norm_gain],
        [vmem((width, width), BF), dma((owners,))],
        waits=[sent],
    )
    d_att_pieces = sum_parts(d_heads, "seq")
    kept, arrived, sent = owner_sums(kept, swap(sent, "fsdp", 1), place, "feed_step")

    d_query, *d_kv = run(
        functools.partial(attend_back_kernel, blocks, heads, seqs, rows),
        "attend_back",
        [shape((block_rows, head_width), BF), shape((block_rows, 2 * head_width), F32)]
        + [shape((block_rows, 2 * head_width), BF)] * (blocks - 1),
        [place, counts],
        [],
        [queries, log_total, *d_att_pieces, *kv_blocks],
        waits=[sent],
    )
    d_projected, column_sums, first_sums, *d_normed1 = run(
        functools.partial(project_back_kernel, blocks, seqs),
        "project_back",
        [
            shape((block_rows, third), BF),
            shape((1, third), F32),
            shape((2, width), F32),
        ]
        + [shape((rows, width), BF)] * seqs,
        [],
        [],
        [d_query, *sum_parts(d_kv, "blk"), qkv_full, *normed1_pieces, norm_gain, norm_bias],
    )
    d_normed1_pieces = sum_parts(d_normed1, "seq")
    feed_chunks = run(
        functools.partial(chunk_kernel, seqs),
        "feed_chunks",
        [shape((chunk_rows, width), BF)] * seqs,
        [place],
        [],
        [kept, arrived],
    )
    (feed_sums,) = run(
        add_kernel,
        "feed_sums",
        [shape((chunk_rows, width), BF)],
        [],
        [],
        sum_parts(feed_chunks, "seq"),
    )
    feed_seq = from_all(feed_sums, "seq")

    sent, kept = run(
        functools.partial(last_grads_kernel, owners, seqs, blocks),
        "last_grads",
        [shape((owners // 2, own_rows + 16, third + width), BF)] * 2,
        [place],
        [],
        [
            *normed1_pieces,
            *att_pieces,
            d_projected,
            d_branch,
            column_sums,
            first_sums,
            middle_sums,
            up_sums,
        ],
        [vmem((seqs, rows, head_width), BF)],
        waits=[feed_chunks[0]],
    )
    kept, arrived, _ = owner_sums(kept, swap(sent, "fsdp", 1), place, "last_step")
    blk_rows = own_rows // blocks
    last_blocks = run(
        functools.partial(block_kernel, blocks),
        "last_blocks",
        [shape((blk_rows + 16, third + width), BF)] * blocks,
        [place],
        [],
        [kept, arrived],
    )
    last_main, *out_chunks = run(
        functools.partial(seq_kernel, blocks, seqs),
        "last_chunks",
        [shape((blk_rows + 16, width), BF)] + [shape((blk_rows, head_width), BF)] * seqs,
        [place],
        [],
        sum_parts(last_blocks, "blk"),
    )
    (last_sums,) = run(
        functools.partial(join_kernel, seqs),
        "last_sums",
        [shape((blk_rows + 16, width), BF)],
        [],
        [],
        [last_main, *sum_parts(out_chunks, "seq")],
    )
    last_seq = from_all(last_sums, "seq")
    (grad_tokens,) = run(
        functools.partial(first_back_kernel, seqs),
        "first_back",
        [shape((rows, width), F32)],
        [],
        [],
        [*d_normed1_pieces, inputs, d_middle, norm_gain],
        waits=[feed_sums],
    )
    outcome = sum(one.astype(F32) for one in sum_parts(rest[blocks:], "blk"))
    valid = lax.broadcasted_iota(jnp.int32, (rows, 1), 0) < counts[0, blk * seqs + seq]
    activations = jnp.where(valid, middle + outcome + biases[3], 0.0)

    feed_all = [from_all(one, "blk") for one in feed_seq]
    last_all = [from_all(one, "blk") for one in last_seq]
    grad_down, grad_up = run(
        functools.partial(
            place_kernel,
            seqs,
            blocks,
            [
                lambda b, k: [(0, chunk, 0, width, b * hidden_rows + k * chunk, 0)],
                lambda b, k: [
                    (
                        chunk + (i * hidden_rows // width) * up_chunk,
                        up_chunk,
                        i * hidden_rows % width,
                        hidden_rows,
                        k * up_chunk,
                        (i * blocks + b) * hidden_rows,
                    )
                    for i in range(owners)
                ],
            ],
        ),
        "place_feed",
        [shape((blocks * hidden_rows, width), F32), shape((own_rows, blocks * hidden_width), F32)],
        [place],
        [feed_all[k][m] for m in range(blocks) for k in range(seqs)],
        [],
        [vmem((blocks, seqs, chunk_rows, width), BF), dma((blocks * seqs,))],
        waits=last_seq[1:],
    )
    grad_qkv, grad_w_out = run(
        functools.partial(
            place_kernel,
            seqs,
            blocks,
            [
                lambda b, k: [
                    (
                        0,
                        blk_rows,
                        i * head_width,
                        head_width,
                        b * blk_rows,
                        i * width + k * head_width,
                    )
                    for i in range(3)
                ],
                lambda b, k: [(0, blk_rows, third, head_width, b * blk_rows, k * head_width)],
            ],
        ),
        "place_last",
        [shape((own_rows, 3 * width), F32), shape((own_rows, width), F32)],
        [place],
        [last_all[k][m] for m in range(blocks) for k in range(seqs)],
        [],
        [vmem((blocks, seqs, blk_rows + 16, width), BF), dma((blocks * seqs,))],
    )
    small = tree_sum([one[blk_rows:] for one in last_seq])
    lines = small[:8, :own_rows]
    return (
        activations[None],
        grad_tokens[None],
        jnp.stack([lines[0], lines[4]]),
        jnp.stack([lines[1], lines[5]]),
        jnp.stack([lines[2], lines[3], lines[6], lines[7]]),
        small[8, : blocks * hidden_rows],
        grad_qkv,
        grad_w_out,
        grad_up,
        grad_down,
    )


def solution(mesh):
    rows = P("fsdp", ("blk", "seq"), None)
    split = P("fsdp", None)
    return jax.shard_map(
        shards,
        mesh=mesh,
        in_specs=(rows, split, P(), P(), P(), P(), split, split, split, split, rows),
        out_specs=(
            rows,
            rows,
            P(None, "fsdp"),
            P(None, "fsdp"),
            P(None, "fsdp"),
            P("fsdp"),
            split,
            split,
            split,
            split,
        ),
        check_vma=False,
    )
```

```python
import functools

import jax
import jax.numpy as jnp
from jax import lax
from jax.experimental import pallas as pl
from jax.experimental.pallas import tpu as pltpu
from jax.sharding import PartitionSpec as P

HD = 64
EPSILON = 1e-06
MASKED = -1e30
SCALE = HD ** (-0.5)
BF = jnp.bfloat16
F32 = jnp.float32
VMEM_LIMIT = 44 * 1024 * 1024


def dot_nn(left_side, right_side):
    return lax.dot_general(
        left_side, right_side, (((1,), (0,)), ((), ())), preferred_element_type=F32
    )


def dot_nt(left_side, right_side):
    return lax.dot_general(
        left_side, right_side, (((1,), (1,)), ((), ())), preferred_element_type=F32
    )


def dot_tn(left_side, right_side):
    return lax.dot_general(
        left_side, right_side, (((0,), (0,)), ((), ())), preferred_element_type=F32
    )


def swap(array, axis, bits):
    return lax.ppermute(array, axis, [(i, i ^ bits) for i in range(lax.axis_size(axis))])


def from_all(array, axis):
    return [array] + [swap(array, axis, j) for j in range(1, lax.axis_size(axis))]


def doubled(array, axis, waits=()):
    pieces = {0: array}
    bit = lax.axis_size(axis) // 2
    while bit:
        pieces.update({j | bit: swap(piece, axis, bit) for j, piece in list(pieces.items())})
        if waits and bit == lax.axis_size(axis) // 2:
            pieces[bit] = gate(pieces[bit], waits)
        bit //= 2
    return [pieces[j] for j in range(lax.axis_size(axis))]


def piece_bias(place_ref, counts_ref, block, pieces, slot_rows):
    row = lax.broadcasted_iota(jnp.int32, (pieces * slot_rows, 1), 0)
    limit = jnp.zeros_like(row)
    for piece in range(pieces):
        held = (place_ref[0] ^ block) * pieces + (place_ref[1] ^ piece)
        end = counts_ref[0, held] + piece * slot_rows
        limit = jnp.where(row >= piece * slot_rows, end, limit)
    return jnp.where(row < limit, 0.0, MASKED)


def own_rows_valid(place_ref, counts_ref, seqs, rows):
    count = counts_ref[0, place_ref[0] * seqs + place_ref[1]]
    return lax.broadcasted_iota(jnp.int32, (rows, 1), 0) < count


def normalised(matrix_rows):
    centre = matrix_rows - jnp.mean(matrix_rows, axis=-1, keepdims=True)
    inverse = lax.rsqrt(jnp.mean(centre * centre, axis=-1, keepdims=True) + EPSILON)
    return centre * inverse, inverse


def norm_back(upstream, unit_rows, inverse, gain_row):
    scaled = upstream * gain_row
    return inverse * (
        scaled
        - jnp.mean(scaled, axis=-1, keepdims=True)
        - unit_rows * jnp.mean(scaled * unit_rows, axis=-1, keepdims=True)
    )


def row_of(ref, index):
    return ref[...].astype(F32)[index : index + 1]


def fetches(pieces, own, first, size, target, sems):
    return [
        pltpu.make_async_copy(
            piece.at[pl.ds(first, size)],
            target.at[pl.ds(pl.multiple_of((own ^ j) * size, 16), size)],
            sems.at[j],
        )
        for j, piece in enumerate(pieces)
    ]


def prepare_kernel(
    seqs,
    place_ref,
    counts_ref,
    grad_ref,
    qkv_ref,
    w_out_ref,
    outcome_ref,
    mine_ref,
    out_ref,
):
    out_ref[...] = w_out_ref[...]
    width = grad_ref.shape[1]
    size = width // seqs
    for part in range(3):
        chosen = qkv_ref[:, part * width : part * width + size]
        for k in range(1, seqs):
            first = part * width + k * size
            chosen = jnp.where(place_ref[1] == k, qkv_ref[:, first : first + size], chosen)
        mine_ref[:, part * size : (part + 1) * size] = chosen
    valid = own_rows_valid(place_ref, counts_ref, seqs, grad_ref.shape[0])
    outcome_ref[...] = jnp.where(valid, grad_ref[...], 0.0).astype(BF)


def first_norm_kernel(tokens_ref, gain_ref, shift_ref, normed_ref):
    unit = normalised(tokens_ref[...])[0]
    normed_ref[...] = (unit * row_of(gain_ref, 0) + row_of(shift_ref, 0)).astype(BF)


def pack_kernel(owners, blocks, parts, place_ref, up_ref, down_ref, out_ref, sems):
    rows, width = up_ref.shape[0], down_ref.shape[1]
    size = down_ref.shape[0] // blocks
    copies = []
    for i in range(owners):
        first = pl.multiple_of((i * blocks + place_ref[0]) * size, 128)
        part, column = divmod(i * size, width)
        copies.append((up_ref.at[:, pl.ds(first, size)],
                       out_ref.at[pl.ds(part * rows, rows), pl.ds(column, size)]))
    first = pl.multiple_of(place_ref[0] * size, 16)
    copies.append((down_ref.at[pl.ds(first, size)], out_ref.at[pl.ds(parts * rows, size)]))
    copies = [
        pltpu.make_async_copy(source, target, sems.at[i])
        for i, (source, target) in enumerate(copies)
    ]
    for copy in copies:
        copy.start()
    for copy in copies:
        copy.wait()


def qkv_kernel(owners, seqs, place_ref, *refs):
    pieces, normed_refs, refs = refs[:owners], refs[owners : owners + seqs], refs[owners + seqs :]
    shift_ref, kv_ref, q_ref, w_ref, sems = refs
    own_rows, size = pieces[0].shape[0], q_ref.shape[1]
    copies = fetches(pieces, place_ref[2], 0, own_rows, w_ref, sems)
    for copy in copies:
        copy.start()
    normed = jnp.concatenate([ref[...] for ref in normed_refs])
    for copy in copies:
        copy.wait()
    result = (dot_nn(normed, w_ref[...]) + shift_ref[...]).astype(BF)
    q_ref[...] = result[:, :size]
    kv_ref[...] = result[:, size:]


def attend_kernel(blocks, heads, pieces, slot_rows, place_ref, counts_ref, q_ref, *refs):
    kv_refs, out_refs, log_ref = refs[:blocks], refs[blocks:-1], refs[-1]
    width = heads * HD
    biases = [piece_bias(place_ref, counts_ref, m, pieces, slot_rows) for m in range(blocks)]
    for head in range(heads):
        low, high = head * HD, (head + 1) * HD
        query = q_ref[:, low:high] * SCALE
        scores = [dot_nt(kv[:, low:high], query) + bias for kv, bias in zip(kv_refs, biases)]
        top = functools.reduce(
            jnp.maximum, [jnp.max(block, axis=0, keepdims=True) for block in scores]
        )
        powers = [jnp.exp(block - top) for block in scores]
        total = sum(jnp.sum(block, axis=0, keepdims=True) for block in powers)
        inverse = 1.0 / total
        result = sum(
            dot_tn((block * inverse).astype(BF), kv[:, width + low : width + high])
            for block, kv in zip(powers, kv_refs)
        ).astype(BF)
        for k, out_ref in enumerate(out_refs):
            out_ref[:, low:high] = result[k * slot_rows : (k + 1) * slot_rows]
        log_ref[head : head + 1, :] = top + jnp.log(total)


def attend_back_kernel(blocks, heads, pieces, slot_rows, place_ref, counts_ref, q_ref, log_ref, *refs):
    d_refs, refs = refs[:pieces], refs[pieces:]
    kv_refs, dq_ref, dkv_refs = refs[:blocks], refs[blocks], refs[blocks + 1 :]
    width = heads * HD
    biases = [piece_bias(place_ref, counts_ref, m, pieces, slot_rows) for m in range(blocks)]
    for head in range(heads):
        low, high = head * HD, (head + 1) * HD
        query = q_ref[:, low:high] * SCALE
        d_out = jnp.concatenate([d_ref[:, low:high] for d_ref in d_refs])
        log_row = log_ref[head : head + 1, :]
        softs, d_softs, delta = [], [], 0.0
        for kv, bias in zip(kv_refs, biases):
            soft = jnp.exp(dot_nt(kv[:, low:high], query) + bias - log_row)
            d_soft = dot_nt(kv[:, width + low : width + high], d_out)
            delta = delta + jnp.sum(soft * d_soft, axis=0, keepdims=True)
            softs.append(soft)
            d_softs.append(d_soft)
        d_query = 0.0
        for kv, dkv, soft, d_soft in zip(kv_refs, dkv_refs, softs, d_softs):
            d_scores = (soft * (d_soft - delta)).astype(BF)
            d_query = d_query + dot_tn(d_scores, kv[:, low:high])
            dkv[:, low:high] = dot_nn(d_scores, query).astype(dkv.dtype)
            dkv[:, width + low : width + high] = dot_nn(soft.astype(BF), d_out).astype(dkv.dtype)
        dq_ref[:, low:high] = (d_query * SCALE).astype(BF)


def project_kernel(owners, seqs, place_ref, *refs):
    pieces, att_refs = refs[:owners], refs[owners : owners + seqs]
    tokens_ref, vec_ref, gain_ref, shift_ref, middle_ref, normed_ref, w_ref, sems = refs[owners + seqs :]
    own_rows, head_width = w_ref.shape[0] // owners, w_ref.shape[0] // seqs
    copies = fetches(pieces, place_ref[2], 0, own_rows, w_ref, sems)
    for copy in copies:
        copy.start()
    middle = tokens_ref[...] + row_of(vec_ref, 2)
    for copy in copies:
        copy.wait()
    for k, att_ref in enumerate(att_refs):
        first = pl.multiple_of((place_ref[1] ^ k) * head_width, 16)
        middle = middle + dot_nn(att_ref[...], w_ref[pl.ds(first, head_width), :])
    middle_ref[...] = middle
    unit = normalised(middle)[0]
    normed_ref[...] = (unit * row_of(gain_ref, 1) + row_of(shift_ref, 1)).astype(BF)


def hidden_kernel(owners, blocks, own_rows, hidden_rows, place_ref, *refs):
    pieces, refs = refs[:owners], refs[owners:]
    normed_refs, outcome_refs, refs = refs[:blocks], refs[blocks : 2 * blocks], refs[2 * blocks :]
    shift_ref, hidden_ref, d_up_ref, sums_ref = refs[:4]
    d_normed_refs, out_refs = refs[4 : 4 + blocks], refs[4 + blocks : 4 + 2 * blocks]
    up_ref, down_ref, sems = refs[4 + 2 * blocks :]
    parts, width = up_ref.shape[0], up_ref.shape[1]
    own = place_ref[2]
    waits = []
    for part in range(parts):
        waits += fetches(
            pieces, own, part * own_rows, own_rows, up_ref.at[part], sems.at[part]
        )
    waits += fetches(pieces, own, parts * own_rows, hidden_rows, down_ref, sems.at[parts])
    for copy in waits:
        copy.start()
    normed = jnp.concatenate([ref[...] for ref in normed_refs])
    outcome = jnp.concatenate([ref[...] for ref in outcome_refs])
    for copy in waits:
        copy.wait()
    size = min(384, parts * width)
    d_normed, result = 0.0, 0.0
    for first in range(0, parts * width, size):
        part, column = first // width, first % width
        up_weights = up_ref[part, :, column : column + size]
        down_weights = down_ref[first : first + size, :]
        up_proj = dot_nn(normed, up_weights) + shift_ref[:, first : first + size]
        chance = 0.5 * (1.0 + lax.erf(up_proj * (0.5**0.5)))
        hidden = (up_proj * chance).astype(BF)
        slope = chance + up_proj * (jnp.exp(-0.5 * up_proj * up_proj) * 0.3989422804014327)
        d_up = (dot_nt(outcome, down_weights) * slope).astype(BF)
        hidden_ref[:, first : first + size] = hidden
        d_up_ref[:, first : first + size] = d_up
        sums_ref[:, first : first + size] = jnp.sum(d_up.astype(F32), axis=0, keepdims=True)
        d_normed = d_normed + dot_nt(d_up, up_weights)
        result = result + dot_nn(hidden, down_weights)
    rows = normed_refs[0].shape[0]
    for m in range(blocks):
        d_normed_refs[m][...] = d_normed[m * rows : (m + 1) * rows].astype(d_normed_refs[m].dtype)
        out_refs[m][...] = result[m * rows : (m + 1) * rows].astype(out_refs[m].dtype)


def middle_kernel(owners, seqs, blocks, place_ref, counts_ref, *refs):
    pieces, refs = refs[:owners], refs[owners:]
    d_normed_refs, refs = refs[:blocks], refs[blocks:]
    middle_in_ref, grad_ref, gain_ref, d_middle_ref, d_branch_ref, sums_ref = refs[:6]
    head_refs, (w_ref, sems) = refs[6 : 6 + seqs], refs[6 + seqs :]
    own_rows, head_width = w_ref.shape[0] // owners, w_ref.shape[0] // seqs
    copies = fetches(pieces, place_ref[2], 0, own_rows, w_ref, sems)
    for copy in copies:
        copy.start()
    valid = own_rows_valid(place_ref, counts_ref, seqs, grad_ref.shape[0])
    grad_rows = jnp.where(valid, grad_ref[...], 0.0)
    unit, inverse = normalised(middle_in_ref[...])
    upstream = sum(ref[...].astype(F32) for ref in d_normed_refs)
    d_middle = grad_rows + norm_back(upstream, unit, inverse, row_of(gain_ref, 1))
    d_branch = d_middle.astype(BF)
    d_middle_ref[...] = d_middle
    d_branch_ref[...] = d_branch
    for copy in copies:
        copy.wait()
    for k, head_ref in enumerate(head_refs):
        first = pl.multiple_of((place_ref[1] ^ k) * head_width, 16)
        head_ref[...] = dot_nt(d_branch, w_ref[pl.ds(first, head_width), :]).astype(BF)
    rows = (
        upstream * unit,
        upstream,
        d_branch.astype(F32),
        grad_rows.astype(BF).astype(F32),
    )
    for index, one in enumerate(rows):
        sums_ref[index : index + 1, :] = jnp.sum(one, axis=0, keepdims=True)


def grads_kernel(owners, seqs, blocks, own_rows, hidden_rows, place_ref, *refs):
    normed_refs, outcome_refs, refs = refs[:blocks], refs[blocks : 2 * blocks], refs[2 * blocks :]
    hidden_ref, d_up_ref, sent_ref, kept_ref = refs
    width = outcome_refs[0].shape[1]
    parts = d_up_ref.shape[1] // width
    bit = place_ref[2] & 1
    normed = jnp.concatenate([ref[...] for ref in normed_refs])
    outcome = jnp.concatenate([ref[...] for ref in outcome_refs])
    chunk, up_chunk = hidden_rows // seqs, own_rows // seqs
    for owner in range(owners):
        down = dot_tn(hidden_ref[:, owner * hidden_rows : (owner + 1) * hidden_rows], outcome)
        rows_in = normed[:, owner * own_rows : (owner + 1) * own_rows]
        ups = [
            dot_tn(rows_in, d_up_ref[:, part * width : (part + 1) * width]) for part in range(parts)
        ]

        def store(ref, owner=owner, down=down, ups=ups):
            for k in range(seqs):
                ref[owner // 2, k, 0:chunk, :] = down[k * chunk : (k + 1) * chunk].astype(BF)
                for part, up in enumerate(ups):
                    first = chunk + part * up_chunk
                    ref[owner // 2, k, first : first + up_chunk, :] = up[
                        k * up_chunk : (k + 1) * up_chunk
                    ].astype(BF)

        @pl.when(bit == owner % 2)
        def keep():
            store(kept_ref)

        @pl.when(bit != owner % 2)
        def send():
            store(sent_ref)


def step_kernel(bit, place_ref, kept_ref, arrived_ref, sent_ref, next_ref):
    high = (place_ref[2] // bit) & 1
    for i in range(sent_ref.shape[0]):
        for ref, index in ((sent_ref, 2 * i + 1 - high), (next_ref, 2 * i + high)):
            ref[i] = (kept_ref[index].astype(F32) + arrived_ref[index].astype(F32)).astype(BF)


def chunk_kernel(seqs, place_ref, kept_ref, arrived_ref, *out_refs):
    for j in range(seqs):
        index = place_ref[1] ^ j
        total = kept_ref[0, index].astype(F32) + arrived_ref[0, index].astype(F32)
        out_refs[j][...] = total.astype(BF)


def add_kernel(*refs):
    refs[-1][...] = sum(ref[...].astype(F32) for ref in refs[:-1]).astype(BF)


def out_chunks_kernel(blocks, seqs, place_ref, *refs):
    total = sum(ref[...].astype(F32) for ref in refs[:blocks])
    size = total.shape[1] // seqs
    for j in range(seqs):
        chosen = total[:, :size]
        for k in range(1, seqs):
            columns = total[:, k * size : (k + 1) * size]
            chosen = jnp.where(place_ref[1] ^ j == k, columns, chosen)
        refs[blocks + j][...] = chosen.astype(BF)


def join_kernel(blocks, seqs, *refs):
    in_refs, part_refs, out_ref = refs[:blocks], refs[blocks : blocks + seqs], refs[-1]
    terms = [ref[...].astype(F32) for ref in in_refs]
    while len(terms) > 1:
        terms = [terms[i] + terms[i + 1] for i in range(0, len(terms), 2)]
    out_ref[...] = terms[0].astype(BF)
    total = sum(ref[...].astype(F32) for ref in part_refs)
    size, columns = total.shape
    out_ref[0:size, 3 * columns :] = total.astype(BF)


def project_back_kernel(blocks, seqs, *refs):
    q_ref, kv_refs, w_ref, refs = refs[0], refs[1 : 1 + blocks], refs[1 + blocks], refs[2 + blocks :]
    normed_refs, (gain_ref, shift_ref), refs = refs[:seqs], refs[seqs : seqs + 2], refs[seqs + 2 :]
    projected_ref, columns_ref, sums_ref, part_refs = refs[0], refs[1], refs[2], refs[3:]
    d_kv = sum(ref[...].astype(F32) for ref in kv_refs).astype(BF)
    d_projected = jnp.concatenate([q_ref[...], d_kv], axis=1)
    projected_ref[...] = d_projected
    columns_ref[...] = jnp.sum(d_projected.astype(F32), axis=0, keepdims=True)
    rows = normed_refs[0].shape[0]
    gain, shift = row_of(gain_ref, 0), row_of(shift_ref, 0)
    with_normed, plain = 0.0, 0.0
    for k in range(seqs):
        part = dot_nt(d_projected[k * rows : (k + 1) * rows], w_ref[...])
        part_refs[k][...] = part.astype(BF)
        with_normed = with_normed + jnp.sum(
            part * (normed_refs[k][...].astype(F32) - shift), axis=0, keepdims=True
        )
        plain = plain + jnp.sum(part, axis=0, keepdims=True)
    sums_ref[0:1, :] = with_normed / gain
    sums_ref[1:2, :] = plain


def by_core(bit, owner, refs, store):
    sent_ref, kept_ref = refs

    @pl.when(bit == owner % 2)
    def keep():
        store(kept_ref)

    @pl.when(bit != owner % 2)
    def send():
        store(sent_ref)


def out_grads_kernel(owners, seqs, place_ref, *refs):
    att_refs, branch_ref, (sent_ref, kept_ref, att_ref) = refs[:seqs], refs[seqs], refs[seqs + 1 :]
    size = att_refs[0].shape[1]
    own_rows = branch_ref.shape[1] // owners
    for k in range(seqs):
        att_ref[place_ref[1] ^ k] = att_refs[k][...]
    for owner in range(owners):
        group, column = divmod(owner * own_rows, size)
        out = dot_tn(att_ref[group][:, column : column + own_rows], branch_ref[...]).astype(BF)

        def store(ref, owner=owner, out=out):
            ref[owner // 2] = out

        by_core(place_ref[2] & 1, owner, (sent_ref, kept_ref), store)


def last_grads_kernel(owners, seqs, blocks, place_ref, *refs):
    normed_refs, refs = refs[:seqs], refs[seqs:]
    (projected_ref, columns_ref, first_ref, middle_ref, up_ref, sent_ref, kept_ref) = refs
    width, third = first_ref.shape[1], projected_ref.shape[1]
    size = third // 3
    own_rows, hidden_rows = width // owners, up_ref.shape[1] // owners
    normed = jnp.concatenate([ref[...] for ref in normed_refs])
    projected = projected_ref[...]
    for owner in range(owners):
        first = owner * own_rows
        group, column = divmod(first, size)
        qkv = dot_tn(normed[:, first : first + own_rows], projected).astype(BF)
        is_group = place_ref[1] == group
        bias = [
            jnp.where(is_group, columns_ref[:, start : start + own_rows], 0.0)
            for start in (column, 2 * size + column)
        ]
        lines = [
            first_ref[0:1, first : first + own_rows],
            first_ref[1:2, first : first + own_rows],
            *bias,
        ] + [middle_ref[i : i + 1, first : first + own_rows] for i in range(4)]
        lines = jnp.concatenate(lines).astype(BF)
        up_line = up_ref[:, owner * hidden_rows : (owner + 1) * hidden_rows]
        up_line = jnp.concatenate(
            [jnp.where(place_ref[0] == b, up_line, 0.0) for b in range(blocks)], axis=1
        ).astype(BF)

        def store(ref, owner=owner, qkv=qkv, lines=lines, up_line=up_line):
            ref[owner // 2, 0:own_rows, 0:third] = qkv
            ref[owner // 2, 0:own_rows, third:] = jnp.zeros((own_rows, width - third), BF)
            ref[owner // 2, own_rows:, :] = jnp.zeros((16, width), BF)
            ref[owner // 2, own_rows : own_rows + 8, 0:own_rows] = lines
            ref[owner // 2, own_rows + 8 : own_rows + 9, 0 : up_line.shape[1]] = up_line

        by_core(place_ref[2] & 1, owner, (sent_ref, kept_ref), store)


def block_kernel(blocks, tail, place_ref, kept_ref, arrived_ref, *out_refs):
    total = kept_ref[0].astype(F32) + arrived_ref[0].astype(F32)
    own_rows = total.shape[0] - tail
    size = own_rows // blocks
    for m in range(blocks):
        chosen = total[:size]
        for j in range(1, blocks):
            chosen = jnp.where(place_ref[0] ^ m == j, total[j * size : (j + 1) * size], chosen)
        out_refs[m][0:size, :] = chosen.astype(BF)
        if tail:
            out_refs[m][size:, :] = total[own_rows:].astype(BF)


def first_back_kernel(pieces, *refs):
    part_refs, (tokens_ref, d_middle_ref, gain_ref, out_ref) = refs[:pieces], refs[pieces:]
    upstream = sum(ref[:, : out_ref.shape[1]].astype(F32) for ref in part_refs)
    unit, inverse = normalised(tokens_ref[...])
    out_ref[...] = d_middle_ref[...] + norm_back(upstream, unit, inverse, row_of(gain_ref, 0))


def place_kernel(seqs, blocks, layouts, place_ref, *refs):
    pieces = refs[: blocks * seqs]
    outs = refs[blocks * seqs : -2]
    held, sems = refs[-2:]
    blk, seq = place_ref[0], place_ref[1]
    copies = [
        pltpu.make_async_copy(
            pieces[m * seqs + k],
            held.at[jnp.bitwise_xor(blk, m), jnp.bitwise_xor(seq, k)],
            sems.at[m * seqs + k],
        )
        for m in range(blocks)
        for k in range(seqs)
    ]
    for copy in copies:
        copy.start()
    for copy in copies:
        copy.wait()
    for out, spots in zip(outs, layouts):
        for b in range(blocks):
            for k in range(seqs):
                for top, rows, first, size, row, column in spots(b, k):
                    piece = held[b, k, top : top + rows, first : first + size]
                    out[row : row + rows, column : column + size] = piece.astype(F32)


def run(kernel, label, outs, scalars, remote, arrays, scratch=(), waits=(), in_hbm=False, cost=1.0):
    inputs = len(scalars) + len(remote) + len(arrays)

    def without_waits(*refs):
        kernel(*refs[:inputs], *refs[inputs + len(waits) :])

    return pl.pallas_call(
        without_waits,
        out_shape=tuple(outs),
        in_specs=[pl.BlockSpec(memory_space=pltpu.SMEM)] * len(scalars)
        + [pl.BlockSpec(memory_space=pltpu.HBM)] * len(remote)
        + [pl.BlockSpec(memory_space=pltpu.VMEM)] * len(arrays)
        + [pl.BlockSpec(memory_space=pltpu.HBM)] * len(waits),
        out_specs=(pl.BlockSpec(memory_space=pltpu.HBM if in_hbm else pltpu.VMEM),) * len(outs),
        scratch_shapes=list(scratch),
        compiler_params=pltpu.CompilerParams(vmem_limit_bytes=VMEM_LIMIT),
        cost_estimate=pl.CostEstimate(
            flops=1, bytes_accessed=int(cost * 1.2e6), transcendentals=0
        ),
        name=label,
    )(*scalars, *remote, *arrays, *waits)


def shape(dims, kind):
    return jax.ShapeDtypeStruct(tuple(dims), kind)


def gate(array, waits):
    def nothing(*refs):
        pass

    return pl.pallas_call(
        nothing,
        out_shape=shape(array.shape, array.dtype),
        in_specs=[pl.BlockSpec(memory_space=pltpu.HBM)] * (1 + len(waits)),
        out_specs=pl.BlockSpec(memory_space=pltpu.HBM),
        input_output_aliases={0: 0},
        cost_estimate=pl.CostEstimate(flops=1, bytes_accessed=1, transcendentals=0),
        name="gate",
    )(array, *waits)


def owner_sums(kept, arrived, place, label, waits=()):
    sent, bit = None, 2
    while bit < lax.axis_size("fsdp"):
        half = (kept.shape[0] // 2, *kept.shape[1:])
        sent, kept = run(
            functools.partial(step_kernel, bit),
            label,
            [shape(half, BF)] * 2,
            [place],
            [],
            [kept, arrived],
            waits=waits,
        )
        arrived = swap(sent, "fsdp", bit)
        bit *= 2
    return kept, arrived, sent


def sum_parts(parts, axis):
    return [parts[0]] + [swap(parts[j], axis, j) for j in range(1, len(parts))]


def tree_sum(pieces):
    pieces = [piece.astype(F32) for piece in pieces]
    while len(pieces) > 1:
        pieces = [pieces[i] + pieces[i + 1] for i in range(0, len(pieces), 2)]
    return pieces[0]


def shards(
    tokens, counts, norm_gain, norm_bias, vec_bias, up_bias, w_qkv, w_out, w_up, w_down, grad_out
):
    owners, blocks, seqs = (lax.axis_size(name) for name in ("fsdp", "blk", "seq"))
    own, blk, seq = (lax.axis_index(name) for name in ("fsdp", "blk", "seq"))
    place = jnp.stack([blk, seq, own]).astype(jnp.int32)
    rows, width = tokens.shape[1:]
    head_width = width // seqs
    heads, third = head_width // HD, 3 * head_width
    own_rows = width // owners
    hidden_rows = w_down.shape[0] // blocks
    hidden_width = hidden_rows * owners
    parts = hidden_width // width
    block_rows, all_rows = seqs * rows, blocks * rows
    inputs, grad_in = tokens[0], grad_out[0]
    vmem, dma = pltpu.VMEM, pltpu.SemaphoreType.DMA

    (normed1,) = run(
        first_norm_kernel,
        "first_norm",
        [shape((rows, width), BF)],
        [],
        [],
        [inputs, norm_gain, norm_bias],
    )
    normed1_pieces = from_all(normed1, "seq")
    d_outcome, qkv_mine, out_mine = run(
        functools.partial(prepare_kernel, seqs),
        "prepare",
        [
            shape((rows, width), BF),
            shape((own_rows, third), BF),
            shape((own_rows, width), BF),
        ],
        [place, counts],
        [],
        [grad_in, w_qkv, w_out],
        waits=[normed1],
    )
    qkv_pieces = doubled(qkv_mine, "fsdp")
    out_pieces = doubled(out_mine, "fsdp")
    outcome_pieces = from_all(d_outcome, "blk")

    biases = vec_bias.astype(F32)
    qkv_shift = jnp.concatenate(
        [
            lax.dynamic_slice_in_dim(biases[0], seq * head_width, head_width),
            jnp.zeros((head_width,), F32),
            lax.dynamic_slice_in_dim(biases[1], seq * head_width, head_width),
        ]
    ).reshape(1, third)
    up_shift = (
        lax.dynamic_index_in_dim(up_bias.reshape(owners, blocks, hidden_rows), blk, 1, False)
        .astype(F32)
        .reshape(1, hidden_width)
    )

    key_value, queries, qkv_full = run(
        functools.partial(qkv_kernel, owners, seqs),
        "project_in",
        [
            shape((block_rows, 2 * head_width), BF),
            shape((block_rows, head_width), BF),
            shape((width, third), BF),
        ],
        [place],
        qkv_pieces,
        [*normed1_pieces, qkv_shift],
        [dma((owners,))],
        waits=[*outcome_pieces[1:], out_pieces[owners // 2]],
    )
    packed = shape((parts * own_rows + hidden_rows, width), BF)
    if hidden_rows % 128 == 0:
        (weights_mine,) = run(
            functools.partial(pack_kernel, owners, blocks, parts),
            "pack",
            [packed],
            [place],
            [w_up, w_down],
            [],
            [dma((owners + 1,))],
            waits=[key_value],
            in_hbm=True,
        )
    else:
        columns = [
            lax.dynamic_slice_in_dim(w_up, (i * blocks + blk) * hidden_rows, hidden_rows, axis=1)
            for i in range(owners)
        ]
        in_part = owners // parts
        weights_mine = jnp.concatenate(
            [
                jnp.concatenate(columns[part * in_part : (part + 1) * in_part], axis=1)
                for part in range(parts)
            ]
            + [lax.dynamic_slice_in_dim(w_down, blk * hidden_rows, hidden_rows, axis=0)]
        )

    kv_blocks = from_all(key_value, "blk")
    *att_out, log_total = run(
        functools.partial(attend_kernel, blocks, heads, seqs, rows),
        "attend",
        [shape((rows, head_width), BF)] * seqs + [shape((heads, block_rows), F32)],
        [place, counts],
        [],
        [queries, *kv_blocks],
        waits=out_pieces[1:],
        cost=1.3,
    )
    att_pieces = sum_parts(att_out, "seq")
    weights = doubled(weights_mine, "fsdp", att_pieces[1:])
    middle, normed2 = run(
        functools.partial(project_kernel, owners, seqs),
        "project_out",
        [shape((rows, width), F32), shape((rows, width), BF)],
        [place],
        out_pieces,
        [*att_pieces, inputs, vec_bias, norm_gain, norm_bias],
        [vmem((width, width), BF), dma((owners,))],
    )

    normed_pieces = from_all(normed2, "blk")
    row_shapes = [shape((rows, width), F32)] + [shape((rows, width), BF)] * (blocks - 1)
    hidden, d_up, up_sums, *rest = run(
        functools.partial(hidden_kernel, owners, blocks, own_rows, hidden_rows),
        "hidden",
        [shape((all_rows, hidden_width), BF)] * 2
        + [shape((1, hidden_width), F32)]
        + row_shapes * 2,
        [place],
        weights,
        [*normed_pieces, *outcome_pieces, up_shift],
        [
            vmem((parts, width, width), BF),
            vmem((hidden_width, width), BF),
            dma((parts + 1, owners)),
        ],
        cost=2.3,
    )
    d_normed_pieces = sum_parts(rest[:blocks], "blk")
    chunk, up_chunk = hidden_rows // seqs, own_rows // seqs
    chunk_rows = chunk + parts * up_chunk
    sent, kept = run(
        functools.partial(grads_kernel, owners, seqs, blocks, own_rows, hidden_rows),
        "feed_grads",
        [shape((owners // 2, seqs, chunk_rows, width), BF)] * 2,
        [place],
        [],
        [*normed_pieces, *outcome_pieces, hidden, d_up],
        cost=1.3,
    )
    d_middle, d_branch, middle_sums, *d_heads = run(
        functools.partial(middle_kernel, owners, seqs, blocks),
        "middle",
        [shape((rows, width), F32), shape((rows, width), BF), shape((4, width), F32)]
        + [shape((rows, head_width), BF)] * seqs,
        [place, counts],
        out_pieces,
        [*d_normed_pieces, middle, grad_in, norm_gain],
        [vmem((width, width), BF), dma((owners,))],
        waits=[sent],
    )
    d_att_pieces = sum_parts(d_heads, "seq")
    kept, arrived, feed_sent = owner_sums(
        kept, swap(gate(sent, [d_branch]), "fsdp", 1), place, "feed_step"
    )
    d_query, *d_kv = run(
        functools.partial(attend_back_kernel, blocks, heads, seqs, rows),
        "attend_back",
        [shape((block_rows, head_width), BF), shape((block_rows, 2 * head_width), F32)]
        + [shape((block_rows, 2 * head_width), BF)] * (blocks - 1),
        [place, counts],
        [],
        [queries, log_total, *d_att_pieces, *kv_blocks],
        waits=[feed_sent],
        cost=1.9,
    )
    out_sent, out_kept = run(
        functools.partial(out_grads_kernel, owners, seqs),
        "out_grads",
        [shape((owners // 2, own_rows, width), BF)] * 2,
        [place],
        [],
        [*att_pieces, d_branch],
        [vmem((seqs, rows, head_width), BF)],
        waits=[d_query],
    )
    out_kept, out_arrived, out_step = owner_sums(
        out_kept, swap(out_sent, "fsdp", 1), place, "out_step"
    )
    blk_rows = own_rows // blocks
    d_projected, column_sums, first_sums, *d_normed1 = run(
        functools.partial(project_back_kernel, blocks, seqs),
        "project_back",
        [
            shape((block_rows, third), BF),
            shape((1, third), F32),
            shape((2, width), F32),
        ]
        + [shape((rows, width), BF)] * seqs,
        [],
        [],
        [d_query, *sum_parts(d_kv, "blk"), qkv_full, *normed1_pieces, norm_gain, norm_bias],
    )
    d_normed1_pieces = sum_parts(d_normed1, "seq")
    (grad_tokens,) = run(
        functools.partial(first_back_kernel, seqs),
        "first_back",
        [shape((rows, width), F32)],
        [],
        [],
        [*d_normed1_pieces, inputs, d_middle, norm_gain],
    )

    out_blocks = run(
        functools.partial(block_kernel, blocks, 0),
        "out_blocks",
        [shape((blk_rows, width), BF)] * blocks,
        [place],
        [],
        [out_kept, out_arrived],
        waits=[grad_tokens],
    )
    feed_chunks = run(
        functools.partial(chunk_kernel, seqs),
        "feed_chunks",
        [shape((chunk_rows, width), BF)] * seqs,
        [place],
        [],
        [kept, arrived],
    )
    (feed_sums,) = run(
        add_kernel,
        "feed_sums",
        [shape((chunk_rows, width), BF)],
        [],
        [],
        sum_parts(feed_chunks, "seq"),
    )

    sent, last_kept = run(
        functools.partial(last_grads_kernel, owners, seqs, blocks),
        "last_grads",
        [shape((owners // 2, own_rows + 16, width), BF)] * 2,
        [place],
        [],
        [*normed1_pieces, d_projected, column_sums, first_sums, middle_sums, up_sums],
        waits=[out_step],
    )
    last_kept, last_arrived, _ = owner_sums(
        last_kept, swap(sent, "fsdp", 1), place, "last_step", waits=feed_chunks[:1]
    )
    last_blocks = run(
        functools.partial(block_kernel, blocks, 16),
        "last_blocks",
        [shape((blk_rows + 16, width), BF)] * blocks,
        [place],
        [],
        [last_kept, last_arrived],
        waits=[feed_sums],
    )
    out_chunks = run(
        functools.partial(out_chunks_kernel, blocks, seqs),
        "out_chunks",
        [shape((blk_rows, head_width), BF)] * seqs,
        [place],
        [],
        sum_parts(out_blocks, "blk"),
    )
    (last_sums,) = run(
        functools.partial(join_kernel, blocks, seqs),
        "last_sums",
        [shape((blk_rows + 16, width), BF)],
        [],
        [],
        [*sum_parts(last_blocks, "blk"), *sum_parts(out_chunks, "seq")],
    )
    feed_seq = from_all(feed_sums, "seq")
    last_seq = from_all(gate(last_sums, [feed_seq[1]]), "seq")
    outcome = sum(one.astype(F32) for one in sum_parts(rest[blocks:], "blk"))
    valid = lax.broadcasted_iota(jnp.int32, (rows, 1), 0) < counts[0, blk * seqs + seq]
    activations = jnp.where(valid, middle + outcome + biases[3], 0.0)

    feed_all = [from_all(one, "blk") for one in feed_seq]
    last_all = [from_all(one, "blk") for one in last_seq]
    grad_down, grad_up = run(
        functools.partial(
            place_kernel,
            seqs,
            blocks,
            [
                lambda b, k: [(0, chunk, 0, width, b * hidden_rows + k * chunk, 0)],
                lambda b, k: [
                    (
                        chunk + (i * hidden_rows // width) * up_chunk,
                        up_chunk,
                        i * hidden_rows % width,
                        hidden_rows,
                        k * up_chunk,
                        (i * blocks + b) * hidden_rows,
                    )
                    for i in range(owners)
                ],
            ],
        ),
        "place_feed",
        [shape((blocks * hidden_rows, width), F32), shape((own_rows, blocks * hidden_width), F32)],
        [place],
        [feed_all[k][m] for m in range(blocks) for k in range(seqs)],
        [],
        [vmem((blocks, seqs, chunk_rows, width), BF), dma((blocks * seqs,))],
        waits=last_seq[1:],
    )
    grad_qkv, grad_w_out = run(
        functools.partial(
            place_kernel,
            seqs,
            blocks,
            [
                lambda b, k: [
                    (
                        0,
                        blk_rows,
                        i * head_width,
                        head_width,
                        b * blk_rows,
                        i * width + k * head_width,
                    )
                    for i in range(3)
                ],
                lambda b, k: [(0, blk_rows, third, head_width, b * blk_rows, k * head_width)],
            ],
        ),
        "place_last",
        [shape((own_rows, 3 * width), F32), shape((own_rows, width), F32)],
        [place],
        [last_all[k][m] for m in range(blocks) for k in range(seqs)],
        [],
        [vmem((blocks, seqs, blk_rows + 16, width), BF), dma((blocks * seqs,))],
        waits=[grad_down],
    )
    small = tree_sum([one[blk_rows:] for one in last_seq])
    lines = small[:8, :own_rows]
    return (
        activations[None],
        grad_tokens[None],
        jnp.stack([lines[0], lines[4]]),
        jnp.stack([lines[1], lines[5]]),
        jnp.stack([lines[2], lines[3], lines[6], lines[7]]),
        small[8, : blocks * hidden_rows],
        grad_qkv,
        grad_w_out,
        grad_up,
        grad_down,
    )


def solution(mesh):
    rows = P("fsdp", ("blk", "seq"), None)
    split = P("fsdp", None)
    return jax.shard_map(
        shards,
        mesh=mesh,
        in_specs=(rows, split, P(), P(), P(), P(), split, split, split, split, rows),
        out_specs=(
            rows,
            rows,
            P(None, "fsdp"),
            P(None, "fsdp"),
            P(None, "fsdp"),
            P("fsdp"),
            split,
            split,
            split,
            split,
        ),
        check_vma=False,
    )
```

```python
import functools

import jax
import jax.numpy as jnp
from jax import lax
from jax.experimental import pallas as pl
from jax.experimental.pallas import tpu as pltpu
from jax.sharding import PartitionSpec as P

HD = 64
EPSILON = 1e-06
MASKED = -1e30
SCALE = HD ** (-0.5)
BF = jnp.bfloat16
F32 = jnp.float32


def dot_nn(left_side, right_side):
    return lax.dot_general(
        left_side, right_side, (((1,), (0,)), ((), ())), preferred_element_type=F32
    )


def dot_nt(left_side, right_side):
    return lax.dot_general(
        left_side, right_side, (((1,), (1,)), ((), ())), preferred_element_type=F32
    )


def dot_tn(left_side, right_side):
    return lax.dot_general(
        left_side, right_side, (((0,), (0,)), ((), ())), preferred_element_type=F32
    )


def swap(array, axis, bits):
    return lax.ppermute(array, axis, [(i, i ^ bits) for i in range(lax.axis_size(axis))])


def from_all(array, axis):
    return [array] + [swap(array, axis, j) for j in range(1, lax.axis_size(axis))]


def doubled(array, axis, waits=()):
    pieces = {0: array}
    bit = lax.axis_size(axis) // 2
    while bit:
        pieces.update({j | bit: swap(piece, axis, bit) for j, piece in list(pieces.items())})
        if waits and bit == lax.axis_size(axis) // 2:
            pieces[bit] = gate(pieces[bit], waits)
        bit //= 2
    return [pieces[j] for j in range(lax.axis_size(axis))]


def piece_bias(place_ref, counts_ref, block, pieces, slot_rows):
    row = lax.broadcasted_iota(jnp.int32, (pieces * slot_rows, 1), 0)
    limit = jnp.zeros_like(row)
    for piece in range(pieces):
        held = (place_ref[0] ^ block) * pieces + (place_ref[1] ^ piece)
        end = counts_ref[0, held] + piece * slot_rows
        limit = jnp.where(row >= piece * slot_rows, end, limit)
    return jnp.where(row < limit, 0.0, MASKED)


def own_rows_valid(place_ref, counts_ref, seqs, rows):
    count = counts_ref[0, place_ref[0] * seqs + place_ref[1]]
    return lax.broadcasted_iota(jnp.int32, (rows, 1), 0) < count


def normalised(matrix_rows):
    centre = matrix_rows - jnp.mean(matrix_rows, axis=-1, keepdims=True)
    inverse = lax.rsqrt(jnp.mean(centre * centre, axis=-1, keepdims=True) + EPSILON)
    return centre * inverse, inverse


def norm_back(upstream, unit_rows, inverse, gain_row):
    scaled = upstream * gain_row
    return inverse * (
        scaled
        - jnp.mean(scaled, axis=-1, keepdims=True)
        - unit_rows * jnp.mean(scaled * unit_rows, axis=-1, keepdims=True)
    )


def row_of(ref, index):
    return ref[...].astype(F32)[index : index + 1]


def fetches(pieces, own, first, size, target, sems):
    return [
        pltpu.make_async_copy(
            piece.at[pl.ds(first, size)],
            target.at[pl.ds(pl.multiple_of((own ^ j) * size, 16), size)],
            sems.at[j],
        )
        for j, piece in enumerate(pieces)
    ]


def prepare_kernel(
    seqs,
    place_ref,
    counts_ref,
    grad_ref,
    w_out_ref,
    outcome_ref,
    out_ref,
):
    out_ref[...] = w_out_ref[...]
    valid = own_rows_valid(place_ref, counts_ref, seqs, grad_ref.shape[0])
    outcome_ref[...] = jnp.where(valid, grad_ref[...], 0.0).astype(BF)


def columns_kernel(seqs, place_ref, qkv_ref, mine_ref):
    width = qkv_ref.shape[1] // 3
    size = width // seqs
    for part in range(3):
        chosen = qkv_ref[:, part * width : part * width + size]
        for k in range(1, seqs):
            first = part * width + k * size
            chosen = jnp.where(place_ref[1] == k, qkv_ref[:, first : first + size], chosen)
        mine_ref[:, part * size : (part + 1) * size] = chosen


def first_norm_kernel(tokens_ref, gain_ref, shift_ref, normed_ref):
    unit = normalised(tokens_ref[...])[0]
    normed_ref[...] = (unit * row_of(gain_ref, 0) + row_of(shift_ref, 0)).astype(BF)


def pack_kernel(owners, blocks, parts, place_ref, up_ref, down_ref, out_ref, sems):
    rows, width = up_ref.shape[0], down_ref.shape[1]
    size = down_ref.shape[0] // blocks
    copies = []
    for i in range(owners):
        first = pl.multiple_of((i * blocks + place_ref[0]) * size, 128)
        part, column = divmod(i * size, width)
        copies.append((up_ref.at[:, pl.ds(first, size)],
                       out_ref.at[pl.ds(part * rows, rows), pl.ds(column, size)]))
    first = pl.multiple_of(place_ref[0] * size, 16)
    copies.append((down_ref.at[pl.ds(first, size)], out_ref.at[pl.ds(parts * rows, size)]))
    copies = [
        pltpu.make_async_copy(source, target, sems.at[i])
        for i, (source, target) in enumerate(copies)
    ]
    for copy in copies:
        copy.start()
    for copy in copies:
        copy.wait()


def qkv_kernel(owners, seqs, place_ref, *refs):
    pieces, normed_refs, refs = refs[:owners], refs[owners : owners + seqs], refs[owners + seqs :]
    shift_ref, kv_ref, q_ref, w_ref, sems = refs
    own_rows, size = pieces[0].shape[0], q_ref.shape[1]
    copies = fetches(pieces, place_ref[2], 0, own_rows, w_ref, sems)
    for copy in copies:
        copy.start()
    normed = jnp.concatenate([ref[...] for ref in normed_refs])
    for copy in copies:
        copy.wait()
    result = (dot_nn(normed, w_ref[...]) + shift_ref[...]).astype(BF)
    q_ref[...] = result[:, :size]
    kv_ref[...] = result[:, size:]


def attend_kernel(blocks, heads, pieces, slot_rows, place_ref, counts_ref, q_ref, *refs):
    kv_refs, out_refs, log_ref = refs[:blocks], refs[blocks:-1], refs[-1]
    width = heads * HD
    biases = [piece_bias(place_ref, counts_ref, m, pieces, slot_rows) for m in range(blocks)]
    for head in range(heads):
        low, high = head * HD, (head + 1) * HD
        query = q_ref[:, low:high] * SCALE
        scores = [dot_nt(kv[:, low:high], query) + bias for kv, bias in zip(kv_refs, biases)]
        top = functools.reduce(
            jnp.maximum, [jnp.max(block, axis=0, keepdims=True) for block in scores]
        )
        powers = [jnp.exp(block - top) for block in scores]
        total = sum(jnp.sum(block, axis=0, keepdims=True) for block in powers)
        inverse = 1.0 / total
        result = sum(
            dot_tn((block * inverse).astype(BF), kv[:, width + low : width + high])
            for block, kv in zip(powers, kv_refs)
        ).astype(BF)
        for k, out_ref in enumerate(out_refs):
            out_ref[:, low:high] = result[k * slot_rows : (k + 1) * slot_rows]
        log_ref[head : head + 1, :] = top + jnp.log(total)


def attend_back_kernel(blocks, heads, pieces, slot_rows, place_ref, counts_ref, q_ref, log_ref, *refs):
    d_refs, refs = refs[:pieces], refs[pieces:]
    kv_refs, dq_ref, dkv_refs = refs[:blocks], refs[blocks], refs[blocks + 1 :]
    width = heads * HD
    biases = [piece_bias(place_ref, counts_ref, m, pieces, slot_rows) for m in range(blocks)]
    for head in range(heads):
        low, high = head * HD, (head + 1) * HD
        query = q_ref[:, low:high] * SCALE
        d_out = jnp.concatenate([d_ref[:, low:high] for d_ref in d_refs])
        log_row = log_ref[head : head + 1, :]
        softs, d_softs, delta = [], [], 0.0
        for kv, bias in zip(kv_refs, biases):
            soft = jnp.exp(dot_nt(kv[:, low:high], query) + bias - log_row)
            d_soft = dot_nt(kv[:, width + low : width + high], d_out)
            delta = delta + jnp.sum(soft * d_soft, axis=0, keepdims=True)
            softs.append(soft)
            d_softs.append(d_soft)
        d_query = 0.0
        for kv, dkv, soft, d_soft in zip(kv_refs, dkv_refs, softs, d_softs):
            d_scores = (soft * (d_soft - delta)).astype(BF)
            d_query = d_query + dot_tn(d_scores, kv[:, low:high])
            dkv[:, low:high] = dot_nn(d_scores, query).astype(dkv.dtype)
            dkv[:, width + low : width + high] = dot_nn(soft.astype(BF), d_out).astype(dkv.dtype)
        dq_ref[:, low:high] = (d_query * SCALE).astype(BF)


def project_kernel(owners, seqs, place_ref, *refs):
    pieces, att_refs = refs[:owners], refs[owners : owners + seqs]
    tokens_ref, vec_ref, gain_ref, shift_ref, middle_ref, normed_ref, w_ref, sems = refs[owners + seqs :]
    own_rows, head_width = w_ref.shape[0] // owners, w_ref.shape[0] // seqs
    copies = fetches(pieces, place_ref[2], 0, own_rows, w_ref, sems)
    for copy in copies:
        copy.start()
    middle = tokens_ref[...] + row_of(vec_ref, 2)
    for copy in copies:
        copy.wait()
    for k, att_ref in enumerate(att_refs):
        first = pl.multiple_of((place_ref[1] ^ k) * head_width, 16)
        middle = middle + dot_nn(att_ref[...], w_ref[pl.ds(first, head_width), :])
    middle_ref[...] = middle
    unit = normalised(middle)[0]
    normed_ref[...] = (unit * row_of(gain_ref, 1) + row_of(shift_ref, 1)).astype(BF)


def hidden_kernel(owners, blocks, own_rows, hidden_rows, place_ref, *refs):
    pieces, refs = refs[:owners], refs[owners:]
    normed_refs, outcome_refs, refs = refs[:blocks], refs[blocks : 2 * blocks], refs[2 * blocks :]
    shift_ref, hidden_ref, d_up_ref, sums_ref = refs[:4]
    d_normed_refs, out_refs = refs[4 : 4 + blocks], refs[4 + blocks : 4 + 2 * blocks]
    up_ref, down_ref, sems = refs[4 + 2 * blocks :]
    parts, width = up_ref.shape[0], up_ref.shape[1]
    own = place_ref[2]
    waits = []
    for part in range(parts):
        waits += fetches(
            pieces, own, part * own_rows, own_rows, up_ref.at[part], sems.at[part]
        )
    waits += fetches(pieces, own, parts * own_rows, hidden_rows, down_ref, sems.at[parts])
    for copy in waits:
        copy.start()
    normed = jnp.concatenate([ref[...] for ref in normed_refs])
    outcome = jnp.concatenate([ref[...] for ref in outcome_refs])
    for copy in waits:
        copy.wait()
    size = min(384, parts * width)
    d_normed, result = 0.0, 0.0
    for first in range(0, parts * width, size):
        part, column = first // width, first % width
        up_weights = up_ref[part, :, column : column + size]
        down_weights = down_ref[first : first + size, :]
        up_proj = dot_nn(normed, up_weights) + shift_ref[:, first : first + size]
        chance = 0.5 * (1.0 + lax.erf(up_proj * (0.5**0.5)))
        hidden = (up_proj * chance).astype(BF)
        slope = chance + up_proj * (jnp.exp(-0.5 * up_proj * up_proj) * 0.3989422804014327)
        d_up = (dot_nt(outcome, down_weights) * slope).astype(BF)
        hidden_ref[:, first : first + size] = hidden
        d_up_ref[:, first : first + size] = d_up
        sums_ref[:, first : first + size] = jnp.sum(d_up.astype(F32), axis=0, keepdims=True)
        d_normed = d_normed + dot_nt(d_up, up_weights)
        result = result + dot_nn(hidden, down_weights)
    rows = normed_refs[0].shape[0]
    for m in range(blocks):
        d_normed_refs[m][...] = d_normed[m * rows : (m + 1) * rows].astype(d_normed_refs[m].dtype)
        out_refs[m][...] = result[m * rows : (m + 1) * rows].astype(out_refs[m].dtype)


def middle_kernel(owners, seqs, blocks, place_ref, counts_ref, *refs):
    pieces, refs = refs[:owners], refs[owners:]
    d_normed_refs, refs = refs[:blocks], refs[blocks:]
    middle_in_ref, grad_ref, gain_ref, d_middle_ref, d_branch_ref, sums_ref = refs[:6]
    head_refs, (w_ref, sems) = refs[6 : 6 + seqs], refs[6 + seqs :]
    own_rows, head_width = w_ref.shape[0] // owners, w_ref.shape[0] // seqs
    copies = fetches(pieces, place_ref[2], 0, own_rows, w_ref, sems)
    for copy in copies:
        copy.start()
    valid = own_rows_valid(place_ref, counts_ref, seqs, grad_ref.shape[0])
    grad_rows = jnp.where(valid, grad_ref[...], 0.0)
    unit, inverse = normalised(middle_in_ref[...])
    upstream = sum(ref[...].astype(F32) for ref in d_normed_refs)
    d_middle = grad_rows + norm_back(upstream, unit, inverse, row_of(gain_ref, 1))
    d_branch = d_middle.astype(BF)
    d_middle_ref[...] = d_middle
    d_branch_ref[...] = d_branch
    for copy in copies:
        copy.wait()
    for k, head_ref in enumerate(head_refs):
        first = pl.multiple_of((place_ref[1] ^ k) * head_width, 16)
        head_ref[...] = dot_nt(d_branch, w_ref[pl.ds(first, head_width), :]).astype(BF)
    rows = (
        upstream * unit,
        upstream,
        d_branch.astype(F32),
        grad_rows.astype(BF).astype(F32),
    )
    for index, one in enumerate(rows):
        sums_ref[index : index + 1, :] = jnp.sum(one, axis=0, keepdims=True)


def grads_kernel(owners, seqs, blocks, own_rows, hidden_rows, place_ref, *refs):
    normed_refs, outcome_refs, refs = refs[:blocks], refs[blocks : 2 * blocks], refs[2 * blocks :]
    hidden_ref, d_up_ref, sent_ref, kept_ref = refs
    width = outcome_refs[0].shape[1]
    parts = d_up_ref.shape[1] // width
    bit = place_ref[2] & 1
    normed = jnp.concatenate([ref[...] for ref in normed_refs])
    outcome = jnp.concatenate([ref[...] for ref in outcome_refs])
    chunk, up_chunk = hidden_rows // seqs, own_rows // seqs
    for owner in range(owners):
        down = dot_tn(hidden_ref[:, owner * hidden_rows : (owner + 1) * hidden_rows], outcome)
        rows_in = normed[:, owner * own_rows : (owner + 1) * own_rows]
        ups = [
            dot_tn(rows_in, d_up_ref[:, part * width : (part + 1) * width]) for part in range(parts)
        ]

        def store(ref, owner=owner, down=down, ups=ups):
            for k in range(seqs):
                ref[owner // 2, k, 0:chunk, :] = down[k * chunk : (k + 1) * chunk].astype(BF)
                for part, up in enumerate(ups):
                    first = chunk + part * up_chunk
                    ref[owner // 2, k, first : first + up_chunk, :] = up[
                        k * up_chunk : (k + 1) * up_chunk
                    ].astype(BF)

        @pl.when(bit == owner % 2)
        def keep():
            store(kept_ref)

        @pl.when(bit != owner % 2)
        def send():
            store(sent_ref)


def step_kernel(bit, place_ref, kept_ref, arrived_ref, sent_ref, next_ref):
    high = (place_ref[2] // bit) & 1
    for i in range(sent_ref.shape[0]):
        for ref, index in ((sent_ref, 2 * i + 1 - high), (next_ref, 2 * i + high)):
            ref[i] = (kept_ref[index].astype(F32) + arrived_ref[index].astype(F32)).astype(BF)


def chunk_kernel(seqs, place_ref, kept_ref, arrived_ref, *out_refs):
    for j in range(seqs):
        index = place_ref[1] ^ j
        total = kept_ref[0, index].astype(F32) + arrived_ref[0, index].astype(F32)
        out_refs[j][...] = total.astype(BF)


def add_kernel(*refs):
    refs[-1][...] = sum(ref[...].astype(F32) for ref in refs[:-1]).astype(BF)


def out_chunks_kernel(blocks, seqs, place_ref, *refs):
    total = sum(ref[...].astype(F32) for ref in refs[:blocks])
    size = total.shape[1] // seqs
    for j in range(seqs):
        chosen = total[:, :size]
        for k in range(1, seqs):
            columns = total[:, k * size : (k + 1) * size]
            chosen = jnp.where(place_ref[1] ^ j == k, columns, chosen)
        refs[blocks + j][...] = chosen.astype(BF)


def join_kernel(blocks, seqs, *refs):
    in_refs, part_refs, out_ref = refs[:blocks], refs[blocks : blocks + seqs], refs[-1]
    terms = [ref[...].astype(F32) for ref in in_refs]
    while len(terms) > 1:
        terms = [terms[i] + terms[i + 1] for i in range(0, len(terms), 2)]
    out_ref[...] = terms[0].astype(BF)
    total = sum(ref[...].astype(F32) for ref in part_refs)
    size, columns = total.shape
    out_ref[0:size, 3 * columns :] = total.astype(BF)


def project_back_kernel(blocks, seqs, *refs):
    q_ref, kv_refs, w_ref, refs = refs[0], refs[1 : 1 + blocks], refs[1 + blocks], refs[2 + blocks :]
    normed_refs, (gain_ref, shift_ref), refs = refs[:seqs], refs[seqs : seqs + 2], refs[seqs + 2 :]
    projected_ref, columns_ref, sums_ref, part_refs = refs[0], refs[1], refs[2], refs[3:]
    d_kv = sum(ref[...].astype(F32) for ref in kv_refs).astype(BF)
    d_projected = jnp.concatenate([q_ref[...], d_kv], axis=1)
    projected_ref[...] = d_projected
    columns_ref[...] = jnp.sum(d_projected.astype(F32), axis=0, keepdims=True)
    rows = normed_refs[0].shape[0]
    gain, shift = row_of(gain_ref, 0), row_of(shift_ref, 0)
    with_normed, plain = 0.0, 0.0
    for k in range(seqs):
        part = dot_nt(d_projected[k * rows : (k + 1) * rows], w_ref[...])
        part_refs[k][...] = part.astype(BF)
        with_normed = with_normed + jnp.sum(
            part * (normed_refs[k][...].astype(F32) - shift), axis=0, keepdims=True
        )
        plain = plain + jnp.sum(part, axis=0, keepdims=True)
    sums_ref[0:1, :] = with_normed / gain
    sums_ref[1:2, :] = plain


def by_core(bit, owner, refs, store):
    sent_ref, kept_ref = refs

    @pl.when(bit == owner % 2)
    def keep():
        store(kept_ref)

    @pl.when(bit != owner % 2)
    def send():
        store(sent_ref)


def out_grads_kernel(owners, seqs, place_ref, *refs):
    att_refs, branch_ref, (sent_ref, kept_ref, att_ref) = refs[:seqs], refs[seqs], refs[seqs + 1 :]
    size = att_refs[0].shape[1]
    own_rows = branch_ref.shape[1] // owners
    for k in range(seqs):
        att_ref[place_ref[1] ^ k] = att_refs[k][...]
    for owner in range(owners):
        group, column = divmod(owner * own_rows, size)
        out = dot_tn(att_ref[group][:, column : column + own_rows], branch_ref[...]).astype(BF)

        def store(ref, owner=owner, out=out):
            ref[owner // 2] = out

        by_core(place_ref[2] & 1, owner, (sent_ref, kept_ref), store)


def last_grads_kernel(owners, seqs, blocks, place_ref, *refs):
    normed_refs, refs = refs[:seqs], refs[seqs:]
    (projected_ref, columns_ref, first_ref, middle_ref, up_ref, sent_ref, kept_ref) = refs
    width, third = first_ref.shape[1], projected_ref.shape[1]
    size = third // 3
    own_rows, hidden_rows = width // owners, up_ref.shape[1] // owners
    normed = jnp.concatenate([ref[...] for ref in normed_refs])
    projected = projected_ref[...]
    for owner in range(owners):
        first = owner * own_rows
        group, column = divmod(first, size)
        qkv = dot_tn(normed[:, first : first + own_rows], projected).astype(BF)
        is_group = place_ref[1] == group
        bias = [
            jnp.where(is_group, columns_ref[:, start : start + own_rows], 0.0)
            for start in (column, 2 * size + column)
        ]
        lines = [
            first_ref[0:1, first : first + own_rows],
            first_ref[1:2, first : first + own_rows],
            *bias,
        ] + [middle_ref[i : i + 1, first : first + own_rows] for i in range(4)]
        lines = jnp.concatenate(lines).astype(BF)
        up_line = up_ref[:, owner * hidden_rows : (owner + 1) * hidden_rows]
        up_line = jnp.concatenate(
            [jnp.where(place_ref[0] == b, up_line, 0.0) for b in range(blocks)], axis=1
        ).astype(BF)

        def store(ref, owner=owner, qkv=qkv, lines=lines, up_line=up_line):
            ref[owner // 2, 0:own_rows, 0:third] = qkv
            ref[owner // 2, 0:own_rows, third:] = jnp.zeros((own_rows, width - third), BF)
            ref[owner // 2, own_rows:, :] = jnp.zeros((16, width), BF)
            ref[owner // 2, own_rows : own_rows + 8, 0:own_rows] = lines
            ref[owner // 2, own_rows + 8 : own_rows + 9, 0 : up_line.shape[1]] = up_line

        by_core(place_ref[2] & 1, owner, (sent_ref, kept_ref), store)


def block_kernel(blocks, tail, place_ref, kept_ref, arrived_ref, *out_refs):
    total = kept_ref[0].astype(F32) + arrived_ref[0].astype(F32)
    own_rows = total.shape[0] - tail
    size = own_rows // blocks
    for m in range(blocks):
        chosen = total[:size]
        for j in range(1, blocks):
            chosen = jnp.where(place_ref[0] ^ m == j, total[j * size : (j + 1) * size], chosen)
        out_refs[m][0:size, :] = chosen.astype(BF)
        if tail:
            out_refs[m][size:, :] = total[own_rows:].astype(BF)


def first_back_kernel(pieces, *refs):
    part_refs, (tokens_ref, d_middle_ref, gain_ref, out_ref) = refs[:pieces], refs[pieces:]
    upstream = sum(ref[:, : out_ref.shape[1]].astype(F32) for ref in part_refs)
    unit, inverse = normalised(tokens_ref[...])
    out_ref[...] = d_middle_ref[...] + norm_back(upstream, unit, inverse, row_of(gain_ref, 0))


def place_kernel(seqs, blocks, layouts, place_ref, *refs):
    pieces = refs[: blocks * seqs]
    outs = refs[blocks * seqs : -2]
    held, sems = refs[-2:]
    blk, seq = place_ref[0], place_ref[1]
    copies = [
        pltpu.make_async_copy(
            pieces[m * seqs + k],
            held.at[jnp.bitwise_xor(blk, m), jnp.bitwise_xor(seq, k)],
            sems.at[m * seqs + k],
        )
        for m in range(blocks)
        for k in range(seqs)
    ]
    for copy in copies:
        copy.start()
    for copy in copies:
        copy.wait()
    for out, spots in zip(outs, layouts):
        for b in range(blocks):
            for k in range(seqs):
                for top, rows, first, size, row, column in spots(b, k):
                    piece = held[b, k, top : top + rows, first : first + size]
                    out[row : row + rows, column : column + size] = piece.astype(F32)


def run(kernel, label, outs, scalars, remote, arrays, scratch=(), waits=(), in_hbm=False, cost=1.0, mib=10):
    inputs = len(scalars) + len(remote) + len(arrays)

    def without_waits(*refs):
        kernel(*refs[:inputs], *refs[inputs + len(waits) :])

    return pl.pallas_call(
        without_waits,
        out_shape=tuple(outs),
        in_specs=[pl.BlockSpec(memory_space=pltpu.SMEM)] * len(scalars)
        + [pl.BlockSpec(memory_space=pl.ANY)] * len(remote)
        + [pl.BlockSpec(memory_space=pltpu.VMEM)] * len(arrays)
        + [pl.BlockSpec(memory_space=pl.ANY)] * len(waits),
        out_specs=(pl.BlockSpec(memory_space=pl.ANY if in_hbm else pltpu.VMEM),) * len(outs),
        scratch_shapes=list(scratch),
        compiler_params=pltpu.CompilerParams(vmem_limit_bytes=mib * 1024 * 1024),
        cost_estimate=pl.CostEstimate(
            flops=1, bytes_accessed=int(cost * 1.2e6), transcendentals=0
        ),
        name=label,
    )(*scalars, *remote, *arrays, *waits)


def shape(dims, kind):
    return jax.ShapeDtypeStruct(tuple(dims), kind)


def gate(array, waits):
    def nothing(*refs):
        pass

    return pl.pallas_call(
        nothing,
        out_shape=shape(array.shape, array.dtype),
        in_specs=[pl.BlockSpec(memory_space=pl.ANY)] * (1 + len(waits)),
        out_specs=pl.BlockSpec(memory_space=pl.ANY),
        input_output_aliases={0: 0},
        cost_estimate=pl.CostEstimate(flops=1, bytes_accessed=1, transcendentals=0),
        name="gate",
    )(array, *waits)


def owner_sums(kept, arrived, place, label, waits=()):
    sent, bit = None, 2
    while bit < lax.axis_size("fsdp"):
        half = (kept.shape[0] // 2, *kept.shape[1:])
        sent, kept = run(
            functools.partial(step_kernel, bit),
            label,
            [shape(half, BF)] * 2,
            [place],
            [],
            [kept, arrived],
            waits=waits,
            mib=14,
        )
        arrived = swap(sent, "fsdp", bit)
        bit *= 2
    return kept, arrived, sent


def sum_parts(parts, axis):
    return [parts[0]] + [swap(parts[j], axis, j) for j in range(1, len(parts))]


def tree_sum(pieces):
    pieces = [piece.astype(F32) for piece in pieces]
    while len(pieces) > 1:
        pieces = [pieces[i] + pieces[i + 1] for i in range(0, len(pieces), 2)]
    return pieces[0]


def shards(
    tokens, counts, norm_gain, norm_bias, vec_bias, up_bias, w_qkv, w_out, w_up, w_down, grad_out
):
    owners, blocks, seqs = (lax.axis_size(name) for name in ("fsdp", "blk", "seq"))
    own, blk, seq = (lax.axis_index(name) for name in ("fsdp", "blk", "seq"))
    place = jnp.stack([blk, seq, own]).astype(jnp.int32)
    rows, width = tokens.shape[1:]
    head_width = width // seqs
    heads, third = head_width // HD, 3 * head_width
    own_rows = width // owners
    hidden_rows = w_down.shape[0] // blocks
    hidden_width = hidden_rows * owners
    parts = hidden_width // width
    block_rows, all_rows = seqs * rows, blocks * rows
    inputs, grad_in = tokens[0], grad_out[0]
    vmem, dma = pltpu.VMEM, pltpu.SemaphoreType.DMA

    (normed1,) = run(
        first_norm_kernel,
        "first_norm",
        [shape((rows, width), BF)],
        [],
        [],
        [inputs, norm_gain, norm_bias],
    )
    normed1_pieces = from_all(normed1, "seq")
    (qkv_mine,) = run(
        functools.partial(columns_kernel, seqs),
        "columns",
        [shape((own_rows, third), BF)],
        [place],
        [],
        [w_qkv],
        waits=[normed1],
    )
    qkv_pieces = doubled(qkv_mine, "fsdp")
    d_outcome, out_mine = run(
        functools.partial(prepare_kernel, seqs),
        "prepare",
        [shape((rows, width), BF), shape((own_rows, width), BF)],
        [place, counts],
        [],
        [grad_in, w_out],
        waits=[qkv_pieces[owners // 2]],
    )
    out_pieces = doubled(out_mine, "fsdp")
    outcome_pieces = from_all(d_outcome, "blk")

    biases = vec_bias.astype(F32)
    qkv_shift = jnp.concatenate(
        [
            lax.dynamic_slice_in_dim(biases[0], seq * head_width, head_width),
            jnp.zeros((head_width,), F32),
            lax.dynamic_slice_in_dim(biases[1], seq * head_width, head_width),
        ]
    ).reshape(1, third)
    up_shift = (
        lax.dynamic_index_in_dim(up_bias.reshape(owners, blocks, hidden_rows), blk, 1, False)
        .astype(F32)
        .reshape(1, hidden_width)
    )

    key_value, queries, qkv_full = run(
        functools.partial(qkv_kernel, owners, seqs),
        "project_in",
        [
            shape((block_rows, 2 * head_width), BF),
            shape((block_rows, head_width), BF),
            shape((width, third), BF),
        ],
        [place],
        qkv_pieces,
        [*normed1_pieces, qkv_shift],
        [dma((owners,))],
        waits=outcome_pieces[1:],
        mib=16,
    )
    packed = shape((parts * own_rows + hidden_rows, width), BF)
    if hidden_rows % 128 == 0:
        (weights_mine,) = run(
            functools.partial(pack_kernel, owners, blocks, parts),
            "pack",
            [packed],
            [place],
            [w_up, w_down],
            [],
            [dma((owners + 1,))],
            waits=[key_value, out_pieces[owners // 2]],
            in_hbm=True,
        )
    else:
        columns = [
            lax.dynamic_slice_in_dim(w_up, (i * blocks + blk) * hidden_rows, hidden_rows, axis=1)
            for i in range(owners)
        ]
        in_part = owners // parts
        weights_mine = jnp.concatenate(
            [
                jnp.concatenate(columns[part * in_part : (part + 1) * in_part], axis=1)
                for part in range(parts)
            ]
            + [lax.dynamic_slice_in_dim(w_down, blk * hidden_rows, hidden_rows, axis=0)]
        )

    kv_blocks = from_all(key_value, "blk")
    *att_out, log_total = run(
        functools.partial(attend_kernel, blocks, heads, seqs, rows),
        "attend",
        [shape((rows, head_width), BF)] * seqs + [shape((heads, block_rows), F32)],
        [place, counts],
        [],
        [queries, *kv_blocks],
        waits=out_pieces[1:],
        cost=1.3,
        mib=20,
    )
    att_pieces = sum_parts(att_out, "seq")
    weights = doubled(weights_mine, "fsdp", att_pieces[1:])
    middle, normed2 = run(
        functools.partial(project_kernel, owners, seqs),
        "project_out",
        [shape((rows, width), F32), shape((rows, width), BF)],
        [place],
        out_pieces,
        [*att_pieces, inputs, vec_bias, norm_gain, norm_bias],
        [vmem((width, width), BF), dma((owners,))],
        mib=12,
    )

    normed_pieces = from_all(normed2, "blk")
    row_shapes = [shape((rows, width), F32)] + [shape((rows, width), BF)] * (blocks - 1)
    hidden, d_up, up_sums, *rest = run(
        functools.partial(hidden_kernel, owners, blocks, own_rows, hidden_rows),
        "hidden",
        [shape((all_rows, hidden_width), BF)] * 2
        + [shape((1, hidden_width), F32)]
        + row_shapes * 2,
        [place],
        weights,
        [*normed_pieces, *outcome_pieces, up_shift],
        [
            vmem((parts, width, width), BF),
            vmem((hidden_width, width), BF),
            dma((parts + 1, owners)),
        ],
        cost=2.3,
        mib=24,
    )
    d_normed_pieces = sum_parts(rest[:blocks], "blk")
    chunk, up_chunk = hidden_rows // seqs, own_rows // seqs
    chunk_rows = chunk + parts * up_chunk
    sent, kept = run(
        functools.partial(grads_kernel, owners, seqs, blocks, own_rows, hidden_rows),
        "feed_grads",
        [shape((owners // 2, seqs, chunk_rows, width), BF)] * 2,
        [place],
        [],
        [*normed_pieces, *outcome_pieces, hidden, d_up],
        cost=1.3,
        mib=24,
    )
    d_middle, d_branch, middle_sums, *d_heads = run(
        functools.partial(middle_kernel, owners, seqs, blocks),
        "middle",
        [shape((rows, width), F32), shape((rows, width), BF), shape((4, width), F32)]
        + [shape((rows, head_width), BF)] * seqs,
        [place, counts],
        out_pieces,
        [*d_normed_pieces, middle, grad_in, norm_gain],
        [vmem((width, width), BF), dma((owners,))],
        waits=[sent],
        mib=12,
    )
    d_att_pieces = sum_parts(d_heads, "seq")
    result_pieces = sum_parts(rest[blocks:], "blk")
    d_query, *d_kv = run(
        functools.partial(attend_back_kernel, blocks, heads, seqs, rows),
        "attend_back",
        [shape((block_rows, head_width), BF), shape((block_rows, 2 * head_width), F32)]
        + [shape((block_rows, 2 * head_width), BF)] * (blocks - 1),
        [place, counts],
        [],
        [queries, log_total, *d_att_pieces, *kv_blocks],
        cost=1.9,
        mib=28,
    )
    kept, arrived, feed_sent = owner_sums(
        kept, swap(gate(sent, d_att_pieces[1:]), "fsdp", 1), place, "feed_step", waits=[d_query]
    )
    out_sent, out_kept = run(
        functools.partial(out_grads_kernel, owners, seqs),
        "out_grads",
        [shape((owners // 2, own_rows, width), BF)] * 2,
        [place],
        [],
        [*att_pieces, d_branch],
        [vmem((seqs, rows, head_width), BF)],
        waits=[feed_sent],
        mib=12,
    )
    blk_rows = own_rows // blocks
    d_projected, column_sums, first_sums, *d_normed1 = run(
        functools.partial(project_back_kernel, blocks, seqs),
        "project_back",
        [
            shape((block_rows, third), BF),
            shape((1, third), F32),
            shape((2, width), F32),
        ]
        + [shape((rows, width), BF)] * seqs,
        [],
        [],
        [d_query, *sum_parts(d_kv, "blk"), qkv_full, *normed1_pieces, norm_gain, norm_bias],
        waits=[feed_sent, out_sent],
        mib=16,
    )
    out_kept, out_arrived, out_step = owner_sums(
        out_kept, swap(gate(out_sent, [column_sums]), "fsdp", 1), place, "out_step"
    )
    d_normed1_pieces = sum_parts(d_normed1, "seq")
    (grad_tokens,) = run(
        functools.partial(first_back_kernel, seqs),
        "first_back",
        [shape((rows, width), F32)],
        [],
        [],
        [*d_normed1_pieces, inputs, d_middle, norm_gain],
    )

    out_blocks = run(
        functools.partial(block_kernel, blocks, 0),
        "out_blocks",
        [shape((blk_rows, width), BF)] * blocks,
        [place],
        [],
        [out_kept, out_arrived],
        waits=[grad_tokens],
    )
    feed_chunks = run(
        functools.partial(chunk_kernel, seqs),
        "feed_chunks",
        [shape((chunk_rows, width), BF)] * seqs,
        [place],
        [],
        [kept, arrived],
        waits=[grad_tokens],
        mib=12,
    )

    sent, last_kept = run(
        functools.partial(last_grads_kernel, owners, seqs, blocks),
        "last_grads",
        [shape((owners // 2, own_rows + 16, width), BF)] * 2,
        [place],
        [],
        [*normed1_pieces, d_projected, column_sums, first_sums, middle_sums, up_sums],
        waits=[out_step],
        mib=16,
    )
    last_kept, last_arrived, _ = owner_sums(
        last_kept, swap(sent, "fsdp", 1), place, "last_step"
    )
    last_blocks = run(
        functools.partial(block_kernel, blocks, 16),
        "last_blocks",
        [shape((blk_rows + 16, width), BF)] * blocks,
        [place],
        [],
        [last_kept, last_arrived],
    )
    out_chunks = run(
        functools.partial(out_chunks_kernel, blocks, seqs),
        "out_chunks",
        [shape((blk_rows, head_width), BF)] * seqs,
        [place],
        [],
        sum_parts(out_blocks, "blk"),
    )
    (last_sums,) = run(
        functools.partial(join_kernel, blocks, seqs),
        "last_sums",
        [shape((blk_rows + 16, width), BF)],
        [],
        [],
        [*sum_parts(last_blocks, "blk"), *sum_parts(out_chunks, "seq")],
    )
    (feed_sums,) = run(
        add_kernel,
        "feed_sums",
        [shape((chunk_rows, width), BF)],
        [],
        [],
        sum_parts(feed_chunks, "seq"),
        waits=[last_sums, *result_pieces[1:]],
    )
    feed_seq = from_all(feed_sums, "seq")
    last_seq = from_all(gate(last_sums, [feed_seq[1]]), "seq")
    outcome = sum(one.astype(F32) for one in result_pieces)
    valid = lax.broadcasted_iota(jnp.int32, (rows, 1), 0) < counts[0, blk * seqs + seq]
    activations = jnp.where(valid, middle + outcome + biases[3], 0.0)

    feed_all = [from_all(one, "blk") for one in feed_seq]
    last_all = [from_all(one, "blk") for one in last_seq]
    grad_down, grad_up = run(
        functools.partial(
            place_kernel,
            seqs,
            blocks,
            [
                lambda b, k: [(0, chunk, 0, width, b * hidden_rows + k * chunk, 0)],
                lambda b, k: [
                    (
                        chunk + (i * hidden_rows // width) * up_chunk,
                        up_chunk,
                        i * hidden_rows % width,
                        hidden_rows,
                        k * up_chunk,
                        (i * blocks + b) * hidden_rows,
                    )
                    for i in range(owners)
                ],
            ],
        ),
        "place_feed",
        [shape((blocks * hidden_rows, width), F32), shape((own_rows, blocks * hidden_width), F32)],
        [place],
        [feed_all[k][m] for m in range(blocks) for k in range(seqs)],
        [],
        [vmem((blocks, seqs, chunk_rows, width), BF), dma((blocks * seqs,))],
        waits=last_seq[1:],
        mib=24,
    )
    grad_qkv, grad_w_out = run(
        functools.partial(
            place_kernel,
            seqs,
            blocks,
            [
                lambda b, k: [
                    (
                        0,
                        blk_rows,
                        i * head_width,
                        head_width,
                        b * blk_rows,
                        i * width + k * head_width,
                    )
                    for i in range(3)
                ],
                lambda b, k: [(0, blk_rows, third, head_width, b * blk_rows, k * head_width)],
            ],
        ),
        "place_last",
        [shape((own_rows, 3 * width), F32), shape((own_rows, width), F32)],
        [place],
        [last_all[k][m] for m in range(blocks) for k in range(seqs)],
        [],
        [vmem((blocks, seqs, blk_rows + 16, width), BF), dma((blocks * seqs,))],
        waits=[grad_down],
        mib=20,
    )
    small = tree_sum([one[blk_rows:] for one in last_seq])
    lines = small[:8, :own_rows]
    return (
        activations[None],
        grad_tokens[None],
        jnp.stack([lines[0], lines[4]]),
        jnp.stack([lines[1], lines[5]]),
        jnp.stack([lines[2], lines[3], lines[6], lines[7]]),
        small[8, : blocks * hidden_rows],
        grad_qkv,
        grad_w_out,
        grad_up,
        grad_down,
    )


def solution(mesh):
    rows = P("fsdp", ("blk", "seq"), None)
    split = P("fsdp", None)
    return jax.shard_map(
        shards,
        mesh=mesh,
        in_specs=(rows, split, P(), P(), P(), P(), split, split, split, split, rows),
        out_specs=(
            rows,
            rows,
            P(None, "fsdp"),
            P(None, "fsdp"),
            P(None, "fsdp"),
            P("fsdp"),
            split,
            split,
            split,
            split,
        ),
        check_vma=False,
    )
```

```python
import functools

import jax
import jax.numpy as jnp
from jax import lax
from jax.experimental import pallas as pl
from jax.experimental.pallas import tpu as pltpu
from jax.sharding import PartitionSpec as P

HD = 64
EPSILON = 1e-06
MASKED = -1e30
SCALE = HD ** (-0.5)
BF = jnp.bfloat16
F32 = jnp.float32


def dot_nn(left_side, right_side):
    return lax.dot_general(
        left_side, right_side, (((1,), (0,)), ((), ())), preferred_element_type=F32
    )


def dot_nt(left_side, right_side):
    return lax.dot_general(
        left_side, right_side, (((1,), (1,)), ((), ())), preferred_element_type=F32
    )


def dot_tn(left_side, right_side):
    return lax.dot_general(
        left_side, right_side, (((0,), (0,)), ((), ())), preferred_element_type=F32
    )


def swap(array, axis, bits):
    return lax.ppermute(array, axis, [(i, i ^ bits) for i in range(lax.axis_size(axis))])


def from_all(array, axis):
    return [array] + [swap(array, axis, j) for j in range(1, lax.axis_size(axis))]


def doubled(array, axis, waits=()):
    pieces = {0: array}
    bit = lax.axis_size(axis) // 2
    while bit:
        pieces.update({j | bit: swap(piece, axis, bit) for j, piece in list(pieces.items())})
        if waits and bit == lax.axis_size(axis) // 2:
            pieces[bit] = gate(pieces[bit], waits)
        bit //= 2
    return [pieces[j] for j in range(lax.axis_size(axis))]


def piece_bias(place_ref, counts_ref, block, pieces, slot_rows):
    row = lax.broadcasted_iota(jnp.int32, (pieces * slot_rows, 1), 0)
    limit = jnp.zeros_like(row)
    for piece in range(pieces):
        held = (place_ref[0] ^ block) * pieces + (place_ref[1] ^ piece)
        end = counts_ref[0, held] + piece * slot_rows
        limit = jnp.where(row >= piece * slot_rows, end, limit)
    return jnp.where(row < limit, 0.0, MASKED)


def own_rows_valid(place_ref, counts_ref, seqs, rows):
    count = counts_ref[0, place_ref[0] * seqs + place_ref[1]]
    return lax.broadcasted_iota(jnp.int32, (rows, 1), 0) < count


def normalised(matrix_rows):
    centre = matrix_rows - jnp.mean(matrix_rows, axis=-1, keepdims=True)
    inverse = lax.rsqrt(jnp.mean(centre * centre, axis=-1, keepdims=True) + EPSILON)
    return centre * inverse, inverse


def norm_back(upstream, unit_rows, inverse, gain_row):
    scaled = upstream * gain_row
    return inverse * (
        scaled
        - jnp.mean(scaled, axis=-1, keepdims=True)
        - unit_rows * jnp.mean(scaled * unit_rows, axis=-1, keepdims=True)
    )


def row_of(ref, index):
    return ref[...].astype(F32)[index : index + 1]


def fetches(pieces, own, first, size, target, sems):
    return [
        pltpu.make_async_copy(
            piece.at[pl.ds(first, size)],
            target.at[pl.ds(pl.multiple_of((own ^ j) * size, 16), size)],
            sems.at[j],
        )
        for j, piece in enumerate(pieces)
    ]


def prepare_kernel(
    seqs,
    place_ref,
    counts_ref,
    grad_ref,
    w_out_ref,
    outcome_ref,
    out_ref,
):
    out_ref[...] = w_out_ref[...]
    valid = own_rows_valid(place_ref, counts_ref, seqs, grad_ref.shape[0])
    outcome_ref[...] = jnp.where(valid, grad_ref[...], 0.0).astype(BF)


def columns_kernel(seqs, place_ref, qkv_ref, mine_ref):
    width = qkv_ref.shape[1] // 3
    size = width // seqs
    for part in range(3):
        chosen = qkv_ref[:, part * width : part * width + size]
        for k in range(1, seqs):
            first = part * width + k * size
            chosen = jnp.where(place_ref[1] == k, qkv_ref[:, first : first + size], chosen)
        mine_ref[:, part * size : (part + 1) * size] = chosen


def first_norm_kernel(tokens_ref, gain_ref, shift_ref, normed_ref):
    unit = normalised(tokens_ref[...])[0]
    normed_ref[...] = (unit * row_of(gain_ref, 0) + row_of(shift_ref, 0)).astype(BF)


def pack_kernel(owners, blocks, parts, place_ref, up_ref, down_ref, out_ref, sems):
    rows, width = up_ref.shape[0], down_ref.shape[1]
    size = down_ref.shape[0] // blocks
    copies = []
    for i in range(owners):
        first = pl.multiple_of((i * blocks + place_ref[0]) * size, 128)
        part, column = divmod(i * size, width)
        copies.append((up_ref.at[:, pl.ds(first, size)],
                       out_ref.at[pl.ds(part * rows, rows), pl.ds(column, size)]))
    first = pl.multiple_of(place_ref[0] * size, 16)
    copies.append((down_ref.at[pl.ds(first, size)], out_ref.at[pl.ds(parts * rows, size)]))
    copies = [
        pltpu.make_async_copy(source, target, sems.at[i])
        for i, (source, target) in enumerate(copies)
    ]
    for copy in copies:
        copy.start()
    for copy in copies:
        copy.wait()


def qkv_kernel(owners, seqs, place_ref, *refs):
    pieces, normed_refs, refs = refs[:owners], refs[owners : owners + seqs], refs[owners + seqs :]
    shift_ref, kv_ref, q_ref, w_ref, sems = refs
    own_rows, size = pieces[0].shape[0], q_ref.shape[1]
    copies = fetches(pieces, place_ref[2], 0, own_rows, w_ref, sems)
    for copy in copies:
        copy.start()
    normed = jnp.concatenate([ref[...] for ref in normed_refs])
    for copy in copies:
        copy.wait()
    result = (dot_nn(normed, w_ref[...]) + shift_ref[...]).astype(BF)
    q_ref[...] = result[:, :size]
    kv_ref[...] = result[:, size:]


def attend_kernel(blocks, heads, pieces, slot_rows, place_ref, counts_ref, q_ref, *refs):
    kv_refs, out_refs, log_ref = refs[:blocks], refs[blocks:-1], refs[-1]
    width = heads * HD
    biases = [piece_bias(place_ref, counts_ref, m, pieces, slot_rows) for m in range(blocks)]
    for head in range(heads):
        low, high = head * HD, (head + 1) * HD
        query = q_ref[:, low:high] * SCALE
        scores = [dot_nt(kv[:, low:high], query) + bias for kv, bias in zip(kv_refs, biases)]
        top = functools.reduce(
            jnp.maximum, [jnp.max(block, axis=0, keepdims=True) for block in scores]
        )
        powers = [jnp.exp(block - top) for block in scores]
        total = sum(jnp.sum(block, axis=0, keepdims=True) for block in powers)
        inverse = 1.0 / total
        result = sum(
            dot_tn((block * inverse).astype(BF), kv[:, width + low : width + high])
            for block, kv in zip(powers, kv_refs)
        ).astype(BF)
        for k, out_ref in enumerate(out_refs):
            out_ref[:, low:high] = result[k * slot_rows : (k + 1) * slot_rows]
        log_ref[head : head + 1, :] = top + jnp.log(total)


def attend_back_kernel(blocks, heads, pieces, slot_rows, place_ref, counts_ref, q_ref, log_ref, *refs):
    d_refs, refs = refs[:pieces], refs[pieces:]
    kv_refs, dq_ref, dkv_refs = refs[:blocks], refs[blocks], refs[blocks + 1 :]
    width = heads * HD
    biases = [piece_bias(place_ref, counts_ref, m, pieces, slot_rows) for m in range(blocks)]
    for head in range(heads):
        low, high = head * HD, (head + 1) * HD
        query = q_ref[:, low:high] * SCALE
        d_out = jnp.concatenate([d_ref[:, low:high] for d_ref in d_refs])
        log_row = log_ref[head : head + 1, :]
        softs, d_softs, delta = [], [], 0.0
        for kv, bias in zip(kv_refs, biases):
            soft = jnp.exp(dot_nt(kv[:, low:high], query) + bias - log_row)
            d_soft = dot_nt(kv[:, width + low : width + high], d_out)
            delta = delta + jnp.sum(soft * d_soft, axis=0, keepdims=True)
            softs.append(soft)
            d_softs.append(d_soft)
        d_query = 0.0
        for kv, dkv, soft, d_soft in zip(kv_refs, dkv_refs, softs, d_softs):
            d_scores = (soft * (d_soft - delta)).astype(BF)
            d_query = d_query + dot_tn(d_scores, kv[:, low:high])
            dkv[:, low:high] = dot_nn(d_scores, query).astype(dkv.dtype)
            dkv[:, width + low : width + high] = dot_nn(soft.astype(BF), d_out).astype(dkv.dtype)
        dq_ref[:, low:high] = (d_query * SCALE).astype(BF)


def project_kernel(owners, seqs, place_ref, *refs):
    pieces, att_refs = refs[:owners], refs[owners : owners + seqs]
    tokens_ref, vec_ref, gain_ref, shift_ref, middle_ref, normed_ref, w_ref, sems = refs[owners + seqs :]
    own_rows, head_width = w_ref.shape[0] // owners, w_ref.shape[0] // seqs
    copies = fetches(pieces, place_ref[2], 0, own_rows, w_ref, sems)
    for copy in copies:
        copy.start()
    middle = tokens_ref[...] + row_of(vec_ref, 2)
    for copy in copies:
        copy.wait()
    for k, att_ref in enumerate(att_refs):
        first = pl.multiple_of((place_ref[1] ^ k) * head_width, 16)
        middle = middle + dot_nn(att_ref[...], w_ref[pl.ds(first, head_width), :])
    middle_ref[...] = middle
    unit = normalised(middle)[0]
    normed_ref[...] = (unit * row_of(gain_ref, 1) + row_of(shift_ref, 1)).astype(BF)


def hidden_kernel(owners, blocks, own_rows, hidden_rows, place_ref, *refs):
    pieces, refs = refs[:owners], refs[owners:]
    normed_refs, outcome_refs, refs = refs[:blocks], refs[blocks : 2 * blocks], refs[2 * blocks :]
    shift_ref, hidden_ref, d_up_ref, sums_ref = refs[:4]
    d_normed_refs, out_refs = refs[4 : 4 + blocks], refs[4 + blocks : 4 + 2 * blocks]
    up_ref, down_ref, sems = refs[4 + 2 * blocks :]
    parts, width = up_ref.shape[0], up_ref.shape[1]
    own = place_ref[2]
    waits = []
    for part in range(parts):
        waits += fetches(
            pieces, own, part * own_rows, own_rows, up_ref.at[part], sems.at[part]
        )
    waits += fetches(pieces, own, parts * own_rows, hidden_rows, down_ref, sems.at[parts])
    for copy in waits:
        copy.start()
    normed = jnp.concatenate([ref[...] for ref in normed_refs])
    outcome = jnp.concatenate([ref[...] for ref in outcome_refs])
    for copy in waits:
        copy.wait()
    size = min(384, parts * width)
    d_normed, result = 0.0, 0.0
    for first in range(0, parts * width, size):
        part, column = first // width, first % width
        up_weights = up_ref[part, :, column : column + size]
        down_weights = down_ref[first : first + size, :]
        up_proj = dot_nn(normed, up_weights) + shift_ref[:, first : first + size]
        chance = 0.5 * (1.0 + lax.erf(up_proj * (0.5**0.5)))
        hidden = (up_proj * chance).astype(BF)
        slope = chance + up_proj * (jnp.exp(-0.5 * up_proj * up_proj) * 0.3989422804014327)
        d_up = (dot_nt(outcome, down_weights) * slope).astype(BF)
        hidden_ref[:, first : first + size] = hidden
        d_up_ref[:, first : first + size] = d_up
        sums_ref[:, first : first + size] = jnp.sum(d_up.astype(F32), axis=0, keepdims=True)
        d_normed = d_normed + dot_nt(d_up, up_weights)
        result = result + dot_nn(hidden, down_weights)
    rows = normed_refs[0].shape[0]
    for m in range(blocks):
        d_normed_refs[m][...] = d_normed[m * rows : (m + 1) * rows].astype(d_normed_refs[m].dtype)
        out_refs[m][...] = result[m * rows : (m + 1) * rows].astype(out_refs[m].dtype)


def middle_kernel(owners, seqs, blocks, place_ref, counts_ref, *refs):
    pieces, refs = refs[:owners], refs[owners:]
    d_normed_refs, refs = refs[:blocks], refs[blocks:]
    middle_in_ref, grad_ref, gain_ref, d_middle_ref, d_branch_ref, sums_ref = refs[:6]
    head_refs, (w_ref, sems) = refs[6 : 6 + seqs], refs[6 + seqs :]
    own_rows, head_width = w_ref.shape[0] // owners, w_ref.shape[0] // seqs
    copies = fetches(pieces, place_ref[2], 0, own_rows, w_ref, sems)
    for copy in copies:
        copy.start()
    valid = own_rows_valid(place_ref, counts_ref, seqs, grad_ref.shape[0])
    grad_rows = jnp.where(valid, grad_ref[...], 0.0)
    unit, inverse = normalised(middle_in_ref[...])
    upstream = sum(ref[...].astype(F32) for ref in d_normed_refs)
    d_middle = grad_rows + norm_back(upstream, unit, inverse, row_of(gain_ref, 1))
    d_branch = d_middle.astype(BF)
    d_middle_ref[...] = d_middle
    d_branch_ref[...] = d_branch
    for copy in copies:
        copy.wait()
    for k, head_ref in enumerate(head_refs):
        first = pl.multiple_of((place_ref[1] ^ k) * head_width, 16)
        head_ref[...] = dot_nt(d_branch, w_ref[pl.ds(first, head_width), :]).astype(BF)
    rows = (
        upstream * unit,
        upstream,
        d_branch.astype(F32),
        grad_rows.astype(BF).astype(F32),
    )
    for index, one in enumerate(rows):
        sums_ref[index : index + 1, :] = jnp.sum(one, axis=0, keepdims=True)


def grads_kernel(owners, seqs, blocks, own_rows, hidden_rows, place_ref, *refs):
    normed_refs, outcome_refs, refs = refs[:blocks], refs[blocks : 2 * blocks], refs[2 * blocks :]
    hidden_ref, d_up_ref, sent_ref, kept_ref = refs
    width = outcome_refs[0].shape[1]
    parts = d_up_ref.shape[1] // width
    bit = place_ref[2] & 1
    normed = jnp.concatenate([ref[...] for ref in normed_refs])
    outcome = jnp.concatenate([ref[...] for ref in outcome_refs])
    chunk, up_chunk = hidden_rows // seqs, own_rows // seqs
    for owner in range(owners):
        down = dot_tn(hidden_ref[:, owner * hidden_rows : (owner + 1) * hidden_rows], outcome)
        rows_in = normed[:, owner * own_rows : (owner + 1) * own_rows]
        ups = [
            dot_tn(rows_in, d_up_ref[:, part * width : (part + 1) * width]) for part in range(parts)
        ]

        def store(ref, owner=owner, down=down, ups=ups):
            for k in range(seqs):
                ref[owner // 2, k, 0:chunk, :] = down[k * chunk : (k + 1) * chunk].astype(BF)
                for part, up in enumerate(ups):
                    first = chunk + part * up_chunk
                    ref[owner // 2, k, first : first + up_chunk, :] = up[
                        k * up_chunk : (k + 1) * up_chunk
                    ].astype(BF)

        @pl.when(bit == owner % 2)
        def keep():
            store(kept_ref)

        @pl.when(bit != owner % 2)
        def send():
            store(sent_ref)


def step_kernel(bit, place_ref, kept_ref, arrived_ref, sent_ref, next_ref):
    high = (place_ref[2] // bit) & 1
    for i in range(sent_ref.shape[0]):
        for ref, index in ((sent_ref, 2 * i + 1 - high), (next_ref, 2 * i + high)):
            ref[i] = (kept_ref[index].astype(F32) + arrived_ref[index].astype(F32)).astype(BF)


def chunk_kernel(seqs, blocks, place_ref, kept_ref, arrived_ref, *refs):
    in_refs, out_refs = refs[:blocks], refs[blocks:]
    out_grads = sum(ref[...].astype(F32) for ref in in_refs)
    count, width = out_grads.shape
    size = width // seqs
    rows = out_refs[0].shape[0]
    for j in range(seqs):
        index = place_ref[1] ^ j
        total = kept_ref[0, index].astype(F32) + arrived_ref[0, index].astype(F32)
        out_refs[j][:, :width] = total.astype(BF)
        chosen = out_grads[:, :size]
        for k in range(1, seqs):
            chosen = jnp.where(index == k, out_grads[:, k * size : (k + 1) * size], chosen)
        out_refs[j][0:count, width:] = chosen.astype(BF)
        if count < rows:
            out_refs[j][count:, width:] = jnp.zeros((rows - count, size), BF)


def sums_kernel(seqs, blocks, *refs):
    part_refs, in_refs, (feed_ref, last_ref) = refs[:seqs], refs[seqs:-2], refs[-2:]
    width = feed_ref.shape[1]
    total = sum(ref[...].astype(F32) for ref in part_refs)
    feed_ref[...] = total[:, :width].astype(BF)
    terms = [ref[...].astype(F32) for ref in in_refs]
    while len(terms) > 1:
        terms = [terms[i] + terms[i + 1] for i in range(0, len(terms), 2)]
    last_ref[...] = terms[0].astype(BF)
    size = last_ref.shape[0] - 16
    last_ref[0:size, 3 * (width // seqs) :] = total[:size, width:].astype(BF)


def project_back_kernel(blocks, seqs, *refs):
    q_ref, kv_refs, w_ref, refs = refs[0], refs[1 : 1 + blocks], refs[1 + blocks], refs[2 + blocks :]
    normed_refs, (gain_ref, shift_ref), refs = refs[:seqs], refs[seqs : seqs + 2], refs[seqs + 2 :]
    projected_ref, columns_ref, sums_ref, part_refs = refs[0], refs[1], refs[2], refs[3:]
    d_kv = sum(ref[...].astype(F32) for ref in kv_refs).astype(BF)
    d_projected = jnp.concatenate([q_ref[...], d_kv], axis=1)
    projected_ref[...] = d_projected
    columns_ref[...] = jnp.sum(d_projected.astype(F32), axis=0, keepdims=True)
    rows = normed_refs[0].shape[0]
    gain, shift = row_of(gain_ref, 0), row_of(shift_ref, 0)
    with_normed, plain = 0.0, 0.0
    for k in range(seqs):
        part = dot_nt(d_projected[k * rows : (k + 1) * rows], w_ref[...])
        part_refs[k][...] = part.astype(BF)
        with_normed = with_normed + jnp.sum(
            part * (normed_refs[k][...].astype(F32) - shift), axis=0, keepdims=True
        )
        plain = plain + jnp.sum(part, axis=0, keepdims=True)
    sums_ref[0:1, :] = with_normed / gain
    sums_ref[1:2, :] = plain


def by_core(bit, owner, refs, store):
    sent_ref, kept_ref = refs

    @pl.when(bit == owner % 2)
    def keep():
        store(kept_ref)

    @pl.when(bit != owner % 2)
    def send():
        store(sent_ref)


def out_grads_kernel(owners, seqs, place_ref, *refs):
    att_refs, branch_ref, (sent_ref, kept_ref, att_ref) = refs[:seqs], refs[seqs], refs[seqs + 1 :]
    size = att_refs[0].shape[1]
    own_rows = branch_ref.shape[1] // owners
    for k in range(seqs):
        att_ref[place_ref[1] ^ k] = att_refs[k][...]
    for owner in range(owners):
        group, column = divmod(owner * own_rows, size)
        out = dot_tn(att_ref[group][:, column : column + own_rows], branch_ref[...]).astype(BF)

        def store(ref, owner=owner, out=out):
            ref[owner // 2] = out

        by_core(place_ref[2] & 1, owner, (sent_ref, kept_ref), store)


def last_grads_kernel(owners, seqs, blocks, place_ref, *refs):
    normed_refs, refs = refs[:seqs], refs[seqs:]
    (projected_ref, columns_ref, first_ref, middle_ref, up_ref, sent_ref, kept_ref) = refs
    width, third = first_ref.shape[1], projected_ref.shape[1]
    size = third // 3
    own_rows, hidden_rows = width // owners, up_ref.shape[1] // owners
    normed = jnp.concatenate([ref[...] for ref in normed_refs])
    projected = projected_ref[...]
    for owner in range(owners):
        first = owner * own_rows
        group, column = divmod(first, size)
        qkv = dot_tn(normed[:, first : first + own_rows], projected).astype(BF)
        is_group = place_ref[1] == group
        bias = [
            jnp.where(is_group, columns_ref[:, start : start + own_rows], 0.0)
            for start in (column, 2 * size + column)
        ]
        lines = [
            first_ref[0:1, first : first + own_rows],
            first_ref[1:2, first : first + own_rows],
            *bias,
        ] + [middle_ref[i : i + 1, first : first + own_rows] for i in range(4)]
        lines = jnp.concatenate(lines).astype(BF)
        up_line = up_ref[:, owner * hidden_rows : (owner + 1) * hidden_rows]
        up_line = jnp.concatenate(
            [jnp.where(place_ref[0] == b, up_line, 0.0) for b in range(blocks)], axis=1
        ).astype(BF)

        def store(ref, owner=owner, qkv=qkv, lines=lines, up_line=up_line):
            ref[owner // 2, 0:own_rows, 0:third] = qkv
            ref[owner // 2, 0:own_rows, third:] = jnp.zeros((own_rows, width - third), BF)
            ref[owner // 2, own_rows:, :] = jnp.zeros((16, width), BF)
            ref[owner // 2, own_rows : own_rows + 8, 0:own_rows] = lines
            ref[owner // 2, own_rows + 8 : own_rows + 9, 0 : up_line.shape[1]] = up_line

        by_core(place_ref[2] & 1, owner, (sent_ref, kept_ref), store)


def block_kernel(blocks, tail, place_ref, kept_ref, arrived_ref, *out_refs):
    total = kept_ref[0].astype(F32) + arrived_ref[0].astype(F32)
    own_rows = total.shape[0] - tail
    size = own_rows // blocks
    for m in range(blocks):
        chosen = total[:size]
        for j in range(1, blocks):
            chosen = jnp.where(place_ref[0] ^ m == j, total[j * size : (j + 1) * size], chosen)
        out_refs[m][0:size, :] = chosen.astype(BF)
        if tail:
            out_refs[m][size:, :] = total[own_rows:].astype(BF)


def first_back_kernel(pieces, *refs):
    part_refs, (tokens_ref, d_middle_ref, gain_ref, out_ref) = refs[:pieces], refs[pieces:]
    upstream = sum(ref[:, : out_ref.shape[1]].astype(F32) for ref in part_refs)
    unit, inverse = normalised(tokens_ref[...])
    out_ref[...] = d_middle_ref[...] + norm_back(upstream, unit, inverse, row_of(gain_ref, 0))


def place_kernel(seqs, blocks, layouts, place_ref, *refs):
    pieces = refs[: blocks * seqs]
    outs = refs[blocks * seqs : -2]
    held, sems = refs[-2:]
    blk, seq = place_ref[0], place_ref[1]
    copies = [
        pltpu.make_async_copy(
            pieces[m * seqs + k],
            held.at[jnp.bitwise_xor(blk, m), jnp.bitwise_xor(seq, k)],
            sems.at[m * seqs + k],
        )
        for m in range(blocks)
        for k in range(seqs)
    ]
    for copy in copies:
        copy.start()
    for copy in copies:
        copy.wait()
    for out, spots in zip(outs, layouts):
        for b in range(blocks):
            for k in range(seqs):
                for top, rows, first, size, row, column in spots(b, k):
                    piece = held[b, k, top : top + rows, first : first + size]
                    out[row : row + rows, column : column + size] = piece.astype(F32)


def run(kernel, label, outs, scalars, remote, arrays, scratch=(), waits=(), cost=1.0, mib=10):
    inputs = len(scalars) + len(remote) + len(arrays)

    def without_waits(*refs):
        kernel(*refs[:inputs], *refs[inputs + len(waits) :])

    return pl.pallas_call(
        without_waits,
        out_shape=tuple(outs),
        in_specs=[pl.BlockSpec(memory_space=pltpu.SMEM)] * len(scalars)
        + [pl.BlockSpec(memory_space=pltpu.VMEM)] * len(remote)
        + [pl.BlockSpec(memory_space=pltpu.VMEM)] * len(arrays)
        + [pl.BlockSpec(memory_space=pltpu.VMEM)] * len(waits),
        out_specs=(pl.BlockSpec(memory_space=pltpu.VMEM),) * len(outs),
        scratch_shapes=list(scratch),
        compiler_params=pltpu.CompilerParams(vmem_limit_bytes=mib * 1024 * 1024),
        cost_estimate=pl.CostEstimate(
            flops=1, bytes_accessed=int(cost * 1.2e6), transcendentals=0
        ),
        name=label,
    )(*scalars, *remote, *arrays, *waits)


def shape(dims, kind):
    return jax.ShapeDtypeStruct(tuple(dims), kind)


def copy_kernel(from_ref, to_ref):
    to_ref[...] = from_ref[...]


def gate(array, waits):
    (result,) = run(
        copy_kernel, "gate", [shape(array.shape, array.dtype)], [], [], [array], waits=waits
    )
    return result


def owner_sums(kept, arrived, place, label, waits=()):
    sent, bit = None, 2
    while bit < lax.axis_size("fsdp"):
        half = (kept.shape[0] // 2, *kept.shape[1:])
        sent, kept = run(
            functools.partial(step_kernel, bit),
            label,
            [shape(half, BF)] * 2,
            [place],
            [],
            [kept, arrived],
            waits=waits,
            mib=14,
        )
        arrived = swap(sent, "fsdp", bit)
        bit *= 2
    return kept, arrived, sent


def sum_parts(parts, axis):
    return [parts[0]] + [swap(parts[j], axis, j) for j in range(1, len(parts))]


def tree_sum(pieces):
    pieces = [piece.astype(F32) for piece in pieces]
    while len(pieces) > 1:
        pieces = [pieces[i] + pieces[i + 1] for i in range(0, len(pieces), 2)]
    return pieces[0]


def shards(
    tokens, counts, norm_gain, norm_bias, vec_bias, up_bias, w_qkv, w_out, w_up, w_down, grad_out
):
    owners, blocks, seqs = (lax.axis_size(name) for name in ("fsdp", "blk", "seq"))
    own, blk, seq = (lax.axis_index(name) for name in ("fsdp", "blk", "seq"))
    place = jnp.stack([blk, seq, own]).astype(jnp.int32)
    rows, width = tokens.shape[1:]
    head_width = width // seqs
    heads, third = head_width // HD, 3 * head_width
    own_rows = width // owners
    hidden_rows = w_down.shape[0] // blocks
    hidden_width = hidden_rows * owners
    parts = hidden_width // width
    block_rows, all_rows = seqs * rows, blocks * rows
    inputs, grad_in = tokens[0], grad_out[0]
    vmem, dma = pltpu.VMEM, pltpu.SemaphoreType.DMA

    (normed1,) = run(
        first_norm_kernel,
        "first_norm",
        [shape((rows, width), BF)],
        [],
        [],
        [inputs, norm_gain, norm_bias],
    )
    normed1_pieces = from_all(normed1, "seq")
    (qkv_mine,) = run(
        functools.partial(columns_kernel, seqs),
        "columns",
        [shape((own_rows, third), BF)],
        [place],
        [],
        [w_qkv],
        waits=[normed1],
    )
    qkv_pieces = doubled(qkv_mine, "fsdp")
    d_outcome, out_mine = run(
        functools.partial(prepare_kernel, seqs),
        "prepare",
        [shape((rows, width), BF), shape((own_rows, width), BF)],
        [place, counts],
        [],
        [grad_in, w_out],
        waits=[qkv_pieces[owners // 2]],
    )
    out_pieces = doubled(out_mine, "fsdp")
    outcome_pieces = from_all(d_outcome, "blk")

    biases = vec_bias.astype(F32)
    qkv_shift = jnp.concatenate(
        [
            lax.dynamic_slice_in_dim(biases[0], seq * head_width, head_width),
            jnp.zeros((head_width,), F32),
            lax.dynamic_slice_in_dim(biases[1], seq * head_width, head_width),
        ]
    ).reshape(1, third)
    up_shift = (
        lax.dynamic_index_in_dim(up_bias.reshape(owners, blocks, hidden_rows), blk, 1, False)
        .astype(F32)
        .reshape(1, hidden_width)
    )

    key_value, queries, qkv_full = run(
        functools.partial(qkv_kernel, owners, seqs),
        "project_in",
        [
            shape((block_rows, 2 * head_width), BF),
            shape((block_rows, head_width), BF),
            shape((width, third), BF),
        ],
        [place],
        qkv_pieces,
        [*normed1_pieces, qkv_shift],
        [dma((owners,))],
        waits=outcome_pieces[1:],
        mib=16,
    )
    packed = shape((parts * own_rows + hidden_rows, width), BF)
    if hidden_rows % 128 == 0:
        (weights_mine,) = run(
            functools.partial(pack_kernel, owners, blocks, parts),
            "pack",
            [packed],
            [place],
            [w_up, w_down],
            [],
            [dma((owners + 1,))],
            waits=[key_value, out_pieces[owners // 2]],
        )
    else:
        columns = [
            lax.dynamic_slice_in_dim(w_up, (i * blocks + blk) * hidden_rows, hidden_rows, axis=1)
            for i in range(owners)
        ]
        in_part = owners // parts
        weights_mine = jnp.concatenate(
            [
                jnp.concatenate(columns[part * in_part : (part + 1) * in_part], axis=1)
                for part in range(parts)
            ]
            + [lax.dynamic_slice_in_dim(w_down, blk * hidden_rows, hidden_rows, axis=0)]
        )

    kv_blocks = from_all(key_value, "blk")
    *att_out, log_total = run(
        functools.partial(attend_kernel, blocks, heads, seqs, rows),
        "attend",
        [shape((rows, head_width), BF)] * seqs + [shape((heads, block_rows), F32)],
        [place, counts],
        [],
        [queries, *kv_blocks],
        waits=out_pieces[1:],
        cost=1.3,
        mib=20,
    )
    att_pieces = sum_parts(att_out, "seq")
    weights = doubled(weights_mine, "fsdp", att_pieces[1:])
    middle, normed2 = run(
        functools.partial(project_kernel, owners, seqs),
        "project_out",
        [shape((rows, width), F32), shape((rows, width), BF)],
        [place],
        out_pieces,
        [*att_pieces, inputs, vec_bias, norm_gain, norm_bias],
        [vmem((width, width), BF), dma((owners,))],
        mib=12,
    )

    normed_pieces = from_all(normed2, "blk")
    row_shapes = [shape((rows, width), F32)] + [shape((rows, width), BF)] * (blocks - 1)
    hidden, d_up, up_sums, *rest = run(
        functools.partial(hidden_kernel, owners, blocks, own_rows, hidden_rows),
        "hidden",
        [shape((all_rows, hidden_width), BF)] * 2
        + [shape((1, hidden_width), F32)]
        + row_shapes * 2,
        [place],
        weights,
        [*normed_pieces, *outcome_pieces, up_shift],
        [
            vmem((parts, width, width), BF),
            vmem((hidden_width, width), BF),
            dma((parts + 1, owners)),
        ],
        cost=2.3,
        mib=24,
    )
    d_normed_pieces = sum_parts(rest[:blocks], "blk")
    chunk, up_chunk = hidden_rows // seqs, own_rows // seqs
    chunk_rows = chunk + parts * up_chunk
    sent, kept = run(
        functools.partial(grads_kernel, owners, seqs, blocks, own_rows, hidden_rows),
        "feed_grads",
        [shape((owners // 2, seqs, chunk_rows, width), BF)] * 2,
        [place],
        [],
        [*normed_pieces, *outcome_pieces, hidden, d_up],
        cost=1.3,
        mib=24,
    )
    d_middle, d_branch, middle_sums, *d_heads = run(
        functools.partial(middle_kernel, owners, seqs, blocks),
        "middle",
        [shape((rows, width), F32), shape((rows, width), BF), shape((4, width), F32)]
        + [shape((rows, head_width), BF)] * seqs,
        [place, counts],
        out_pieces,
        [*d_normed_pieces, middle, grad_in, norm_gain],
        [vmem((width, width), BF), dma((owners,))],
        waits=[sent],
        mib=12,
    )
    d_att_pieces = sum_parts(d_heads, "seq")
    result_pieces = sum_parts(rest[blocks:], "blk")
    d_query, *d_kv = run(
        functools.partial(attend_back_kernel, blocks, heads, seqs, rows),
        "attend_back",
        [shape((block_rows, head_width), BF), shape((block_rows, 2 * head_width), F32)]
        + [shape((block_rows, 2 * head_width), BF)] * (blocks - 1),
        [place, counts],
        [],
        [queries, log_total, *d_att_pieces, *kv_blocks],
        cost=1.9,
        mib=28,
    )
    kept, arrived, feed_sent = owner_sums(
        kept, swap(gate(sent, d_att_pieces[1:]), "fsdp", 1), place, "feed_step", waits=[d_query]
    )
    out_sent, out_kept = run(
        functools.partial(out_grads_kernel, owners, seqs),
        "out_grads",
        [shape((owners // 2, own_rows, width), BF)] * 2,
        [place],
        [],
        [*att_pieces, d_branch],
        [vmem((seqs, rows, head_width), BF)],
        waits=[feed_sent],
        mib=12,
    )
    blk_rows = own_rows // blocks
    d_projected, column_sums, first_sums, *d_normed1 = run(
        functools.partial(project_back_kernel, blocks, seqs),
        "project_back",
        [
            shape((block_rows, third), BF),
            shape((1, third), F32),
            shape((2, width), F32),
        ]
        + [shape((rows, width), BF)] * seqs,
        [],
        [],
        [d_query, *sum_parts(d_kv, "blk"), qkv_full, *normed1_pieces, norm_gain, norm_bias],
        waits=[feed_sent, out_sent],
        mib=16,
    )
    out_kept, out_arrived, out_step = owner_sums(
        out_kept, swap(gate(out_sent, [column_sums]), "fsdp", 1), place, "out_step"
    )
    d_normed1_pieces = sum_parts(d_normed1, "seq")
    (grad_tokens,) = run(
        functools.partial(first_back_kernel, seqs),
        "first_back",
        [shape((rows, width), F32)],
        [],
        [],
        [*d_normed1_pieces, inputs, d_middle, norm_gain],
        waits=[arrived],
    )

    out_blocks = run(
        functools.partial(block_kernel, blocks, 0),
        "out_blocks",
        [shape((blk_rows, width), BF)] * blocks,
        [place],
        [],
        [out_kept, out_arrived],
    )
    feed_chunks = run(
        functools.partial(chunk_kernel, seqs, blocks),
        "feed_chunks",
        [shape((chunk_rows, width + head_width), BF)] * seqs,
        [place],
        [],
        [kept, arrived, *sum_parts(out_blocks, "blk")],
        waits=[grad_tokens],
        mib=12,
    )

    sent, last_kept = run(
        functools.partial(last_grads_kernel, owners, seqs, blocks),
        "last_grads",
        [shape((owners // 2, own_rows + 16, width), BF)] * 2,
        [place],
        [],
        [*normed1_pieces, d_projected, column_sums, first_sums, middle_sums, up_sums],
        waits=[out_step],
        mib=16,
    )
    last_kept, last_arrived, _ = owner_sums(
        last_kept, swap(sent, "fsdp", 1), place, "last_step"
    )
    last_blocks = run(
        functools.partial(block_kernel, blocks, 16),
        "last_blocks",
        [shape((blk_rows + 16, width), BF)] * blocks,
        [place],
        [],
        [last_kept, last_arrived],
    )
    feed_sums, last_sums = run(
        functools.partial(sums_kernel, seqs, blocks),
        "sums",
        [shape((chunk_rows, width), BF), shape((blk_rows + 16, width), BF)],
        [],
        [],
        [*sum_parts(feed_chunks, "seq"), *sum_parts(last_blocks, "blk")],
        waits=result_pieces[1:],
    )
    feed_seq = from_all(feed_sums, "seq")
    last_seq = from_all(gate(last_sums, [feed_seq[1]]), "seq")
    outcome = sum(one.astype(F32) for one in result_pieces)
    valid = lax.broadcasted_iota(jnp.int32, (rows, 1), 0) < counts[0, blk * seqs + seq]
    activations = jnp.where(valid, middle + outcome + biases[3], 0.0)

    feed_all = [from_all(one, "blk") for one in feed_seq]
    last_all = [from_all(one, "blk") for one in last_seq]
    grad_down, grad_up = run(
        functools.partial(
            place_kernel,
            seqs,
            blocks,
            [
                lambda b, k: [(0, chunk, 0, width, b * hidden_rows + k * chunk, 0)],
                lambda b, k: [
                    (
                        chunk + (i * hidden_rows // width) * up_chunk,
                        up_chunk,
                        i * hidden_rows % width,
                        hidden_rows,
                        k * up_chunk,
                        (i * blocks + b) * hidden_rows,
                    )
                    for i in range(owners)
                ],
            ],
        ),
        "place_feed",
        [shape((blocks * hidden_rows, width), F32), shape((own_rows, blocks * hidden_width), F32)],
        [place],
        [feed_all[k][m] for m in range(blocks) for k in range(seqs)],
        [],
        [vmem((blocks, seqs, chunk_rows, width), BF), dma((blocks * seqs,))],
        waits=last_seq[1:],
        mib=24,
    )
    grad_qkv, grad_w_out = run(
        functools.partial(
            place_kernel,
            seqs,
            blocks,
            [
                lambda b, k: [
                    (
                        0,
                        blk_rows,
                        i * head_width,
                        head_width,
                        b * blk_rows,
                        i * width + k * head_width,
                    )
                    for i in range(3)
                ],
                lambda b, k: [(0, blk_rows, third, head_width, b * blk_rows, k * head_width)],
            ],
        ),
        "place_last",
        [shape((own_rows, 3 * width), F32), shape((own_rows, width), F32)],
        [place],
        [last_all[k][m] for m in range(blocks) for k in range(seqs)],
        [],
        [vmem((blocks, seqs, blk_rows + 16, width), BF), dma((blocks * seqs,))],
        waits=[grad_down],
        mib=20,
    )
    small = tree_sum([one[blk_rows:] for one in last_seq])
    lines = small[:8, :own_rows]
    return (
        activations[None],
        grad_tokens[None],
        jnp.stack([lines[0], lines[4]]),
        jnp.stack([lines[1], lines[5]]),
        jnp.stack([lines[2], lines[3], lines[6], lines[7]]),
        small[8, : blocks * hidden_rows],
        grad_qkv,
        grad_w_out,
        grad_up,
        grad_down,
    )


def solution(mesh):
    rows = P("fsdp", ("blk", "seq"), None)
    split = P("fsdp", None)
    return jax.shard_map(
        shards,
        mesh=mesh,
        in_specs=(rows, split, P(), P(), P(), P(), split, split, split, split, rows),
        out_specs=(
            rows,
            rows,
            P(None, "fsdp"),
            P(None, "fsdp"),
            P(None, "fsdp"),
            P("fsdp"),
            split,
            split,
            split,
            split,
        ),
        check_vma=False,
    )
```

```python
import functools

import jax
import jax.numpy as jnp
from jax import lax
from jax.experimental import pallas as pl
from jax.experimental.pallas import tpu as pltpu
from jax.sharding import PartitionSpec as P

HD = 64
EPSILON = 1e-06
MASKED = -1e30
SCALE = HD ** (-0.5)
BF = jnp.bfloat16
F32 = jnp.float32


def dot_nn(left_side, right_side):
    return lax.dot_general(
        left_side, right_side, (((1,), (0,)), ((), ())), preferred_element_type=F32
    )


def dot_nt(left_side, right_side):
    return lax.dot_general(
        left_side, right_side, (((1,), (1,)), ((), ())), preferred_element_type=F32
    )


def dot_tn(left_side, right_side):
    return lax.dot_general(
        left_side, right_side, (((0,), (0,)), ((), ())), preferred_element_type=F32
    )


def swap(array, axis, bits):
    return lax.ppermute(array, axis, [(i, i ^ bits) for i in range(lax.axis_size(axis))])


def from_all(array, axis):
    return [array] + [swap(array, axis, j) for j in range(1, lax.axis_size(axis))]


def doubled(array, axis, waits=()):
    pieces = {0: array}
    bit = lax.axis_size(axis) // 2
    while bit:
        pieces.update({j | bit: swap(piece, axis, bit) for j, piece in list(pieces.items())})
        if waits and bit == lax.axis_size(axis) // 2:
            pieces[bit] = gate(pieces[bit], waits)
        bit //= 2
    return [pieces[j] for j in range(lax.axis_size(axis))]


def piece_bias(place_ref, counts_ref, block, pieces, slot_rows):
    row = lax.broadcasted_iota(jnp.int32, (pieces * slot_rows, 1), 0)
    limit = jnp.zeros_like(row)
    for piece in range(pieces):
        held = (place_ref[0] ^ block) * pieces + (place_ref[1] ^ piece)
        end = counts_ref[0, held] + piece * slot_rows
        limit = jnp.where(row >= piece * slot_rows, end, limit)
    return jnp.where(row < limit, 0.0, MASKED)


def own_rows_valid(place_ref, counts_ref, seqs, rows):
    count = counts_ref[0, place_ref[0] * seqs + place_ref[1]]
    return lax.broadcasted_iota(jnp.int32, (rows, 1), 0) < count


def normalised(matrix_rows):
    centre = matrix_rows - jnp.mean(matrix_rows, axis=-1, keepdims=True)
    inverse = lax.rsqrt(jnp.mean(centre * centre, axis=-1, keepdims=True) + EPSILON)
    return centre * inverse, inverse


def norm_back(upstream, unit_rows, inverse, gain_row):
    scaled = upstream * gain_row
    return inverse * (
        scaled
        - jnp.mean(scaled, axis=-1, keepdims=True)
        - unit_rows * jnp.mean(scaled * unit_rows, axis=-1, keepdims=True)
    )


def row_of(ref, index):
    return ref[...].astype(F32)[index : index + 1]


def fetches(pieces, own, first, size, target, sems):
    return [
        pltpu.make_async_copy(
            piece.at[pl.ds(first, size)],
            target.at[pl.ds(pl.multiple_of((own ^ j) * size, 16), size)],
            sems.at[j],
        )
        for j, piece in enumerate(pieces)
    ]


def prepare_kernel(
    seqs,
    place_ref,
    counts_ref,
    grad_ref,
    w_out_ref,
    outcome_ref,
    out_ref,
):
    out_ref[...] = w_out_ref[...]
    valid = own_rows_valid(place_ref, counts_ref, seqs, grad_ref.shape[0])
    outcome_ref[...] = jnp.where(valid, grad_ref[...], 0.0).astype(BF)


def columns_kernel(seqs, place_ref, qkv_ref, mine_ref):
    width = qkv_ref.shape[1] // 3
    size = width // seqs
    for part in range(3):
        chosen = qkv_ref[:, part * width : part * width + size]
        for k in range(1, seqs):
            first = part * width + k * size
            chosen = jnp.where(place_ref[1] == k, qkv_ref[:, first : first + size], chosen)
        mine_ref[:, part * size : (part + 1) * size] = chosen


def first_norm_kernel(tokens_ref, gain_ref, shift_ref, normed_ref):
    unit = normalised(tokens_ref[...])[0]
    normed_ref[...] = (unit * row_of(gain_ref, 0) + row_of(shift_ref, 0)).astype(BF)


def pack_kernel(owners, blocks, parts, place_ref, up_ref, down_ref, out_ref, sems):
    rows, width = up_ref.shape[0], down_ref.shape[1]
    size = down_ref.shape[0] // blocks
    copies = []
    for i in range(owners):
        first = pl.multiple_of((i * blocks + place_ref[0]) * size, 128)
        part, column = divmod(i * size, width)
        copies.append((up_ref.at[:, pl.ds(first, size)],
                       out_ref.at[pl.ds(part * rows, rows), pl.ds(column, size)]))
    first = pl.multiple_of(place_ref[0] * size, 16)
    copies.append((down_ref.at[pl.ds(first, size)], out_ref.at[pl.ds(parts * rows, size)]))
    copies = [
        pltpu.make_async_copy(source, target, sems.at[i])
        for i, (source, target) in enumerate(copies)
    ]
    for copy in copies:
        copy.start()
    for copy in copies:
        copy.wait()


def qkv_kernel(owners, seqs, place_ref, *refs):
    pieces, normed_refs, refs = refs[:owners], refs[owners : owners + seqs], refs[owners + seqs :]
    shift_ref, kv_ref, q_ref, w_ref, sems = refs
    own_rows, size = pieces[0].shape[0], q_ref.shape[1]
    copies = fetches(pieces, place_ref[2], 0, own_rows, w_ref, sems)
    for copy in copies:
        copy.start()
    normed = jnp.concatenate([ref[...] for ref in normed_refs])
    for copy in copies:
        copy.wait()
    result = (dot_nn(normed, w_ref[...]) + shift_ref[...]).astype(BF)
    q_ref[...] = result[:, :size]
    kv_ref[...] = result[:, size:]


def attend_kernel(blocks, heads, pieces, slot_rows, place_ref, counts_ref, q_ref, *refs):
    kv_refs, out_refs, log_ref = refs[:blocks], refs[blocks:-1], refs[-1]
    width = heads * HD
    biases = [piece_bias(place_ref, counts_ref, m, pieces, slot_rows) for m in range(blocks)]
    for head in range(heads):
        low, high = head * HD, (head + 1) * HD
        query = q_ref[:, low:high] * SCALE
        scores = [dot_nt(kv[:, low:high], query) + bias for kv, bias in zip(kv_refs, biases)]
        top = functools.reduce(
            jnp.maximum, [jnp.max(block, axis=0, keepdims=True) for block in scores]
        )
        powers = [jnp.exp(block - top) for block in scores]
        total = sum(jnp.sum(block, axis=0, keepdims=True) for block in powers)
        inverse = 1.0 / total
        result = sum(
            dot_tn((block * inverse).astype(BF), kv[:, width + low : width + high])
            for block, kv in zip(powers, kv_refs)
        ).astype(BF)
        for k, out_ref in enumerate(out_refs):
            out_ref[:, low:high] = result[k * slot_rows : (k + 1) * slot_rows]
        log_ref[head : head + 1, :] = top + jnp.log(total)


def attend_back_kernel(blocks, heads, pieces, slot_rows, place_ref, counts_ref, q_ref, log_ref, *refs):
    d_refs, refs = refs[:pieces], refs[pieces:]
    kv_refs, dq_ref, dkv_refs = refs[:blocks], refs[blocks], refs[blocks + 1 :]
    width = heads * HD
    biases = [piece_bias(place_ref, counts_ref, m, pieces, slot_rows) for m in range(blocks)]
    for head in range(heads):
        low, high = head * HD, (head + 1) * HD
        query = q_ref[:, low:high] * SCALE
        d_out = jnp.concatenate([d_ref[:, low:high] for d_ref in d_refs])
        log_row = log_ref[head : head + 1, :]
        softs, d_softs, delta = [], [], 0.0
        for kv, bias in zip(kv_refs, biases):
            soft = jnp.exp(dot_nt(kv[:, low:high], query) + bias - log_row)
            d_soft = dot_nt(kv[:, width + low : width + high], d_out)
            delta = delta + jnp.sum(soft * d_soft, axis=0, keepdims=True)
            softs.append(soft)
            d_softs.append(d_soft)
        d_query = 0.0
        for kv, dkv, soft, d_soft in zip(kv_refs, dkv_refs, softs, d_softs):
            d_scores = (soft * (d_soft - delta)).astype(BF)
            d_query = d_query + dot_tn(d_scores, kv[:, low:high])
            dkv[:, low:high] = dot_nn(d_scores, query).astype(dkv.dtype)
            dkv[:, width + low : width + high] = dot_nn(soft.astype(BF), d_out).astype(dkv.dtype)
        dq_ref[:, low:high] = (d_query * SCALE).astype(BF)


def project_kernel(owners, seqs, place_ref, *refs):
    pieces, att_refs = refs[:owners], refs[owners : owners + seqs]
    tokens_ref, vec_ref, gain_ref, shift_ref, middle_ref, normed_ref, w_ref, sems = refs[owners + seqs :]
    own_rows, head_width = w_ref.shape[0] // owners, w_ref.shape[0] // seqs
    copies = fetches(pieces, place_ref[2], 0, own_rows, w_ref, sems)
    for copy in copies:
        copy.start()
    middle = tokens_ref[...] + row_of(vec_ref, 2)
    for copy in copies:
        copy.wait()
    for k, att_ref in enumerate(att_refs):
        first = pl.multiple_of((place_ref[1] ^ k) * head_width, 16)
        middle = middle + dot_nn(att_ref[...], w_ref[pl.ds(first, head_width), :])
    middle_ref[...] = middle
    unit = normalised(middle)[0]
    normed_ref[...] = (unit * row_of(gain_ref, 1) + row_of(shift_ref, 1)).astype(BF)


def hidden_kernel(owners, blocks, own_rows, hidden_rows, place_ref, *refs):
    pieces, refs = refs[:owners], refs[owners:]
    normed_refs, outcome_refs, refs = refs[:blocks], refs[blocks : 2 * blocks], refs[2 * blocks :]
    shift_ref, hidden_ref, d_up_ref, sums_ref = refs[:4]
    d_normed_refs, out_refs = refs[4 : 4 + blocks], refs[4 + blocks : 4 + 2 * blocks]
    up_ref, down_ref, sems = refs[4 + 2 * blocks :]
    parts, width = up_ref.shape[0], up_ref.shape[1]
    own = place_ref[2]
    waits = []
    for part in range(parts):
        waits += fetches(
            pieces, own, part * own_rows, own_rows, up_ref.at[part], sems.at[part]
        )
    waits += fetches(pieces, own, parts * own_rows, hidden_rows, down_ref, sems.at[parts])
    for copy in waits:
        copy.start()
    normed = jnp.concatenate([ref[...] for ref in normed_refs])
    outcome = jnp.concatenate([ref[...] for ref in outcome_refs])
    for copy in waits:
        copy.wait()
    size = min(384, parts * width)
    d_normed, result = 0.0, 0.0
    for first in range(0, parts * width, size):
        part, column = first // width, first % width
        up_weights = up_ref[part, :, column : column + size]
        down_weights = down_ref[first : first + size, :]
        up_proj = dot_nn(normed, up_weights) + shift_ref[:, first : first + size]
        chance = 0.5 * (1.0 + lax.erf(up_proj * (0.5**0.5)))
        hidden = (up_proj * chance).astype(BF)
        slope = chance + up_proj * (jnp.exp(-0.5 * up_proj * up_proj) * 0.3989422804014327)
        d_up = (dot_nt(outcome, down_weights) * slope).astype(BF)
        hidden_ref[:, first : first + size] = hidden
        d_up_ref[:, first : first + size] = d_up
        sums_ref[:, first : first + size] = jnp.sum(d_up.astype(F32), axis=0, keepdims=True)
        d_normed = d_normed + dot_nt(d_up, up_weights)
        result = result + dot_nn(hidden, down_weights)
    rows = normed_refs[0].shape[0]
    for m in range(blocks):
        d_normed_refs[m][...] = d_normed[m * rows : (m + 1) * rows].astype(d_normed_refs[m].dtype)
        out_refs[m][...] = result[m * rows : (m + 1) * rows].astype(out_refs[m].dtype)


def middle_kernel(owners, seqs, blocks, place_ref, counts_ref, *refs):
    pieces, refs = refs[:owners], refs[owners:]
    d_normed_refs, refs = refs[:blocks], refs[blocks:]
    middle_in_ref, grad_ref, gain_ref, d_middle_ref, d_branch_ref, sums_ref = refs[:6]
    head_refs, (w_ref, sems) = refs[6 : 6 + seqs], refs[6 + seqs :]
    own_rows, head_width = w_ref.shape[0] // owners, w_ref.shape[0] // seqs
    copies = fetches(pieces, place_ref[2], 0, own_rows, w_ref, sems)
    for copy in copies:
        copy.start()
    valid = own_rows_valid(place_ref, counts_ref, seqs, grad_ref.shape[0])
    grad_rows = jnp.where(valid, grad_ref[...], 0.0)
    unit, inverse = normalised(middle_in_ref[...])
    upstream = sum(ref[...].astype(F32) for ref in d_normed_refs)
    d_middle = grad_rows + norm_back(upstream, unit, inverse, row_of(gain_ref, 1))
    d_branch = d_middle.astype(BF)
    d_middle_ref[...] = d_middle
    d_branch_ref[...] = d_branch
    for copy in copies:
        copy.wait()
    for k, head_ref in enumerate(head_refs):
        first = pl.multiple_of((place_ref[1] ^ k) * head_width, 16)
        head_ref[...] = dot_nt(d_branch, w_ref[pl.ds(first, head_width), :]).astype(BF)
    rows = (
        upstream * unit,
        upstream,
        d_branch.astype(F32),
        grad_rows.astype(BF).astype(F32),
    )
    for index, one in enumerate(rows):
        sums_ref[index : index + 1, :] = jnp.sum(one, axis=0, keepdims=True)


def grads_kernel(owners, seqs, blocks, own_rows, hidden_rows, place_ref, *refs):
    normed_refs, outcome_refs, refs = refs[:blocks], refs[blocks : 2 * blocks], refs[2 * blocks :]
    hidden_ref, d_up_ref, sent_ref, kept_ref = refs
    width = outcome_refs[0].shape[1]
    parts = d_up_ref.shape[1] // width
    bit = place_ref[2] & 1
    normed = jnp.concatenate([ref[...] for ref in normed_refs])
    outcome = jnp.concatenate([ref[...] for ref in outcome_refs])
    chunk, up_chunk = hidden_rows // seqs, own_rows // seqs
    for owner in range(owners):
        down = dot_tn(hidden_ref[:, owner * hidden_rows : (owner + 1) * hidden_rows], outcome)
        rows_in = normed[:, owner * own_rows : (owner + 1) * own_rows]
        ups = [
            dot_tn(rows_in, d_up_ref[:, part * width : (part + 1) * width]) for part in range(parts)
        ]

        def store(ref, owner=owner, down=down, ups=ups):
            for k in range(seqs):
                ref[owner // 2, k, 0:chunk, :] = down[k * chunk : (k + 1) * chunk].astype(BF)
                for part, up in enumerate(ups):
                    first = chunk + part * up_chunk
                    ref[owner // 2, k, first : first + up_chunk, :] = up[
                        k * up_chunk : (k + 1) * up_chunk
                    ].astype(BF)

        @pl.when(bit == owner % 2)
        def keep():
            store(kept_ref)

        @pl.when(bit != owner % 2)
        def send():
            store(sent_ref)


def step_kernel(bit, place_ref, kept_ref, arrived_ref, sent_ref, next_ref):
    high = (place_ref[2] // bit) & 1
    for i in range(sent_ref.shape[0]):
        for ref, index in ((sent_ref, 2 * i + 1 - high), (next_ref, 2 * i + high)):
            ref[i] = (kept_ref[index].astype(F32) + arrived_ref[index].astype(F32)).astype(BF)


def chunk_kernel(seqs, blocks, place_ref, kept_ref, arrived_ref, *refs):
    in_refs, out_refs = refs[:blocks], refs[blocks:]
    out_grads = sum(ref[...].astype(F32) for ref in in_refs)
    count, width = out_grads.shape
    size = width // seqs
    rows = out_refs[0].shape[0]
    for j in range(seqs):
        index = place_ref[1] ^ j
        total = kept_ref[0, index].astype(F32) + arrived_ref[0, index].astype(F32)
        out_refs[j][:, :width] = total.astype(BF)
        chosen = out_grads[:, :size]
        for k in range(1, seqs):
            chosen = jnp.where(index == k, out_grads[:, k * size : (k + 1) * size], chosen)
        out_refs[j][0:count, width:] = chosen.astype(BF)
        if count < rows:
            out_refs[j][count:, width:] = jnp.zeros((rows - count, size), BF)


def sums_kernel(seqs, blocks, *refs):
    part_refs, in_refs, out_ref = refs[:seqs], refs[seqs:-1], refs[-1]
    width = out_ref.shape[1]
    total = sum(ref[...].astype(F32) for ref in part_refs)
    base, size = total.shape[0], in_refs[0].shape[0] - 16
    out_ref[0:base, :] = total[:, :width].astype(BF)
    terms = [ref[...].astype(F32) for ref in in_refs]
    while len(terms) > 1:
        terms = [terms[i] + terms[i + 1] for i in range(0, len(terms), 2)]
    out_ref[base:, :] = terms[0].astype(BF)
    out_ref[base : base + size, 3 * (width // seqs) :] = total[:size, width:].astype(BF)


def project_back_kernel(blocks, seqs, *refs):
    q_ref, kv_refs, w_ref, refs = refs[0], refs[1 : 1 + blocks], refs[1 + blocks], refs[2 + blocks :]
    normed_refs, (gain_ref, shift_ref), refs = refs[:seqs], refs[seqs : seqs + 2], refs[seqs + 2 :]
    projected_ref, columns_ref, sums_ref, part_refs = refs[0], refs[1], refs[2], refs[3:]
    d_kv = sum(ref[...].astype(F32) for ref in kv_refs).astype(BF)
    d_projected = jnp.concatenate([q_ref[...], d_kv], axis=1)
    projected_ref[...] = d_projected
    columns_ref[...] = jnp.sum(d_projected.astype(F32), axis=0, keepdims=True)
    rows = normed_refs[0].shape[0]
    gain, shift = row_of(gain_ref, 0), row_of(shift_ref, 0)
    with_normed, plain = 0.0, 0.0
    for k in range(seqs):
        part = dot_nt(d_projected[k * rows : (k + 1) * rows], w_ref[...])
        part_refs[k][...] = part.astype(BF)
        with_normed = with_normed + jnp.sum(
            part * (normed_refs[k][...].astype(F32) - shift), axis=0, keepdims=True
        )
        plain = plain + jnp.sum(part, axis=0, keepdims=True)
    sums_ref[0:1, :] = with_normed / gain
    sums_ref[1:2, :] = plain


def by_core(bit, owner, refs, store):
    sent_ref, kept_ref = refs

    @pl.when(bit == owner % 2)
    def keep():
        store(kept_ref)

    @pl.when(bit != owner % 2)
    def send():
        store(sent_ref)


def out_grads_kernel(owners, seqs, place_ref, *refs):
    att_refs, branch_ref, (sent_ref, kept_ref, att_ref) = refs[:seqs], refs[seqs], refs[seqs + 1 :]
    size = att_refs[0].shape[1]
    own_rows = branch_ref.shape[1] // owners
    for k in range(seqs):
        att_ref[place_ref[1] ^ k] = att_refs[k][...]
    for owner in range(owners):
        group, column = divmod(owner * own_rows, size)
        out = dot_tn(att_ref[group][:, column : column + own_rows], branch_ref[...]).astype(BF)

        def store(ref, owner=owner, out=out):
            ref[owner // 2] = out

        by_core(place_ref[2] & 1, owner, (sent_ref, kept_ref), store)


def last_grads_kernel(owners, seqs, blocks, place_ref, *refs):
    normed_refs, refs = refs[:seqs], refs[seqs:]
    (projected_ref, columns_ref, first_ref, middle_ref, up_ref, sent_ref, kept_ref) = refs
    width, third = first_ref.shape[1], projected_ref.shape[1]
    size = third // 3
    own_rows, hidden_rows = width // owners, up_ref.shape[1] // owners
    normed = jnp.concatenate([ref[...] for ref in normed_refs])
    projected = projected_ref[...]
    for owner in range(owners):
        first = owner * own_rows
        group, column = divmod(first, size)
        qkv = dot_tn(normed[:, first : first + own_rows], projected).astype(BF)
        is_group = place_ref[1] == group
        bias = [
            jnp.where(is_group, columns_ref[:, start : start + own_rows], 0.0)
            for start in (column, 2 * size + column)
        ]
        lines = [
            first_ref[0:1, first : first + own_rows],
            first_ref[1:2, first : first + own_rows],
            *bias,
        ] + [middle_ref[i : i + 1, first : first + own_rows] for i in range(4)]
        lines = jnp.concatenate(lines).astype(BF)
        up_line = up_ref[:, owner * hidden_rows : (owner + 1) * hidden_rows]
        up_line = jnp.concatenate(
            [jnp.where(place_ref[0] == b, up_line, 0.0) for b in range(blocks)], axis=1
        ).astype(BF)

        def store(ref, owner=owner, qkv=qkv, lines=lines, up_line=up_line):
            ref[owner // 2, 0:own_rows, 0:third] = qkv
            ref[owner // 2, 0:own_rows, third:] = jnp.zeros((own_rows, width - third), BF)
            ref[owner // 2, own_rows:, :] = jnp.zeros((16, width), BF)
            ref[owner // 2, own_rows : own_rows + 8, 0:own_rows] = lines
            ref[owner // 2, own_rows + 8 : own_rows + 9, 0 : up_line.shape[1]] = up_line

        by_core(place_ref[2] & 1, owner, (sent_ref, kept_ref), store)


def block_kernel(blocks, tail, place_ref, kept_ref, arrived_ref, *out_refs):
    total = kept_ref[0].astype(F32) + arrived_ref[0].astype(F32)
    own_rows = total.shape[0] - tail
    size = own_rows // blocks
    for m in range(blocks):
        chosen = total[:size]
        for j in range(1, blocks):
            chosen = jnp.where(place_ref[0] ^ m == j, total[j * size : (j + 1) * size], chosen)
        out_refs[m][0:size, :] = chosen.astype(BF)
        if tail:
            out_refs[m][size:, :] = total[own_rows:].astype(BF)


def first_back_kernel(pieces, *refs):
    part_refs, (tokens_ref, d_middle_ref, gain_ref, out_ref) = refs[:pieces], refs[pieces:]
    upstream = sum(ref[:, : out_ref.shape[1]].astype(F32) for ref in part_refs)
    unit, inverse = normalised(tokens_ref[...])
    out_ref[...] = d_middle_ref[...] + norm_back(upstream, unit, inverse, row_of(gain_ref, 0))


def place_kernel(seqs, blocks, layouts, place_ref, *refs):
    pieces = refs[: blocks * seqs]
    outs = refs[blocks * seqs : -2]
    held, sems = refs[-2:]
    blk, seq = place_ref[0], place_ref[1]
    copies = [
        pltpu.make_async_copy(
            pieces[m * seqs + k],
            held.at[jnp.bitwise_xor(blk, m), jnp.bitwise_xor(seq, k)],
            sems.at[m * seqs + k],
        )
        for m in range(blocks)
        for k in range(seqs)
    ]
    for copy in copies:
        copy.start()
    for copy in copies:
        copy.wait()
    for out, spots in zip(outs, layouts):
        for b in range(blocks):
            for k in range(seqs):
                for top, rows, first, size, row, column in spots(b, k):
                    piece = held[b, k, top : top + rows, first : first + size]
                    out[row : row + rows, column : column + size] = piece.astype(F32)


def run(kernel, label, outs, scalars, remote, arrays, scratch=(), waits=(), cost=1.0, mib=10):
    inputs = len(scalars) + len(remote) + len(arrays)

    def without_waits(*refs):
        kernel(*refs[:inputs], *refs[inputs + len(waits) :])

    return pl.pallas_call(
        without_waits,
        out_shape=tuple(outs),
        in_specs=[pl.BlockSpec(memory_space=pltpu.SMEM)] * len(scalars)
        + [pl.BlockSpec(memory_space=pltpu.VMEM)] * len(remote)
        + [pl.BlockSpec(memory_space=pltpu.VMEM)] * len(arrays)
        + [pl.BlockSpec(memory_space=pltpu.VMEM)] * len(waits),
        out_specs=(pl.BlockSpec(memory_space=pltpu.VMEM),) * len(outs),
        scratch_shapes=list(scratch),
        compiler_params=pltpu.CompilerParams(vmem_limit_bytes=mib * 1024 * 1024),
        cost_estimate=pl.CostEstimate(
            flops=1, bytes_accessed=int(cost * 1.2e6), transcendentals=0
        ),
        name=label,
    )(*scalars, *remote, *arrays, *waits)


def shape(dims, kind):
    return jax.ShapeDtypeStruct(tuple(dims), kind)


def copy_kernel(from_ref, to_ref):
    to_ref[...] = from_ref[...]


def gate(array, waits):
    (result,) = run(
        copy_kernel, "gate", [shape(array.shape, array.dtype)], [], [], [array], waits=waits
    )
    return result


def owner_sums(kept, arrived, place, label, waits=()):
    sent, bit = None, 2
    while bit < lax.axis_size("fsdp"):
        half = (kept.shape[0] // 2, *kept.shape[1:])
        sent, kept = run(
            functools.partial(step_kernel, bit),
            label,
            [shape(half, BF)] * 2,
            [place],
            [],
            [kept, arrived],
            waits=waits,
            mib=14,
        )
        arrived = swap(sent, "fsdp", bit)
        bit *= 2
    return kept, arrived, sent


def sum_parts(parts, axis):
    return [parts[0]] + [swap(parts[j], axis, j) for j in range(1, len(parts))]


def tree_sum(pieces):
    pieces = [piece.astype(F32) for piece in pieces]
    while len(pieces) > 1:
        pieces = [pieces[i] + pieces[i + 1] for i in range(0, len(pieces), 2)]
    return pieces[0]


def shards(
    tokens, counts, norm_gain, norm_bias, vec_bias, up_bias, w_qkv, w_out, w_up, w_down, grad_out
):
    owners, blocks, seqs = (lax.axis_size(name) for name in ("fsdp", "blk", "seq"))
    own, blk, seq = (lax.axis_index(name) for name in ("fsdp", "blk", "seq"))
    place = jnp.stack([blk, seq, own]).astype(jnp.int32)
    rows, width = tokens.shape[1:]
    head_width = width // seqs
    heads, third = head_width // HD, 3 * head_width
    own_rows = width // owners
    hidden_rows = w_down.shape[0] // blocks
    hidden_width = hidden_rows * owners
    parts = hidden_width // width
    block_rows, all_rows = seqs * rows, blocks * rows
    inputs, grad_in = tokens[0], grad_out[0]
    vmem, dma = pltpu.VMEM, pltpu.SemaphoreType.DMA

    (normed1,) = run(
        first_norm_kernel,
        "first_norm",
        [shape((rows, width), BF)],
        [],
        [],
        [inputs, norm_gain, norm_bias],
    )
    normed1_pieces = from_all(normed1, "seq")
    (qkv_mine,) = run(
        functools.partial(columns_kernel, seqs),
        "columns",
        [shape((own_rows, third), BF)],
        [place],
        [],
        [w_qkv],
        waits=[normed1],
    )
    qkv_pieces = doubled(qkv_mine, "fsdp")
    d_outcome, out_mine = run(
        functools.partial(prepare_kernel, seqs),
        "prepare",
        [shape((rows, width), BF), shape((own_rows, width), BF)],
        [place, counts],
        [],
        [grad_in, w_out],
        waits=[qkv_pieces[owners // 2]],
    )
    out_pieces = doubled(out_mine, "fsdp")
    outcome_pieces = from_all(d_outcome, "blk")

    biases = vec_bias.astype(F32)
    qkv_shift = jnp.concatenate(
        [
            lax.dynamic_slice_in_dim(biases[0], seq * head_width, head_width),
            jnp.zeros((head_width,), F32),
            lax.dynamic_slice_in_dim(biases[1], seq * head_width, head_width),
        ]
    ).reshape(1, third)
    up_shift = (
        lax.dynamic_index_in_dim(up_bias.reshape(owners, blocks, hidden_rows), blk, 1, False)
        .astype(F32)
        .reshape(1, hidden_width)
    )

    key_value, queries, qkv_full = run(
        functools.partial(qkv_kernel, owners, seqs),
        "project_in",
        [
            shape((block_rows, 2 * head_width), BF),
            shape((block_rows, head_width), BF),
            shape((width, third), BF),
        ],
        [place],
        qkv_pieces,
        [*normed1_pieces, qkv_shift],
        [dma((owners,))],
        waits=outcome_pieces[1:],
        mib=16,
    )
    packed = shape((parts * own_rows + hidden_rows, width), BF)
    if hidden_rows % 128 == 0:
        (weights_mine,) = run(
            functools.partial(pack_kernel, owners, blocks, parts),
            "pack",
            [packed],
            [place],
            [w_up, w_down],
            [],
            [dma((owners + 1,))],
            waits=[key_value, out_pieces[owners // 2]],
        )
    else:
        columns = [
            lax.dynamic_slice_in_dim(w_up, (i * blocks + blk) * hidden_rows, hidden_rows, axis=1)
            for i in range(owners)
        ]
        in_part = owners // parts
        weights_mine = jnp.concatenate(
            [
                jnp.concatenate(columns[part * in_part : (part + 1) * in_part], axis=1)
                for part in range(parts)
            ]
            + [lax.dynamic_slice_in_dim(w_down, blk * hidden_rows, hidden_rows, axis=0)]
        )

    kv_blocks = from_all(key_value, "blk")
    *att_out, log_total = run(
        functools.partial(attend_kernel, blocks, heads, seqs, rows),
        "attend",
        [shape((rows, head_width), BF)] * seqs + [shape((heads, block_rows), F32)],
        [place, counts],
        [],
        [queries, *kv_blocks],
        waits=out_pieces[1:],
        cost=1.3,
        mib=20,
    )
    att_pieces = sum_parts(att_out, "seq")
    weights = doubled(weights_mine, "fsdp", att_pieces[1:])
    middle, normed2 = run(
        functools.partial(project_kernel, owners, seqs),
        "project_out",
        [shape((rows, width), F32), shape((rows, width), BF)],
        [place],
        out_pieces,
        [*att_pieces, inputs, vec_bias, norm_gain, norm_bias],
        [vmem((width, width), BF), dma((owners,))],
        mib=12,
    )

    normed_pieces = from_all(normed2, "blk")
    row_shapes = [shape((rows, width), F32)] + [shape((rows, width), BF)] * (blocks - 1)
    hidden, d_up, up_sums, *rest = run(
        functools.partial(hidden_kernel, owners, blocks, own_rows, hidden_rows),
        "hidden",
        [shape((all_rows, hidden_width), BF)] * 2
        + [shape((1, hidden_width), F32)]
        + row_shapes * 2,
        [place],
        weights,
        [*normed_pieces, *outcome_pieces, up_shift],
        [
            vmem((parts, width, width), BF),
            vmem((hidden_width, width), BF),
            dma((parts + 1, owners)),
        ],
        cost=2.3,
        mib=24,
    )
    d_normed_pieces = sum_parts(rest[:blocks], "blk")
    chunk, up_chunk = hidden_rows // seqs, own_rows // seqs
    chunk_rows = chunk + parts * up_chunk
    sent, kept = run(
        functools.partial(grads_kernel, owners, seqs, blocks, own_rows, hidden_rows),
        "feed_grads",
        [shape((owners // 2, seqs, chunk_rows, width), BF)] * 2,
        [place],
        [],
        [*normed_pieces, *outcome_pieces, hidden, d_up],
        cost=1.3,
        mib=24,
    )
    d_middle, d_branch, middle_sums, *d_heads = run(
        functools.partial(middle_kernel, owners, seqs, blocks),
        "middle",
        [shape((rows, width), F32), shape((rows, width), BF), shape((4, width), F32)]
        + [shape((rows, head_width), BF)] * seqs,
        [place, counts],
        out_pieces,
        [*d_normed_pieces, middle, grad_in, norm_gain],
        [vmem((width, width), BF), dma((owners,))],
        waits=[sent],
        mib=12,
    )
    d_att_pieces = sum_parts(d_heads, "seq")
    result_pieces = sum_parts(rest[blocks:], "blk")
    d_query, *d_kv = run(
        functools.partial(attend_back_kernel, blocks, heads, seqs, rows),
        "attend_back",
        [shape((block_rows, head_width), BF), shape((block_rows, 2 * head_width), F32)]
        + [shape((block_rows, 2 * head_width), BF)] * (blocks - 1),
        [place, counts],
        [],
        [queries, log_total, *d_att_pieces, *kv_blocks],
        cost=1.9,
        mib=28,
    )
    kept, arrived, feed_sent = owner_sums(
        kept, swap(gate(sent, d_att_pieces[1:]), "fsdp", 1), place, "feed_step", waits=[d_query]
    )
    out_sent, out_kept = run(
        functools.partial(out_grads_kernel, owners, seqs),
        "out_grads",
        [shape((owners // 2, own_rows, width), BF)] * 2,
        [place],
        [],
        [*att_pieces, d_branch],
        [vmem((seqs, rows, head_width), BF)],
        waits=[feed_sent],
        mib=12,
    )
    blk_rows = own_rows // blocks
    d_projected, column_sums, first_sums, *d_normed1 = run(
        functools.partial(project_back_kernel, blocks, seqs),
        "project_back",
        [
            shape((block_rows, third), BF),
            shape((1, third), F32),
            shape((2, width), F32),
        ]
        + [shape((rows, width), BF)] * seqs,
        [],
        [],
        [d_query, *sum_parts(d_kv, "blk"), qkv_full, *normed1_pieces, norm_gain, norm_bias],
        waits=[feed_sent, out_sent],
        mib=16,
    )
    d_normed1_pieces = sum_parts(d_normed1, "seq")
    (grad_tokens,) = run(
        functools.partial(first_back_kernel, seqs),
        "first_back",
        [shape((rows, width), F32)],
        [],
        [],
        [*d_normed1_pieces, inputs, d_middle, norm_gain],
        waits=[arrived],
    )

    out_kept, out_arrived, out_step = owner_sums(
        out_kept, swap(gate(out_sent, [column_sums]), "fsdp", 1), place, "out_step", waits=[grad_tokens]
    )
    out_blocks = run(
        functools.partial(block_kernel, blocks, 0),
        "out_blocks",
        [shape((blk_rows, width), BF)] * blocks,
        [place],
        [],
        [out_kept, out_arrived],
    )
    feed_chunks = run(
        functools.partial(chunk_kernel, seqs, blocks),
        "feed_chunks",
        [shape((chunk_rows, width + head_width), BF)] * seqs,
        [place],
        [],
        [kept, arrived, *sum_parts(out_blocks, "blk")],
        waits=[grad_tokens],
        mib=12,
    )

    sent, last_kept = run(
        functools.partial(last_grads_kernel, owners, seqs, blocks),
        "last_grads",
        [shape((owners // 2, own_rows + 16, width), BF)] * 2,
        [place],
        [],
        [*normed1_pieces, d_projected, column_sums, first_sums, middle_sums, up_sums],
        mib=16,
    )
    last_kept, last_arrived, _ = owner_sums(
        last_kept, swap(sent, "fsdp", 1), place, "last_step"
    )
    last_blocks = run(
        functools.partial(block_kernel, blocks, 16),
        "last_blocks",
        [shape((blk_rows + 16, width), BF)] * blocks,
        [place],
        [],
        [last_kept, last_arrived],
    )
    (all_sums,) = run(
        functools.partial(sums_kernel, seqs, blocks),
        "sums",
        [shape((chunk_rows + blk_rows + 16, width), BF)],
        [],
        [],
        [*sum_parts(feed_chunks, "seq"), *sum_parts(last_blocks, "blk")],
        waits=result_pieces[1:],
    )
    sums_seq = from_all(all_sums, "seq")
    outcome = sum(one.astype(F32) for one in result_pieces)
    valid = lax.broadcasted_iota(jnp.int32, (rows, 1), 0) < counts[0, blk * seqs + seq]
    activations = jnp.where(valid, middle + outcome + biases[3], 0.0)

    sums_all = [from_all(one, "blk") for one in sums_seq]
    base = chunk_rows
    grad_down, grad_up, grad_qkv, grad_w_out = run(
        functools.partial(
            place_kernel,
            seqs,
            blocks,
            [
                lambda b, k: [(0, chunk, 0, width, b * hidden_rows + k * chunk, 0)],
                lambda b, k: [
                    (
                        chunk + (i * hidden_rows // width) * up_chunk,
                        up_chunk,
                        i * hidden_rows % width,
                        hidden_rows,
                        k * up_chunk,
                        (i * blocks + b) * hidden_rows,
                    )
                    for i in range(owners)
                ],
                lambda b, k: [
                    (
                        base,
                        blk_rows,
                        i * head_width,
                        head_width,
                        b * blk_rows,
                        i * width + k * head_width,
                    )
                    for i in range(3)
                ],
                lambda b, k: [(base, blk_rows, third, head_width, b * blk_rows, k * head_width)],
            ],
        ),
        "place",
        [
            shape((blocks * hidden_rows, width), F32),
            shape((own_rows, blocks * hidden_width), F32),
            shape((own_rows, 3 * width), F32),
            shape((own_rows, width), F32),
        ],
        [place],
        [sums_all[k][m] for m in range(blocks) for k in range(seqs)],
        [],
        [vmem((blocks, seqs, base + blk_rows + 16, width), BF), dma((blocks * seqs,))],
        mib=36,
    )
    small = tree_sum([one[base + blk_rows :] for one in sums_seq])
    lines = small[:8, :own_rows]
    return (
        activations[None],
        grad_tokens[None],
        jnp.stack([lines[0], lines[4]]),
        jnp.stack([lines[1], lines[5]]),
        jnp.stack([lines[2], lines[3], lines[6], lines[7]]),
        small[8, : blocks * hidden_rows],
        grad_qkv,
        grad_w_out,
        grad_up,
        grad_down,
    )


def solution(mesh):
    rows = P("fsdp", ("blk", "seq"), None)
    split = P("fsdp", None)
    return jax.shard_map(
        shards,
        mesh=mesh,
        in_specs=(rows, split, P(), P(), P(), P(), split, split, split, split, rows),
        out_specs=(
            rows,
            rows,
            P(None, "fsdp"),
            P(None, "fsdp"),
            P(None, "fsdp"),
            P("fsdp"),
            split,
            split,
            split,
            split,
        ),
        check_vma=False,
    )
```
